32 devices in a mesh: ulysses: 4 (over y, core), blk: 8 (over z, x).
Axes of the slice: x: 2, y: 2, z: 4, core: 2. Of those that a mesh axis runs over, the one named last changes fastest.
Arguments:
- block_input: bfloat16 [4096, 2048], P(('blk', 'ulysses')), may hold values from -6 to 6
- w_query: float32 [2048, 2048], P(('ulysses', 'blk')), may hold values from -0.125 to 0.125
- w_key: float32 [2048, 2048], P(('ulysses', 'blk')), may hold values from -0.125 to 0.125
- w_value: float32 [2048, 2048], P(('ulysses', 'blk')), may hold values from -0.125 to 0.125
- w_out: float32 [2048, 2048], P(('ulysses', 'blk')), may hold values from -1 to 1
- attn_gain: float32 [2048], P(('ulysses', 'blk')), may hold values from 0.1 to 1.9
- ffn_gain: float32 [2048], P(('ulysses', 'blk')), may hold values from 0.1 to 1.9
- query_gain: float32 [2048], P(('ulysses', 'blk')), may hold values from 1.2 to 1.6
- key_gain: float32 [2048], P(('ulysses', 'blk')), may hold values from 1.2 to 1.6
- router: float32 [2048, 16], P(('ulysses', 'blk')), may hold values from -0.0625 to 0.0625
- w_gate: float32 [16, 2048, 1024], P('blk', None, 'ulysses'), may hold values from -0.125 to 0.125
- w_up: float32 [16, 2048, 1024], P('blk', None, 'ulysses'), may hold values from -0.125 to 0.125
- w_down: float32 [16, 1024, 2048], P('blk', 'ulysses'), may hold values from -4 to 4
- expert_ids: int32 [4096, 8], P(('blk', 'ulysses')), may hold values from 0 to 15, as said below
- slot_ids: int32 [4096, 8], P(('blk', 'ulysses')), may hold values from 0 to 79, as said below
- doc_starts: int32 [8], replicated, may hold values from 0 to 4095, as said below
- cotangent: bfloat16 [4096, 2048], P(('blk', 'ulysses')), may hold values from -6 to 6
Outputs:
- mixed: bfloat16 [4096, 2048], P(('blk', 'ulysses'))
- input_grad: bfloat16 [4096, 2048], P(('blk', 'ulysses'))
- grad_w_query: float32 [2048, 2048], P(('ulysses', 'blk'))
- grad_w_key: float32 [2048, 2048], P(('ulysses', 'blk'))
- grad_w_value: float32 [2048, 2048], P(('ulysses', 'blk'))
- grad_w_out: float32 [2048, 2048], P(('ulysses', 'blk'))
- grad_attn_gain: float32 [2048], P(('ulysses', 'blk'))
- grad_ffn_gain: float32 [2048], P(('ulysses', 'blk'))
- grad_query_gain: float32 [2048], P(('ulysses', 'blk'))
- grad_key_gain: float32 [2048], P(('ulysses', 'blk'))
- grad_router: float32 [2048, 16], P(('ulysses', 'blk'))
- grad_w_gate: float32 [16, 2048, 1024], P('blk', None, 'ulysses')
- grad_w_up: float32 [16, 2048, 1024], P('blk', None, 'ulysses')
- grad_w_down: float32 [16, 1024, 2048], P('blk', 'ulysses')
The draws below stay inside these ranges and needn't reach their ends.
Inputs may be any that keep to these rules, and one draw needn't show every extreme that they name: `expert_ids`: each row names 8 different experts. In each aligned block of 128 rows (the rows of one device) no expert is named by more than 80 rows, and one expert is named by exactly 80 rows in every block. `slot_ids`: within one aligned block of 128 rows, the choices that name the same expert carry different slots. `doc_starts`: strictly rising, the first is 0; the second lies below 512 and the last 6 lie among the last 512 tokens.
All inputs are finite; a program needn't handle non-finite values.
Results may differ from the reference program's by a relative error of at most 0.02.
The reference program's roundings to bfloat16 on the way count: a program that leaves them out, or rounds other values in their place, can miss the bound.
Values may be sent and summed in bfloat16 or wider, within the bound.
No kernel may reach another device: no remote copies, remote signals or barrier semaphores. Data moves between devices by JAX's collectives and lax.ppermute only.
A program may use at most 320 MiB of HBM per device.

```python
import jax
import jax.numpy as jnp
from jax import lax

D = 2048
HEADS = 16
HEAD_DIM = 128
FF = 1024
TOPK = 8
TOK_DEV = 128
DOCS = 8
E = 16
TOKENS = 4096
BLOCK_TOK = 512
CAP = 80


def route_tables(key):
    full_key, block_base = jax.random.split(key)
    full_expert = jax.random.randint(full_key, (), 0, E)
    mean_load = TOK_DEV * TOPK // E
    block_count = TOKENS // TOK_DEV
    pair_count = TOK_DEV * TOPK

    def one_block(block_key):
        perm_key, load_key, token_key = jax.random.split(block_key, 3)
        expert_order = jax.random.permutation(perm_key, E).astype(jnp.int32)
        leading = expert_order[0]
        expert_order = jnp.where(expert_order == full_expert, leading, expert_order)
        expert_order = expert_order.at[0].set(full_expert)
        load_delta = jax.random.randint(load_key, (E // 2,), 0, CAP - mean_load + 1)
        load_delta = load_delta.at[0].set(CAP - mean_load)
        paired = jnp.stack([mean_load + load_delta, mean_load - load_delta], axis=1).reshape(E).astype(jnp.int32)
        load_table = jnp.zeros((E,), jnp.int32).at[expert_order].set(paired)
        run_ends = jnp.cumsum(load_table)
        position_list = jnp.arange(pair_count, dtype=jnp.int32)
        expert_of = jnp.sum((position_list[:, None] >= run_ends[None, :]).astype(jnp.int32), axis=1)
        slot_rank = position_list - (run_ends - load_table)[expert_of]
        token_order = jax.random.permutation(token_key, TOK_DEV).astype(jnp.int32)
        row_of = token_order[position_list % TOK_DEV]
        column_of = position_list // TOK_DEV
        id_table = jnp.zeros((TOK_DEV, TOPK), jnp.int32).at[row_of, column_of].set(expert_of)
        slot_table = jnp.zeros((TOK_DEV, TOPK), jnp.int32).at[row_of, column_of].set(slot_rank)
        return (id_table, slot_table)
    block_keys = jax.random.split(block_base, block_count)
    id_tables, slot_tables = jax.vmap(one_block)(block_keys)
    return (id_tables.reshape(TOKENS, TOPK), slot_tables.reshape(TOKENS, TOPK))


def draw_expert_ids(key, part):
    return route_tables(key)[0]


def draw_slot_ids(key, part):
    return route_tables(key)[1]


def draw_doc_starts(key, part):
    key = jax.random.fold_in(key, 7)
    first_key, tail_key = jax.random.split(key)
    first_doc = jax.random.randint(first_key, (1,), 1, BLOCK_TOK).astype(jnp.int32)
    tail_docs = jnp.sort(jax.random.permutation(tail_key, BLOCK_TOK - 1)[:DOCS - 2]).astype(jnp.int32)
    tail_docs = tail_docs + (TOKENS - BLOCK_TOK + 1)
    return jnp.concatenate([jnp.zeros((1,), jnp.int32), first_doc, tail_docs])


def levels(rng, extent, shards, least, high):
    gain, own = 1.0, jax.random.fold_in(rng, 6)
    for dim, parts in shards:
        steps = jnp.exp(jax.random.uniform(jax.random.fold_in(own, dim), (parts,), jnp.float32, least / len(shards), high / len(shards)))
        gain = gain * jnp.repeat(steps, extent[dim] // parts).reshape([-1 if axis == dim else 1 for axis in range(len(extent))])
    return gain


def bell_draw(key, dims, spread, most, cuts=(), kind=jnp.bfloat16):
    entries = jax.random.normal(key, dims, jnp.float32) * spread
    if len(cuts) > 0:
        entries = levels(key, dims, cuts, -0.22, 0.18) * entries
    return jnp.clip(entries, min=-most, max=most).astype(kind)


def setup_inputs(seed: int = 0) -> dict:
    keys = jax.random.split(jax.random.key(seed), 18)
    return {
        "block_input": bell_draw(keys[0], (TOKENS, D), 1.0, 6.0, ((0, 32),)),
        "w_query": bell_draw(keys[1], (D, D), D ** -0.5, 0.125, ((0, 32),), jnp.float32),
        "w_key": bell_draw(keys[2], (D, D), D ** -0.5, 0.125, ((0, 32),), jnp.float32),
        "w_value": bell_draw(keys[3], (D, D), D ** -0.5, 0.125, ((0, 32),), jnp.float32),
        "w_out": bell_draw(keys[4], (D, D), (D // 64) ** -0.5, 1.0, ((0, 32),), jnp.float32),
        "attn_gain": jnp.clip(1.0 + 0.18 * jax.random.normal(keys[5], (D,), jnp.float32), 0.1, 1.9),
        "ffn_gain": jnp.clip(1.0 + 0.18 * jax.random.normal(keys[6], (D,), jnp.float32), 0.1, 1.9),
        "query_gain": jnp.clip(1.2 + 0.39999998 * jax.random.uniform(keys[7], (D,), jnp.float32) ** levels(keys[7], (D,), ((0, 32),), -0.2, 0.2), 1.2, 1.6),
        "key_gain": jnp.clip(1.2 + 0.39999998 * jax.random.uniform(keys[8], (D,), jnp.float32) ** levels(keys[8], (D,), ((0, 32),), -0.2, 0.2), 1.2, 1.6),
        "router": bell_draw(keys[9], (D, E), (4 * D) ** -0.5, 0.0625, ((0, 32),), jnp.float32),
        "w_gate": bell_draw(keys[10], (E, D, FF), D ** -0.5, 0.125, ((0, 8), (2, 4)), jnp.float32),
        "w_up": bell_draw(keys[11], (E, D, FF), D ** -0.5, 0.125, ((0, 8), (2, 4)), jnp.float32),
        "w_down": bell_draw(keys[12], (E, FF, D), (0.6 * E * FF ** -0.5), 4.0, ((0, 8), (1, 4)), jnp.float32),
        "expert_ids": draw_expert_ids(jax.random.fold_in(keys[17], 71), 0),
        "slot_ids": draw_slot_ids(jax.random.fold_in(keys[17], 71), 0),
        "doc_starts": draw_doc_starts(jax.random.fold_in(keys[17], 71), 0),
        "cotangent": bell_draw(keys[16], (TOKENS, D), 1.0, 6.0, ((0, 32),)),
    }


NORM_EPSILON = 1e-05
ROPE_BASE = 10000.0
MASKED_SCORE = -1e+30
HIGHEST_PRECISION = lax.Precision.HIGHEST

@jax.custom_vjp
def low(v):
    return lax.optimization_barrier(v.astype(jnp.bfloat16)).astype(jnp.float32)

@jax.custom_vjp
def low_back(v):
    return v

def low_keep(v):
    return (low(v), None)

def low_pass(kept, grad):
    return (grad,)

def back_keep(v):
    return (v, None)

def back_low(kept, grad):
    return (low(grad),)
low.defvjp(low_keep, low_pass)
low_back.defvjp(back_keep, back_low)

def normalize(values):
    return values * lax.rsqrt(lax.optimization_barrier(jnp.mean(values * values, axis=-1, keepdims=True)) + NORM_EPSILON)

def matmul(left, right):
    return jnp.dot(left, right, precision=HIGHEST_PRECISION)

def doc_tables(doc_starts, first_token, token_count):
    tokens_at = first_token + jnp.arange(token_count, dtype=jnp.int32)
    segment = lax.optimization_barrier(jnp.sum((doc_starts[None, :] <= tokens_at[:, None]).astype(jnp.int32), axis=1)) - 1
    picked = jnp.arange(doc_starts.shape[0], dtype=jnp.int32)[None, :] == segment[:, None]
    begins = lax.optimization_barrier(jnp.sum(jnp.where(picked, doc_starts[None, :], 0), axis=1))
    return (segment, tokens_at - begins)

def angles(position, head_size):
    half_size = head_size // 2
    frequency = ROPE_BASE ** (-(jnp.arange(half_size, dtype=jnp.float32) * 2.0 / head_size))
    turned = position.astype(jnp.float32)[:, None] * frequency[None, :]
    return (jnp.cos(turned)[:, None, :], jnp.sin(turned)[:, None, :])

def rotate(values, cosine_table, sine_table):
    half_size = values.shape[-1] // 2
    first_half = values[..., :half_size]
    second_half = values[..., half_size:]
    return jnp.concatenate([first_half * cosine_table - second_half * sine_table, second_half * cosine_table + first_half * sine_table], axis=-1)

def reference(block_input, w_query, w_key, w_value, w_out, attn_gain, ffn_gain, query_gain, key_gain, router, w_gate, w_up, w_down, expert_ids, slot_ids, doc_starts, cotangent):
    token_count = block_input.shape[0]
    experts = router.shape[1]
    sources = token_count // TOK_DEV
    segment, position = doc_tables(doc_starts, 0, token_count)
    cosine_table, sine_table = angles(position, HEAD_DIM)
    token_index = jnp.arange(token_count, dtype=jnp.int32)
    slot_index = (expert_ids * (sources * CAP) + (token_index // TOK_DEV)[:, None] * CAP + slot_ids).reshape(-1)
    score_scale = HEAD_DIM ** (-0.5)
    block_starts = jnp.arange(token_count // BLOCK_TOK, dtype=jnp.int32) * BLOCK_TOK
    choice_onehot = expert_ids[:, :, None] == jnp.arange(experts, dtype=jnp.int32)[None, None, :]

    def attention(q_rot, k_rot, v_low):

        @jax.checkpoint
        def one_block(start):
            q_block = lax.dynamic_slice_in_dim(q_rot, start, BLOCK_TOK, 0)
            seg_block = lax.dynamic_slice_in_dim(segment, start, BLOCK_TOK, 0)
            query_at = start + jnp.arange(BLOCK_TOK, dtype=jnp.int32)
            scores = low_back(jnp.einsum('qhd,khd->hqk', q_block, k_rot, precision=HIGHEST_PRECISION) * score_scale)
            allowed = (seg_block[:, None] == segment[None, :]) & (token_index[None, :] <= query_at[:, None])
            scores = jnp.where(allowed[None], scores, MASKED_SCORE)
            shifted = jnp.exp(scores - lax.optimization_barrier(jnp.max(scores, axis=-1, keepdims=True)))
            attn_probs = low(shifted / lax.optimization_barrier(jnp.sum(shifted, axis=-1, keepdims=True)))
            return jnp.einsum('hqk,khd->qhd', attn_probs, v_low, precision=HIGHEST_PRECISION)
        return lax.map(one_block, block_starts).reshape(token_count, HEADS * HEAD_DIM)

    @jax.checkpoint
    def expert_rows(packed):
        rows, gate_weight, up_weight, down_weight = packed
        gate_val = low_back(matmul(rows, gate_weight))
        up_val = low_back(matmul(rows, up_weight))
        hidden_low = low(gate_val * jax.nn.sigmoid(gate_val) * up_val)
        return low_back(low(matmul(hidden_low, down_weight)))

    def forward(block_input, w_query, w_key, w_value, w_out, attn_gain, ffn_gain, query_gain, key_gain, router, w_gate, w_up, w_down):
        normed = low(normalize(block_input) * low(attn_gain))
        q_lin = low_back(matmul(normed, low(w_query)))
        k_lin = low_back(matmul(normed, low(w_key)))
        v_lin = low_back(matmul(normed, low(w_value)))
        q_rot = low(rotate((normalize(q_lin) * low(query_gain)).reshape(token_count, HEADS, HEAD_DIM), cosine_table, sine_table))
        k_rot = low(rotate((normalize(k_lin) * low(key_gain)).reshape(token_count, HEADS, HEAD_DIM), cosine_table, sine_table))
        v_low = low(v_lin).reshape(token_count, HEADS, HEAD_DIM)
        attended = low(low_back(attention(q_rot, k_rot, v_low)))
        residual_mid = block_input + low_back(matmul(attended, low(w_out)))
        ffn_in = low(normalize(residual_mid) * low(ffn_gain))
        logits = low_back(matmul(ffn_in, low(router)))
        shifted = jnp.exp(logits - lax.optimization_barrier(jnp.max(logits, axis=-1, keepdims=True)))
        router_probs = shifted / lax.optimization_barrier(jnp.sum(shifted, axis=-1, keepdims=True))
        gate_vals = lax.optimization_barrier(jnp.sum(jnp.where(choice_onehot, router_probs[:, None, :], 0.0), axis=-1))
        copies = low_back(jnp.broadcast_to(ffn_in[:, None, :], (token_count, TOPK, D)))
        buffer = jnp.zeros((experts * sources * CAP, D), jnp.float32).at[slot_index].set(copies.reshape(-1, D))
        outputs = lax.map(expert_rows, (buffer.reshape(experts, sources * CAP, D), low(w_gate), low(w_up), low(w_down)))
        returned = jnp.take(outputs.reshape(-1, D), slot_index, axis=0).reshape(token_count, TOPK, D)
        return residual_mid + lax.optimization_barrier(jnp.sum(gate_vals[:, :, None] * returned, axis=1))
    floats = [a.astype(jnp.float32) for a in (block_input, w_query, w_key, w_value, w_out, attn_gain, ffn_gain, query_gain, key_gain, router, w_gate, w_up, w_down)]
    mixed, pullback = jax.vjp(forward, *floats)
    gradients = pullback(cotangent.astype(jnp.float32))
    return (mixed.astype(jnp.bfloat16), gradients[0].astype(jnp.bfloat16), gradients[1], gradients[2], gradients[3], gradients[4], gradients[5], gradients[6], gradients[7], gradients[8], gradients[9], gradients[10], gradients[11], gradients[12])
```

```python
import math

import jax
import jax.numpy as jnp
from jax import lax
from jax.experimental import pallas as pl
from jax.experimental.pallas import tpu as pltpu
from jax.sharding import PartitionSpec as P

HEAD_DIM = 128
NORM_EPSILON = 1e-05
ROPE_BASE = 10000.0
MASKED_SCORE = -1e30
SCORE_SCALE = HEAD_DIM ** (-0.5)
LOG2_SCALE = SCORE_SCALE * math.log2(math.e)
QUERY_ROWS = 256
KEY_ROWS = 512
bfloat = jnp.bfloat16
single = jnp.float32


def norm_parts(values):
    recip_factor = lax.rsqrt(jnp.mean(values * values, axis=-1, keepdims=True) + NORM_EPSILON)
    return (values * recip_factor, recip_factor)


def norm_back(grad_in, hat_values, recip_factor):
    return recip_factor * (
        grad_in - hat_values * jnp.mean(grad_in * hat_values, axis=-1, keepdims=True)
    )


def doc_begins(doc_starts, tokens_at):
    at_or_before = doc_starts[:, None] <= tokens_at.reshape(1, -1)
    begins = jnp.max(jnp.where(at_or_before, doc_starts[:, None], 0), axis=0)
    return begins.reshape(tokens_at.shape)


def angles(position, head_size):
    half_size = head_size // 2
    frequency = ROPE_BASE ** (-(jnp.arange(half_size, dtype=jnp.float32) * 2.0 / head_size))
    turned = position.astype(jnp.float32)[:, None] * frequency[None, :]
    return (jnp.cos(turned)[:, None, :], jnp.sin(turned)[:, None, :])


def rotate(values, cosine_table, sine_table):
    half_size = values.shape[-1] // 2
    first_half = values[..., :half_size]
    second_half = values[..., half_size:]
    return jnp.concatenate(
        [
            first_half * cosine_table - second_half * sine_table,
            second_half * cosine_table + first_half * sine_table,
        ],
        axis=-1,
    )


def rotate_back(values, cosine_table, sine_table):
    return rotate(values, cosine_table, -sine_table)


def swap(values, bit):
    size = lax.axis_size("ulysses")
    return lax.ppermute(values, "ulysses", [(i, i ^ bit) for i in range(size)])


def gather_ulysses(values):
    me = lax.axis_index("ulysses")
    beyond = swap(values, 2)
    core = swap(values, 1)
    beyond_core = swap(beyond, 1)
    out = jnp.zeros((4,) + values.shape, values.dtype)
    for bit, part in enumerate((values, core, beyond, beyond_core)):
        out = lax.dynamic_update_index_in_dim(out, part, me ^ bit, 0)
    return out


def scatter_sum_ulysses(parts):
    far = swap(parts(3).astype(bfloat), 1)
    near = swap(parts(1).astype(bfloat), 1)
    across = swap((parts(2) + far.astype(single)).astype(bfloat), 2)
    return parts(0) + near.astype(single) + across.astype(single)


def sum_ulysses(values):
    return lax.psum(values, "ulysses")


def to_heads(arrays, blk_size):
    core = lax.axis_index("ulysses") % 2
    count = len(arrays)
    tokens, width = arrays[0].shape
    heads = width // HEAD_DIM
    half = tokens // 2
    stacked = jnp.stack(arrays).reshape(count, 2, half, heads, HEAD_DIM)
    stacked = jnp.transpose(stacked, (1, 0, 3, 2, 4))
    keep = lax.dynamic_index_in_dim(stacked, core, 0, keepdims=False)
    send = lax.dynamic_index_in_dim(stacked, 1 - core, 0, keepdims=False)
    got = swap(send, 1)
    both = jnp.where(
        core == 0, jnp.concatenate([keep, got], 1), jnp.concatenate([got, keep], 1)
    )
    groups = blk_size // (2 * heads)
    both = both.reshape(count, 2 * heads, groups, half // groups, HEAD_DIM)
    both = jnp.transpose(both, (1, 2, 0, 3, 4)).reshape(
        blk_size, count, half // groups, HEAD_DIM
    )
    return lax.all_to_all(both, "blk", split_axis=0, concat_axis=0, tiled=True)


def from_heads(stacked, blk_size, heads):
    core = lax.axis_index("ulysses") % 2
    count, rows = stacked.shape[1], stacked.shape[2]
    groups = blk_size // (2 * heads)
    half = rows * groups
    back = lax.all_to_all(stacked, "blk", split_axis=0, concat_axis=0, tiled=True)
    back = back.reshape(2, heads, groups, count, rows, HEAD_DIM)
    back = jnp.transpose(back, (0, 3, 2, 4, 1, 5)).reshape(2, count, half, heads, HEAD_DIM)
    keep = lax.dynamic_index_in_dim(back, core, 0, keepdims=False)
    send = lax.dynamic_index_in_dim(back, 1 - core, 0, keepdims=False)
    got = swap(send, 1)
    whole = jnp.where(
        core == 0, jnp.concatenate([keep, got], 1), jnp.concatenate([got, keep], 1)
    ).reshape(count, 2 * half, heads * HEAD_DIM)
    return [whole[i] for i in range(count)]


def join_halves(mine, other):
    core = lax.axis_index("ulysses") % 2
    return jnp.where(core == 0, jnp.stack([mine, other], 1), jnp.stack([other, mine], 1))


def head_groups(blk_size, groups):
    return [[j * groups + p for p in range(groups)] for j in range(blk_size // groups)]


def gather_keys(part, blk_size, groups):
    if groups > 1:
        part = lax.all_gather(part, "blk", axis=1, axis_index_groups=head_groups(blk_size, groups))
        part = part.reshape(blk_size, -1, HEAD_DIM)
    return join_halves(part, swap(part, 1)).reshape(-1, HEAD_DIM)


def scatter_keys(total, blk_size, groups):
    core = lax.axis_index("ulysses") % 2
    halves = total.reshape(blk_size, 2, -1, HEAD_DIM)
    keep = lax.dynamic_index_in_dim(halves, core, 1, keepdims=False)
    send = lax.dynamic_index_in_dim(halves, 1 - core, 1, keepdims=False)
    mine = (keep + swap(send.astype(bfloat), 1).astype(single)).astype(bfloat)
    if groups > 1:
        mine = mine.reshape(blk_size, groups, -1, HEAD_DIM)
        mine = lax.psum_scatter(
            mine, "blk", scatter_dimension=1, axis_index_groups=head_groups(blk_size, groups)
        )
    return mine


def dot_nt(a, b):
    return lax.dot_general(a, b, (((1,), (1,)), ((), ())), preferred_element_type=single)


def key_loops(low_ref, open_ref, close_ref, high_ref, index, step, carry):
    low, opened = low_ref[index], open_ref[index]
    closed, high = close_ref[index], high_ref[index]
    carry = lax.fori_loop(low, opened, lambda kb, c: step(kb, c, True), carry)
    carry = lax.fori_loop(opened, closed, lambda kb, c: step(kb, c, False), carry)
    return lax.fori_loop(closed, high, lambda kb, c: step(kb, c, True), carry)


def allowed(start, pos, begin):
    key_at = start + lax.broadcasted_iota(jnp.int32, (KEY_ROWS, pos.shape[1]), 0)
    return (key_at <= pos) & (key_at >= begin)


def forward_kernel(low_ref, open_ref, close_ref, high_ref, pos_ref, begin_ref, q_ref, k_ref, vt_ref, o_ref, lse_ref):
    index = pl.program_id(0)
    query = q_ref[...]
    pos, begin = pos_ref[0], begin_ref[0]
    rows = query.shape[0]

    def step(block, carry, masked):
        top, total, acc = carry
        start = pl.multiple_of(block * KEY_ROWS, KEY_ROWS)
        scores = dot_nt(k_ref[pl.ds(start, KEY_ROWS), :], query) * LOG2_SCALE
        if masked:
            scores = jnp.where(allowed(start, pos, begin), scores, MASKED_SCORE)
        new_top = jnp.maximum(top, jnp.max(scores, axis=0, keepdims=True))
        probs = jnp.exp2(scores - new_top)
        shrink = jnp.exp2(top - new_top)
        total = total * shrink + jnp.sum(probs, axis=0, keepdims=True)
        acc = acc * shrink + jnp.dot(
            vt_ref[:, pl.ds(start, KEY_ROWS)], probs.astype(bfloat), preferred_element_type=single
        )
        return new_top, total, acc

    carry = (
        jnp.full((1, rows), MASKED_SCORE, single),
        jnp.zeros((1, rows), single),
        jnp.zeros((HEAD_DIM, rows), single),
    )
    top, total, acc = key_loops(low_ref, open_ref, close_ref, high_ref, index, step, carry)
    o_ref[...] = jnp.transpose(acc / total)
    lse_ref[0] = top + jnp.log2(total)


def backward_kernel(
    low_ref, open_ref, close_ref, high_ref, pos_ref, begin_ref, lse_ref, delta_ref,
    q_ref, do_ref, k_ref, v_ref, kt_ref, dq_ref, dk_ref, dv_ref,
):
    index = pl.program_id(0)

    @pl.when(index == 0)
    def _():
        dk_ref[...] = jnp.zeros_like(dk_ref)
        dv_ref[...] = jnp.zeros_like(dv_ref)

    query, d_out = q_ref[...], do_ref[...]
    pos, begin = pos_ref[0], begin_ref[0]
    lse, delta = lse_ref[0], delta_ref[0]

    def step(block, acc, masked):
        start = pl.multiple_of(block * KEY_ROWS, KEY_ROWS)
        rows = pl.ds(start, KEY_ROWS)
        scores = dot_nt(k_ref[rows, :], query) * LOG2_SCALE
        probs = jnp.exp2(scores - lse)
        if masked:
            probs = jnp.where(allowed(start, pos, begin), probs, 0.0)
        d_probs = dot_nt(v_ref[rows, :], d_out)
        d_scores = (probs * (d_probs - delta)).astype(bfloat)
        dv_ref[rows, :] += jnp.dot(probs.astype(bfloat), d_out, preferred_element_type=single)
        dk_ref[rows, :] += jnp.dot(d_scores, query, preferred_element_type=single)
        return acc + jnp.dot(kt_ref[:, rows], d_scores, preferred_element_type=single)

    acc = jnp.zeros((HEAD_DIM, query.shape[0]), single)
    acc = key_loops(low_ref, open_ref, close_ref, high_ref, index, step, acc)
    dq_ref[...] = jnp.transpose(acc) * SCORE_SCALE


def block_bounds(pos, begin):
    first, last = jnp.min(begin, axis=1), jnp.max(begin, axis=1)
    low = first // KEY_ROWS
    high = jnp.max(pos, axis=1) // KEY_ROWS + 1
    opened = jnp.clip((last + KEY_ROWS - 1) // KEY_ROWS, low, high)
    closed = jnp.clip((jnp.min(pos, axis=1) + 1) // KEY_ROWS, opened, high)
    return low, opened, closed, high


def row_spec(rows):
    return pl.BlockSpec((rows, HEAD_DIM), lambda i, *_: (i, 0))


def line_spec(rows):
    return pl.BlockSpec((1, 1, rows), lambda i, *_: (i, 0, 0))


def whole_spec(shape):
    return pl.BlockSpec(shape, lambda i, *_: (0, 0), pipeline_mode=pl.Buffered(1))


def attention_forward(bounds, pos, begin, query, key, value_t):
    blocks, rows = pos.shape
    keys = key.shape[0]
    return pl.pallas_call(
        forward_kernel,
        grid_spec=pltpu.PrefetchScalarGridSpec(
            num_scalar_prefetch=4,
            grid=(blocks,),
            in_specs=[
                line_spec(rows), line_spec(rows), row_spec(rows),
                whole_spec((keys, HEAD_DIM)), whole_spec((HEAD_DIM, keys)),
            ],
            out_specs=[row_spec(rows), line_spec(rows)],
        ),
        out_shape=[
            jax.ShapeDtypeStruct(query.shape, single),
            jax.ShapeDtypeStruct((blocks, 1, rows), single),
        ],
        compiler_params=pltpu.CompilerParams(vmem_limit_bytes=48 << 20),
        name="attention_forward",
    )(*bounds, pos[:, None], begin[:, None], query, key, value_t)


def attention_backward(bounds, pos, begin, lse, delta, query, d_out, key, value, key_t):
    blocks, rows = pos.shape
    keys = key.shape[0]
    return pl.pallas_call(
        backward_kernel,
        grid_spec=pltpu.PrefetchScalarGridSpec(
            num_scalar_prefetch=4,
            grid=(blocks,),
            in_specs=[
                line_spec(rows), line_spec(rows), line_spec(rows), line_spec(rows),
                row_spec(rows), row_spec(rows),
                whole_spec((keys, HEAD_DIM)), whole_spec((keys, HEAD_DIM)),
                whole_spec((HEAD_DIM, keys)),
            ],
            out_specs=[
                row_spec(rows), whole_spec((keys, HEAD_DIM)), whole_spec((keys, HEAD_DIM)),
            ],
        ),
        out_shape=[
            jax.ShapeDtypeStruct(query.shape, single),
            jax.ShapeDtypeStruct(key.shape, single),
            jax.ShapeDtypeStruct(key.shape, single),
        ],
        compiler_params=pltpu.CompilerParams(vmem_limit_bytes=56 << 20),
        name="attention_backward",
    )(*bounds, pos[:, None], begin[:, None], lse, delta, query, d_out, key, value, key_t)


def per_device(
    block_input, w_query, w_key, w_value, w_out, attn_gain, ffn_gain, query_gain, key_gain,
    router, w_gate, w_up, w_down, expert_ids, slot_ids, doc_starts, cotangent,
):
    ulysses_size = lax.axis_size("ulysses")
    blk_size = lax.axis_size("blk")
    blk = lax.axis_index("blk")
    uly = lax.axis_index("ulysses")
    core = uly % 2
    own_tokens, width = block_input.shape
    picks = expert_ids.shape[1]
    experts = router.shape[1]
    capacity = 5 * own_tokens * picks // (4 * experts)
    local_experts = experts // blk_size
    blk_tokens = ulysses_size * own_tokens
    local_width = width // ulysses_size
    local_heads = local_width // HEAD_DIM
    weight_rows = w_query.shape[0]
    groups = blk_size // (2 * local_heads)

    projections = jnp.stack([w_query, w_key, w_value]).astype(bfloat)
    projections = projections.reshape(3, weight_rows, ulysses_size, local_width)
    projections = lax.all_to_all(
        jnp.transpose(projections, (2, 0, 1, 3)), "ulysses", split_axis=0, concat_axis=0, tiled=True
    )
    projections = lax.all_gather(projections, "blk", axis=0)
    projections = jnp.transpose(projections, (2, 1, 0, 3, 4)).reshape(3, width, local_width)
    w_q, w_k, w_v = projections[0], projections[1], projections[2]
    w_o = lax.all_gather(w_out.astype(bfloat), "blk", axis=0, tiled=True)
    small = jnp.concatenate(
        [jnp.stack([attn_gain, ffn_gain, query_gain, key_gain]), router.T]
    ).astype(bfloat)
    small = lax.all_gather(small, ("ulysses", "blk"), axis=1, tiled=True)
    attn_g = small[0].astype(single)
    ffn_g = small[1].astype(single)
    query_g = lax.dynamic_slice_in_dim(small[2], uly * local_width, local_width).astype(single)
    key_g = lax.dynamic_slice_in_dim(small[3], uly * local_width, local_width).astype(single)
    router_t = small[4:]

    def gather_expert(weight, axis):
        mine = weight.astype(bfloat)
        beyond = swap(mine, 2)
        near = swap(mine, 1)
        far = swap(beyond, 1)
        return jnp.concatenate([mine, near, beyond, far], axis=axis)

    expert_gate = gather_expert(w_gate, 2)
    expert_up = gather_expert(w_up, 2)
    expert_down = gather_expert(w_down, 1)

    named = expert_ids[:, :, None] == jnp.arange(experts, dtype=jnp.int32)[None, None, :]
    slot_map = jnp.sum(jnp.where(named, slot_ids[:, :, None] + 1, 0), axis=1)
    slot_map = slot_map.T.astype(single).reshape(blk_size, local_experts, own_tokens)
    slot_map = lax.all_to_all(slot_map, "blk", split_axis=0, concat_axis=0, tiled=True)
    slot_at = jnp.arange(1, capacity + 1, dtype=jnp.int32).astype(single)
    picked = jnp.transpose(slot_map, (1, 0, 2))[:, :, None, :] == slot_at[None, None, :, None]
    picked_low = picked.astype(bfloat)

    inputs = block_input.astype(single)
    hat_one, recip_one = norm_parts(inputs)
    normed = gather_ulysses((hat_one * attn_g).astype(bfloat)).reshape(blk_tokens, width)
    q_lin = jnp.dot(normed, w_q, preferred_element_type=single)
    k_lin = jnp.dot(normed, w_k, preferred_element_type=single)
    v_lin = jnp.dot(normed, w_v, preferred_element_type=single)
    squares = jnp.stack([jnp.sum(q_lin * q_lin, axis=1), jnp.sum(k_lin * k_lin, axis=1)])
    recips = lax.rsqrt(sum_ulysses(squares) / width + NORM_EPSILON)
    q_recip, k_recip = recips[0][:, None], recips[1][:, None]
    q_hat, k_hat = q_lin * q_recip, k_lin * k_recip
    blk_at = blk * blk_tokens + jnp.arange(blk_tokens, dtype=jnp.int32)
    cosine_table, sine_table = angles(blk_at - doc_begins(doc_starts, blk_at), HEAD_DIM)

    def by_heads(fun, values):
        shaped = fun(values.reshape(blk_tokens, -1, HEAD_DIM), cosine_table, sine_table)
        return shaped.reshape(blk_tokens, local_width)

    q_rot = by_heads(rotate, q_hat * query_g).astype(bfloat)
    k_rot = by_heads(rotate, k_hat * key_g).astype(bfloat)
    heads_in = to_heads([q_rot, k_rot, v_lin.astype(bfloat)], blk_size)
    query = heads_in[:, 0].reshape(-1, HEAD_DIM)
    key = gather_keys(heads_in[:, 1], blk_size, groups)
    value = gather_keys(heads_in[:, 2], blk_size, groups)
    part_rows = heads_in.shape[2]
    query_at = (
        jnp.arange(blk_size, dtype=jnp.int32)[:, None] * blk_tokens
        + core * (blk_tokens // 2)
        + blk % groups * part_rows
        + jnp.arange(part_rows, dtype=jnp.int32)[None, :]
    ).reshape(-1, QUERY_ROWS)
    query_begin = doc_begins(doc_starts, query_at)
    bounds = block_bounds(query_at, query_begin)
    head_out, lse = attention_forward(bounds, query_at, query_begin, query, key, value.T)
    attended, = from_heads(
        head_out.astype(bfloat).reshape(blk_size, 1, part_rows, HEAD_DIM), blk_size, local_heads
    )
    out_part = jnp.dot(attended, w_o, preferred_element_type=single)

    def token_rows(values):
        return lambda bits: lax.dynamic_slice_in_dim(
            values, (uly ^ bits) * own_tokens, own_tokens, 0
        )

    residual_mid = inputs + scatter_sum_ulysses(token_rows(out_part))
    hat_two, recip_two = norm_parts(residual_mid)
    ffn_in = (hat_two * ffn_g).astype(bfloat)

    ffn_all = lax.all_gather(ffn_in, "blk", axis=0)
    cot_all = lax.all_gather(cotangent, "blk", axis=0)
    logits = dot_nt(ffn_all.reshape(-1, width), router_t)
    shifted_logits = jnp.exp(logits - jnp.max(logits, axis=1, keepdims=True))
    probs_all = shifted_logits / jnp.sum(shifted_logits, axis=1, keepdims=True)
    probs_all = probs_all.reshape(blk_size, own_tokens, experts)
    router_probs = lax.dynamic_index_in_dim(probs_all, blk, 0, keepdims=False)
    local_probs = lax.dynamic_slice_in_dim(probs_all, blk * local_experts, local_experts, 2)
    gate_rows = jnp.sum(
        jnp.where(picked, jnp.transpose(local_probs, (2, 0, 1))[:, :, None, :], 0.0), axis=3
    ).reshape(local_experts, -1, 1)

    def dispatch(rows):
        return jnp.einsum("esct,std->escd", picked_low, rows, preferred_element_type=single).astype(
            bfloat
        ).reshape(local_experts, -1, width)

    def combine(rows):
        rows = rows.reshape(local_experts, blk_size, capacity, width)
        total = jnp.einsum("esct,escd->std", picked_low, rows, preferred_element_type=single)
        return lax.psum_scatter(
            total.astype(bfloat), "blk", scatter_dimension=0
        ).astype(single)

    received = dispatch(ffn_all)
    cot_rows = dispatch(cot_all).astype(single)
    d_expert_out = (gate_rows * cot_rows).astype(bfloat)
    gate_val = jnp.einsum("erd,edf->erf", received, expert_gate, preferred_element_type=single)
    up_val = jnp.einsum("erd,edf->erf", received, expert_up, preferred_element_type=single)
    sigmoid_gate = jax.nn.sigmoid(gate_val)
    hidden_low = (gate_val * sigmoid_gate * up_val).astype(bfloat)
    d_hidden = jnp.einsum("erd,efd->erf", d_expert_out, expert_down, preferred_element_type=single)
    d_gate = (d_hidden * up_val * sigmoid_gate * (1.0 + gate_val * (1.0 - sigmoid_gate))).astype(
        bfloat
    )
    d_up = (d_hidden * gate_val * sigmoid_gate).astype(bfloat)
    d_received = (
        jnp.einsum("erf,edf->erd", d_gate, expert_gate, preferred_element_type=single)
        + jnp.einsum("erf,edf->erd", d_up, expert_up, preferred_element_type=single)
    ).astype(bfloat)
    d_ffn_in = combine(d_received)
    expert_out = jnp.einsum(
        "erf,efd->erd", hidden_low, expert_down, preferred_element_type=single
    ).astype(bfloat).astype(single)
    d_gate_rows = jnp.sum(cot_rows * expert_out, axis=2).reshape(
        local_experts, blk_size, capacity, 1
    )
    d_probs = jnp.transpose(jnp.sum(jnp.where(picked, d_gate_rows, 0.0), axis=2), (1, 0, 2))
    d_probs = lax.all_to_all(d_probs, "blk", split_axis=0, concat_axis=0, tiled=True)
    d_probs = d_probs.reshape(experts, own_tokens).T
    mixed = residual_mid + combine((gate_rows * expert_out).astype(bfloat))
    grad_gate_part = jnp.einsum("erd,erf->edf", received, d_gate, preferred_element_type=single)
    grad_up_part = jnp.einsum("erd,erf->edf", received, d_up, preferred_element_type=single)
    grad_down_part = jnp.einsum(
        "erf,erd->efd", hidden_low, d_expert_out, preferred_element_type=single
    )

    def scatter_expert(total, axis):
        size = total.shape[axis] // ulysses_size
        return scatter_sum_ulysses(
            lambda bits: lax.slice_in_dim(total, bits * size, (bits + 1) * size, axis=axis)
        )

    grad_w_gate = scatter_expert(grad_gate_part, 2)
    grad_w_up = scatter_expert(grad_up_part, 2)
    grad_w_down = scatter_expert(grad_down_part, 1)

    d_logits = (
        router_probs * (d_probs - jnp.sum(router_probs * d_probs, axis=1, keepdims=True))
    ).astype(bfloat)
    grad_router_part = jnp.einsum("td,te->de", ffn_in, d_logits, preferred_element_type=single)
    d_ffn_in = d_ffn_in + jnp.dot(d_logits, router_t, preferred_element_type=single)
    grad_ffn_part = jnp.sum(d_ffn_in * hat_two, axis=0)
    d_mid = cotangent.astype(single) + norm_back(d_ffn_in * ffn_g, hat_two, recip_two)

    d_attn_out = gather_ulysses(d_mid.astype(bfloat)).reshape(blk_tokens, width)
    d_attended = dot_nt(d_attn_out, w_o).astype(bfloat)
    grad_out_part = jnp.einsum("ti,to->io", attended, d_attn_out, preferred_element_type=single)
    d_out = to_heads([d_attended], blk_size).reshape(-1, HEAD_DIM)
    delta = jnp.sum(d_out.astype(single) * head_out, axis=1).reshape(lse.shape)
    dq_head, dk_head, dv_head = attention_backward(
        bounds, query_at, query_begin, lse, delta, query, d_out, key, value, key.T
    )
    dq_part = dq_head.astype(bfloat).reshape(blk_size, part_rows, HEAD_DIM)
    dk_part = scatter_keys(dk_head * SCORE_SCALE, blk_size, groups)
    dv_part = scatter_keys(dv_head, blk_size, groups)
    dq_rows, dk_rows, dv_rows = from_heads(
        jnp.stack([dq_part, dk_part, dv_part], 1), blk_size, local_heads
    )
    dq_norm = by_heads(rotate_back, dq_rows.astype(single))
    dk_norm = by_heads(rotate_back, dk_rows.astype(single))
    gain_parts = jnp.stack(
        [jnp.sum(dq_norm * q_hat, axis=0), jnp.sum(dk_norm * k_hat, axis=0)]
    )
    dq_norm, dk_norm = dq_norm * query_g, dk_norm * key_g
    means = sum_ulysses(
        jnp.stack([jnp.sum(dq_norm * q_hat, axis=1), jnp.sum(dk_norm * k_hat, axis=1)])
    ) / width
    d_q_lin = (q_recip * (dq_norm - q_hat * means[0][:, None])).astype(bfloat)
    d_k_lin = (k_recip * (dk_norm - k_hat * means[1][:, None])).astype(bfloat)
    d_normed_part = dot_nt(d_q_lin, w_q) + dot_nt(d_k_lin, w_k) + dot_nt(dv_rows, w_v)
    d_normed = scatter_sum_ulysses(token_rows(d_normed_part))
    grad_attn_part = jnp.sum(d_normed * hat_one, axis=0)
    input_grad = d_mid + norm_back(d_normed * attn_g, hat_one, recip_one)

    def grad_projection(d_lin):
        part = jnp.einsum("td,to->do", normed, d_lin, preferred_element_type=single)
        return part.astype(bfloat).reshape(ulysses_size, blk_size, weight_rows, local_width)

    grads = jnp.stack([grad_projection(d_q_lin), grad_projection(d_k_lin), grad_projection(dv_rows)])
    grads = lax.psum_scatter(
        jnp.transpose(grads, (2, 1, 0, 3, 4)), "blk", scatter_dimension=0
    )
    grads = lax.all_to_all(grads, "ulysses", split_axis=0, concat_axis=0, tiled=True)
    grads = jnp.transpose(grads, (1, 2, 0, 3)).reshape(3, weight_rows, width).astype(single)
    grad_w_out = lax.psum_scatter(
        grad_out_part.astype(bfloat), "blk", scatter_dimension=0, tiled=True
    ).astype(single)
    gain_grads = lax.psum_scatter(gain_parts, "blk", scatter_dimension=1, tiled=True)
    both = ("ulysses", "blk")
    wide = jnp.concatenate([jnp.stack([grad_attn_part, grad_ffn_part]), grad_router_part.T])
    wide = lax.psum_scatter(wide, both, scatter_dimension=1, tiled=True)
    return (
        mixed.astype(bfloat),
        input_grad.astype(bfloat),
        grads[0],
        grads[1],
        grads[2],
        grad_w_out,
        wide[0],
        wide[1],
        gain_grads[0],
        gain_grads[1],
        wide[2:].T,
        grad_w_gate,
        grad_w_up,
        grad_w_down,
    )


def solution(mesh):
    in_specs = (
        P(("blk", "ulysses"), None),
        P(("ulysses", "blk"), None),
        P(("ulysses", "blk"), None),
        P(("ulysses", "blk"), None),
        P(("ulysses", "blk"), None),
        P(("ulysses", "blk")),
        P(("ulysses", "blk")),
        P(("ulysses", "blk")),
        P(("ulysses", "blk")),
        P(("ulysses", "blk"), None),
        P("blk", None, "ulysses"),
        P("blk", None, "ulysses"),
        P("blk", "ulysses", None),
        P(("blk", "ulysses"), None),
        P(("blk", "ulysses"), None),
        P(),
        P(("blk", "ulysses"), None),
    )
    out_specs = (
        P(("blk", "ulysses"), None),
        P(("blk", "ulysses"), None),
        P(("ulysses", "blk"), None),
        P(("ulysses", "blk"), None),
        P(("ulysses", "blk"), None),
        P(("ulysses", "blk"), None),
        P(("ulysses", "blk")),
        P(("ulysses", "blk")),
        P(("ulysses", "blk")),
        P(("ulysses", "blk")),
        P(("ulysses", "blk"), None),
        P("blk", None, "ulysses"),
        P("blk", None, "ulysses"),
        P("blk", "ulysses", None),
    )
    return jax.shard_map(
        per_device, mesh=mesh, in_specs=in_specs, out_specs=out_specs, check_vma=False
    )
```

```python
import math

import jax
import jax.numpy as jnp
from jax import lax
from jax.experimental import pallas as pl
from jax.experimental.pallas import tpu as pltpu
from jax.sharding import PartitionSpec as P

HEAD_DIM = 128
NORM_EPSILON = 1e-05
ROPE_BASE = 10000.0
MASKED_SCORE = -1e30
SCORE_SCALE = HEAD_DIM ** (-0.5)
LOG2_SCALE = SCORE_SCALE * math.log2(math.e)
QUERY_ROWS = 256
HALF_ROWS = 256
KEY_ROWS = 512
BLK = ("far", "near")
PLANE = ("ulysses", "near")
bfloat = jnp.bfloat16
single = jnp.float32


def norm_parts(values):
    recip_factor = lax.rsqrt(jnp.mean(values * values, axis=-1, keepdims=True) + NORM_EPSILON)
    return (values * recip_factor, recip_factor)


def norm_back(grad_in, hat_values, recip_factor):
    return recip_factor * (
        grad_in - hat_values * jnp.mean(grad_in * hat_values, axis=-1, keepdims=True)
    )


def doc_begins(doc_starts, tokens_at):
    at_or_before = doc_starts[:, None] <= tokens_at.reshape(1, -1)
    begins = jnp.max(jnp.where(at_or_before, doc_starts[:, None], 0), axis=0)
    return begins.reshape(tokens_at.shape)


def angles(position, head_size):
    half_size = head_size // 2
    frequency = ROPE_BASE ** (-(jnp.arange(half_size, dtype=jnp.float32) * 2.0 / head_size))
    turn = position.astype(jnp.float32)[:, None] * frequency[None, :]
    cosine, sine = jnp.cos(turn), jnp.sin(turn)
    return jnp.concatenate([cosine, cosine], 1), jnp.concatenate([-sine, sine], 1)


def swap(values, bit, axis="ulysses"):
    size = lax.axis_size(axis)
    return lax.ppermute(values, axis, [(i, i ^ bit) for i in range(size)])


def gather_plane(values):
    me, side = lax.axis_index("ulysses"), lax.axis_index("near")
    near = swap(values, 1, "near")
    beyond = swap(values, 2)
    corner = swap(beyond, 1, "near")
    out = jnp.zeros((2, 4) + values.shape, values.dtype)
    for other, bit, part in ((0, 0, values), (0, 2, beyond), (1, 0, near), (1, 2, corner)):
        for core, piece in ((0, part), (1, swap(part, 1))):
            place = (side ^ other, me ^ bit ^ core) + (0,) * values.ndim
            out = lax.dynamic_update_slice(out, piece[None, None], place)
    return out


def line_steps(size):
    for step in range(1, size):
        up = [(i, i + 1) for i in range(step - 1, size - 1)]
        yield up, [(size - 1 - i, size - 1 - j) for i, j in up]


def gather_line(values, axis):
    size = lax.axis_size("far")
    if size > 4:
        return lax.all_gather(values, "far", axis=axis)
    at = lax.axis_index("far")
    below, above, parts = values, values, []
    for step, (up, down) in enumerate(line_steps(size), 1):
        below, above = lax.ppermute(below, "far", up), lax.ppermute(above, "far", down)
        parts = [(at - step, below), (at + step, above)] + parts
    shape = values.shape[:axis] + (size,) + values.shape[axis:]
    out = jnp.zeros(shape, values.dtype)
    for place, part in parts + [(at, values)]:
        out = lax.dynamic_update_index_in_dim(out, part, jnp.clip(place, 0, size - 1), axis)
    return out


def gather_ulysses(values):
    me = lax.axis_index("ulysses")
    beyond = swap(values, 2)
    core = swap(values, 1)
    beyond_core = swap(beyond, 1)
    out = jnp.zeros((4,) + values.shape, values.dtype)
    for bit, part in enumerate((values, core, beyond, beyond_core)):
        out = lax.dynamic_update_index_in_dim(out, part, me ^ bit, 0)
    return out


def scatter_sum_ulysses(parts, kind=bfloat):
    far = swap(parts(3).astype(kind), 1)
    near = swap(parts(1).astype(kind), 1)
    across = swap((parts(2) + far.astype(single)).astype(kind), 2)
    return parts(0) + near.astype(single) + across.astype(single)


def scatter_sum_plane(parts, beside):
    kept, sent = [], []
    for bits in (0, 2):
        mine, other = parts(bits)
        core_mine, core_other = parts(bits ^ 1)
        got = swap(jnp.stack([core_mine, core_other]).astype(bfloat), 1).astype(single)
        kept.append(mine + got[0])
        sent.append(other + got[1])
    got = swap(jnp.stack(sent).astype(bfloat), 1, "near").astype(single)
    got, beside = tie(got, beside)
    across = swap((kept[1] + got[1]).astype(bfloat), 2)
    return kept[0] + got[0] + across.astype(single), beside


def gather_small(values):
    count, size = values.shape
    blk_size = lax.axis_size(BLK)
    out = lax.all_to_all(
        jnp.broadcast_to(values, (blk_size, count, size)), BLK, split_axis=0, concat_axis=0, tiled=True
    )
    out = jnp.transpose(out, (1, 0, 2)).reshape(count, blk_size * size)
    return jnp.transpose(gather_ulysses(out), (1, 0, 2)).reshape(count, -1)


def scatter_sum_blk_small(values):
    count, blk_size = values.shape[0], lax.axis_size(BLK)
    parts = jnp.transpose(values.reshape(count, blk_size, -1), (1, 0, 2))
    parts = lax.all_to_all(parts, BLK, split_axis=0, concat_axis=0, tiled=True)
    return jnp.sum(parts, axis=0)


def tie(*values):
    return lax.optimization_barrier(values)


def sum_plane(values):
    values = values + swap(values, 1)
    values = values + swap(values, 2)
    return values + swap(values, 1, "near")


def swap_halves(values, core):
    got = swap(lax.dynamic_index_in_dim(values, 1 - core, 0, keepdims=False), 1)
    return lax.dynamic_update_index_in_dim(values, got, 1 - core, 0)


def line_to_heads(split, far_size):
    count, rows = split.shape[4:6]
    both = swap_halves(split, lax.axis_index("ulysses") % 2)
    both = both.reshape(far_size, 2, count, rows, HEAD_DIM)
    both = lax.all_to_all(both, "far", split_axis=0, concat_axis=0, tiled=True)
    return both.reshape(2 * far_size, count, rows, HEAD_DIM)


def line_from_heads(stacked, far_size):
    count, rows = stacked.shape[1:3]
    back = stacked.reshape(far_size, 2, count, rows, HEAD_DIM)
    back = lax.all_to_all(back, "far", split_axis=0, concat_axis=0, tiled=True)
    back = back.reshape(2, 2, far_size // 4, 2, count, rows, HEAD_DIM)
    return swap_halves(back, lax.axis_index("ulysses") % 2)


def blk_to_heads(values, blk_size):
    core = lax.axis_index("ulysses") % 2
    groups = blk_size // 8
    rows = values.shape[0] // (2 * groups)
    split = values.reshape(2, groups, rows, 2, 2, HEAD_DIM)
    split = jnp.transpose(split, (0, 4, 1, 3, 2, 5))
    both = swap_halves(split, core).reshape(blk_size, rows, HEAD_DIM)
    return lax.all_to_all(both, BLK, split_axis=0, concat_axis=0, tiled=True)


def blk_from_heads(stacked, blk_size):
    core = lax.axis_index("ulysses") % 2
    groups, rows = blk_size // 8, stacked.shape[1]
    back = lax.all_to_all(stacked, BLK, split_axis=0, concat_axis=0, tiled=True)
    whole = swap_halves(back.reshape(2, 2, groups, 2, rows, HEAD_DIM), core)
    whole = jnp.transpose(whole, (0, 2, 4, 3, 1, 5))
    return whole.reshape(2 * groups * rows, 4 * HEAD_DIM)


def head_groups(far_size, groups):
    return [[j * groups + p for p in range(groups)] for j in range(far_size // groups)]


def dot_nt(a, b):
    return lax.dot_general(a, b, (((1,), (1,)), ((), ())), preferred_element_type=single)


def key_loops(low_ref, open_ref, close_ref, high_ref, index, step, carry):
    low, opened = low_ref[index], open_ref[index]
    closed, high = close_ref[index], high_ref[index]
    carry = lax.fori_loop(low, opened, lambda kb, c: step(kb, c, True), carry)
    carry = lax.fori_loop(opened, closed, lambda kb, c: step(kb, c, False), carry)
    return lax.fori_loop(closed, high, lambda kb, c: step(kb, c, True), carry)


def allowed(start, pos, begin):
    key_at = start + lax.broadcasted_iota(jnp.int32, (KEY_ROWS, pos.shape[1]), 0)
    return (key_at <= pos) & (key_at >= begin)


def load_keys(core, mine_ref, other_ref, at, store):
    for blk in range(mine_ref.shape[0]):
        start = 2 * blk * HALF_ROWS
        store(pl.multiple_of(start + core * HALF_ROWS, HALF_ROWS), mine_ref[blk, at])
        store(pl.multiple_of(start + (1 - core) * HALF_ROWS, HALF_ROWS), other_ref[blk, at - mine_ref.shape[1] + 2])


def forward_kernel(
    core_ref, low_ref, open_ref, close_ref, high_ref,
    pos_ref, begin_ref, q_ref, mine_ref, other_ref, o_ref, lse_ref, k_ref, vt_ref,
):
    index = pl.program_id(0)

    @pl.when(index == 0)
    def _():
        core, last = core_ref[0], mine_ref.shape[1]

        def store_key(start, rows):
            k_ref[pl.ds(start, HALF_ROWS), :] = rows

        def store_value(start, rows):
            vt_ref[:, pl.ds(start, HALF_ROWS)] = jnp.transpose(rows)

        load_keys(core, mine_ref, other_ref, last - 2, store_key)
        load_keys(core, mine_ref, other_ref, last - 1, store_value)

    query = q_ref[0, 0]
    pos, begin = pos_ref[0], begin_ref[0]
    rows = query.shape[0]

    def step(block, carry, masked):
        top, total, acc = carry
        start = pl.multiple_of(block * KEY_ROWS, KEY_ROWS)
        scores = dot_nt(k_ref[pl.ds(start, KEY_ROWS), :], query) * LOG2_SCALE
        if masked:
            scores = jnp.where(allowed(start, pos, begin), scores, MASKED_SCORE)
        new_top = jnp.maximum(top, jnp.max(scores, axis=0, keepdims=True))
        probs = jnp.exp2(scores - new_top)
        shrink = jnp.exp2(top - new_top)
        total = total * shrink + jnp.sum(probs, axis=0, keepdims=True)
        acc = acc * shrink + jnp.dot(
            vt_ref[:, pl.ds(start, KEY_ROWS)], probs.astype(bfloat), preferred_element_type=single
        )
        return new_top, total, acc

    carry = (
        jnp.full((1, rows), MASKED_SCORE, single),
        jnp.zeros((1, rows), single),
        jnp.zeros((HEAD_DIM, rows), single),
    )
    top, total, acc = key_loops(low_ref, open_ref, close_ref, high_ref, index, step, carry)
    o_ref[0] = jnp.transpose(acc / total)
    lse_ref[0] = top + jnp.log2(total)


def backward_kernel(
    core_ref, low_ref, open_ref, close_ref, high_ref, pos_ref, begin_ref, lse_ref, o_ref,
    q_ref, do_ref, mine_ref, other_ref, dq_ref, keep_ref, send_ref, k_ref, v_ref, kt_ref, dk_ref, dv_ref,
):
    index = pl.program_id(0)
    core = core_ref[0]

    @pl.when(index == 0)
    def _():
        dk_ref[...] = jnp.zeros_like(dk_ref)
        dv_ref[...] = jnp.zeros_like(dv_ref)
        last = mine_ref.shape[1]

        def store_key(start, rows):
            k_ref[pl.ds(start, HALF_ROWS), :] = rows
            kt_ref[:, pl.ds(start, HALF_ROWS)] = jnp.transpose(rows)

        def store_value(start, rows):
            v_ref[pl.ds(start, HALF_ROWS), :] = rows

        load_keys(core, mine_ref, other_ref, last - 2, store_key)
        load_keys(core, mine_ref, other_ref, last - 1, store_value)

    query, d_out = q_ref[0, 0], do_ref[0]
    pos, begin = pos_ref[0], begin_ref[0]
    lse = lse_ref[0]
    products = d_out.astype(single) * o_ref[0]
    delta = jnp.sum(jnp.transpose(products), axis=0, keepdims=True)

    def step(block, acc, masked):
        start = pl.multiple_of(block * KEY_ROWS, KEY_ROWS)
        rows = pl.ds(start, KEY_ROWS)
        scores = dot_nt(k_ref[rows, :], query) * LOG2_SCALE
        probs = jnp.exp2(scores - lse)
        if masked:
            probs = jnp.where(allowed(start, pos, begin), probs, 0.0)
        d_probs = dot_nt(v_ref[rows, :], d_out)
        d_scores = (probs * (d_probs - delta)).astype(bfloat)
        dv_ref[rows, :] += jnp.dot(probs.astype(bfloat), d_out, preferred_element_type=single)
        dk_ref[rows, :] += jnp.dot(d_scores, query, preferred_element_type=single)
        return acc + jnp.dot(kt_ref[:, rows], d_scores, preferred_element_type=single)

    acc = jnp.zeros((HEAD_DIM, query.shape[0]), single)
    acc = key_loops(low_ref, open_ref, close_ref, high_ref, index, step, acc)
    dq_ref[0] = (jnp.transpose(acc) * SCORE_SCALE).astype(bfloat)

    @pl.when(index == pl.num_programs(0) - 1)
    def _():
        for blk in range(keep_ref.shape[0]):
            start = 2 * blk * HALF_ROWS
            mine = pl.ds(pl.multiple_of(start + core * HALF_ROWS, HALF_ROWS), HALF_ROWS)
            other = pl.ds(pl.multiple_of(start + (1 - core) * HALF_ROWS, HALF_ROWS), HALF_ROWS)
            keep_ref[blk, 0] = dk_ref[mine, :] * SCORE_SCALE
            keep_ref[blk, 1] = dv_ref[mine, :]
            send_ref[blk, 0] = (dk_ref[other, :] * SCORE_SCALE).astype(bfloat)
            send_ref[blk, 1] = dv_ref[other, :].astype(bfloat)


def block_bounds(pos, begin):
    first, last = jnp.min(begin, axis=1), jnp.max(begin, axis=1)
    low = first // KEY_ROWS
    high = jnp.max(pos, axis=1) // KEY_ROWS + 1
    opened = jnp.clip((last + KEY_ROWS - 1) // KEY_ROWS, low, high)
    closed = jnp.clip((jnp.min(pos, axis=1) + 1) // KEY_ROWS, opened, high)
    return low, opened, closed, high


def block_spec(shape):
    return pl.BlockSpec((1,) + shape[1:], lambda i, *_: (i,) + (0,) * (len(shape) - 1))


def first_spec(shape):
    return pl.BlockSpec((1, 1) + shape[2:], lambda i, *_: (i,) + (0,) * (len(shape) - 1))


def whole_spec(shape):
    return pl.BlockSpec(shape, lambda *_: (0,) * len(shape), pipeline_mode=pl.Buffered(1))


def attention_forward(scalars, pos, begin, query, mine, other):
    blocks, _, rows = pos.shape
    keys = 2 * mine.shape[0] * HALF_ROWS
    out_shape = [
        jax.ShapeDtypeStruct((blocks, rows, HEAD_DIM), single),
        jax.ShapeDtypeStruct(pos.shape, single),
    ]
    return pl.pallas_call(
        forward_kernel,
        grid_spec=pltpu.PrefetchScalarGridSpec(
            num_scalar_prefetch=5,
            grid=(blocks,),
            in_specs=[
                block_spec(pos.shape), block_spec(pos.shape), first_spec(query.shape),
                whole_spec(mine.shape), whole_spec(other.shape),
            ],
            out_specs=[block_spec(out.shape) for out in out_shape],
            scratch_shapes=[pltpu.VMEM((keys, HEAD_DIM), bfloat), pltpu.VMEM((HEAD_DIM, keys), bfloat)],
        ),
        out_shape=out_shape,
        compiler_params=pltpu.CompilerParams(vmem_limit_bytes=48 << 20),
        name="attention_forward",
    )(*scalars, pos, begin, query, mine, other)


def attention_backward(scalars, pos, begin, lse, head_out, query, d_out, mine, other):
    blocks, _, rows = pos.shape
    keys = 2 * mine.shape[0] * HALF_ROWS
    pair = (mine.shape[0], 2, HALF_ROWS, HEAD_DIM)
    out_shape = [
        jax.ShapeDtypeStruct(d_out.shape, bfloat),
        jax.ShapeDtypeStruct(pair, single),
        jax.ShapeDtypeStruct(pair, bfloat),
    ]
    return pl.pallas_call(
        backward_kernel,
        grid_spec=pltpu.PrefetchScalarGridSpec(
            num_scalar_prefetch=5,
            grid=(blocks,),
            in_specs=[
                block_spec(pos.shape), block_spec(pos.shape), block_spec(pos.shape),
                block_spec(head_out.shape), first_spec(query.shape), block_spec(d_out.shape),
                whole_spec(mine.shape), whole_spec(other.shape),
            ],
            out_specs=[block_spec(d_out.shape), whole_spec(pair), whole_spec(pair)],
            scratch_shapes=[
                pltpu.VMEM((keys, HEAD_DIM), bfloat), pltpu.VMEM((keys, HEAD_DIM), bfloat),
                pltpu.VMEM((HEAD_DIM, keys), bfloat),
                pltpu.VMEM((keys, HEAD_DIM), single), pltpu.VMEM((keys, HEAD_DIM), single),
            ],
        ),
        out_shape=out_shape,
        compiler_params=pltpu.CompilerParams(vmem_limit_bytes=60 << 20),
        name="attention_backward",
    )(*scalars, pos, begin, lse, head_out, query, d_out, mine, other)


def turned(values, cosine, sine):
    return values * cosine + pltpu.roll(values, HEAD_DIM // 2, 1) * sine


def rotate_kernel(lin_ref, recip_ref, gain_ref, cosine_ref, sine_ref, out_ref):
    groups, rows = out_ref.shape[2], out_ref.shape[5]
    cosine, sine = cosine_ref[...], sine_ref[...]
    for which in range(3):
        for head in range(2):
            at = head * HEAD_DIM
            values = lin_ref[:, pl.ds((2 * which + head) * HEAD_DIM, HEAD_DIM)]
            if which < 2:
                values = values * recip_ref[:, which : which + 1]
                values = values * gain_ref[which : which + 1, at : at + HEAD_DIM]
                values = turned(values, cosine, sine)
            values = values.astype(bfloat)
            for group in range(groups):
                out_ref[0, head, group, 0, which] = values[group * rows : (group + 1) * rows]


def back_parts(d_ref, lin_ref, recip_ref, gain_ref, cosine, sine, which, head):
    at = head * HEAD_DIM
    grad = d_ref[0, head, :, 0, which].reshape(-1, HEAD_DIM).astype(single)
    grad = turned(grad, cosine, -sine)
    hat = lin_ref[:, pl.ds((2 * which + head) * HEAD_DIM, HEAD_DIM)] * recip_ref[:, which : which + 1]
    return grad, grad * gain_ref[which : which + 1, at : at + HEAD_DIM], hat


def sums_kernel(d_ref, lin_ref, recip_ref, gain_ref, cosine_ref, sine_ref, gain_out_ref, sum_ref):
    first = (pl.program_id(0) == 0) & (pl.program_id(1) == 0)

    @pl.when(first)
    def _():
        gain_out_ref[...] = jnp.zeros_like(gain_out_ref)

    cosine, sine = cosine_ref[...], sine_ref[...]
    for which in range(2):
        total = None
        for head in range(2):
            grad, scaled, hat = back_parts(
                d_ref, lin_ref, recip_ref, gain_ref, cosine, sine, which, head
            )
            at = pl.ds(head * HEAD_DIM, HEAD_DIM)
            gain_out_ref[which : which + 1, at] += jnp.sum(grad * hat, axis=0, keepdims=True)
            product = jnp.transpose(scaled * hat)
            product = jnp.sum(product, axis=0, keepdims=True)
            total = product if total is None else total + product
        sum_ref[0, 0, which : which + 1, :] = total


def lin_kernel(d_ref, lin_ref, recip_ref, mean_ref, gain_ref, cosine_ref, sine_ref, out_ref):
    cosine, sine = cosine_ref[...], sine_ref[...]
    for head in range(2):
        for which in range(2):
            _, scaled, hat = back_parts(
                d_ref, lin_ref, recip_ref, gain_ref, cosine, sine, which, head
            )
            grad = recip_ref[:, which : which + 1] * (scaled - hat * mean_ref[:, which : which + 1])
            out_ref[:, pl.ds((2 * which + head) * HEAD_DIM, HEAD_DIM)] = grad.astype(bfloat)
        out_ref[:, pl.ds((4 + head) * HEAD_DIM, HEAD_DIM)] = d_ref[0, head, :, 0, 2].reshape(
            -1, HEAD_DIM
        )


def token_spec(columns):
    return pl.BlockSpec((HALF_ROWS, columns), lambda near, half: (2 * near + half, 0))


def split_spec(groups, rows):
    return pl.BlockSpec(
        (1, 2, groups, 1, 3, rows, HEAD_DIM), lambda near, half: (half, 0, 0, near, 0, 0, 0)
    )


def project_kernel(rows_ref, weight_ref, lin_ref, sum_ref):
    part = weight_ref.shape[1] // 3
    lin = jnp.dot(rows_ref[...], weight_ref[...], preferred_element_type=single)
    lin_ref[...] = lin
    for which in range(2):
        values = lin[:, which * part : (which + 1) * part]
        sum_ref[0, 0, which : which + 1, :] = jnp.sum(
            jnp.transpose(values * values), axis=0, keepdims=True
        )


def projected(rows, weight):
    return pl.pallas_call(
        project_kernel,
        grid=(2, 2),
        in_specs=[token_spec(rows.shape[1]), whole_spec(weight.shape)],
        out_specs=[
            token_spec(weight.shape[1]),
            pl.BlockSpec((1, 1, 2, HALF_ROWS), lambda near, half: (near, half, 0, 0)),
        ],
        out_shape=[
            jax.ShapeDtypeStruct((rows.shape[0], weight.shape[1]), single),
            jax.ShapeDtypeStruct((2, 2, 2, HALF_ROWS), single),
        ],
        compiler_params=pltpu.CompilerParams(vmem_limit_bytes=32 << 20),
        name="projected",
    )(rows, weight)


def columns(values):
    return jnp.transpose(values, (0, 1, 3, 2)).reshape(-1, 2)


def rotated_heads(lin, recips, gains, cosine, sine, groups):
    rows = HALF_ROWS // groups
    return pl.pallas_call(
        rotate_kernel,
        grid=(2, 2),
        in_specs=[
            token_spec(lin.shape[1]), token_spec(2), whole_spec(gains.shape),
            token_spec(HEAD_DIM), token_spec(HEAD_DIM),
        ],
        out_specs=split_spec(groups, rows),
        out_shape=jax.ShapeDtypeStruct((2, 2, groups, 2, 3, rows, HEAD_DIM), bfloat),
        name="rotated_heads",
    )(lin, recips, gains, cosine, sine)


def rotated_sums(d_split, lin, recips, gains, cosine, sine):
    groups, rows = d_split.shape[2], d_split.shape[5]
    return pl.pallas_call(
        sums_kernel,
        grid=(2, 2),
        in_specs=[
            split_spec(groups, rows), token_spec(lin.shape[1]), token_spec(2),
            whole_spec(gains.shape), token_spec(HEAD_DIM), token_spec(HEAD_DIM),
        ],
        out_specs=[
            pl.BlockSpec(gains.shape, lambda near, half: (0, 0)),
            pl.BlockSpec((1, 1, 2, HALF_ROWS), lambda near, half: (near, half, 0, 0)),
        ],
        out_shape=[
            jax.ShapeDtypeStruct(gains.shape, single),
            jax.ShapeDtypeStruct((2, 2, 2, HALF_ROWS), single),
        ],
        name="rotated_sums",
    )(d_split, lin, recips, gains, cosine, sine)


def rotated_back(d_split, lin, recips, means, gains, cosine, sine):
    groups, rows = d_split.shape[2], d_split.shape[5]
    return pl.pallas_call(
        lin_kernel,
        grid=(2, 2),
        in_specs=[
            split_spec(groups, rows), token_spec(lin.shape[1]), token_spec(2), token_spec(2),
            whole_spec(gains.shape), token_spec(HEAD_DIM), token_spec(HEAD_DIM),
        ],
        out_specs=token_spec(lin.shape[1]),
        out_shape=jax.ShapeDtypeStruct(lin.shape, bfloat),
        name="rotated_back",
    )(d_split, lin, recips, means, gains, cosine, sine)


def unpack_kernel(in_ref, *out_refs):
    count, rows, width = in_ref.shape
    part = width // 3
    for which in range(3):
        for piece in range(count):
            out_refs[which][:, pl.ds(piece * part, part)] = in_ref[
                piece, :, pl.ds(which * part, part)
            ].astype(single)


def unpacked(values):
    count, rows, width = values.shape
    return pl.pallas_call(
        unpack_kernel,
        out_shape=[jax.ShapeDtypeStruct((rows, count * width // 3), single)] * 3,
        name="unpacked",
    )(values)


def dot_tn(a, b):
    return lax.dot_general(a, b, (((0,), (0,)), ((), ())), preferred_element_type=single)


def picks(slot_ref, source, expert, capacity):
    slots = slot_ref[source, expert : expert + 1, :]
    rows = lax.broadcasted_iota(jnp.int32, (capacity, slots.shape[1]), 0) + 1
    return slots == rows.astype(single)


def spread_tokens(slot_ref, first, second, out_ref, capacity):
    for source in range(slot_ref.shape[0]):
        at = slice(source * capacity, (source + 1) * capacity)
        total = dot_tn(picks(slot_ref, source, 0, capacity).astype(bfloat), first[at])
        total += dot_tn(picks(slot_ref, source, 1, capacity).astype(bfloat), second[at])
        out_ref[source] = total.astype(bfloat)


def expert_kernel(
    blk_ref, slot_ref, ffn_ref, cot_ref, router_ref, gate_ref, up_ref, down_ref, gate_tile_ref,
    up_tile_ref, x_ref, c_ref, value_ref, hidden_ref, d_gate_ref, d_up_ref, probs_ref, out_ref,
    grad_ref, d_both_ref, first_ref,
):
    expert, step = pl.program_id(0), pl.program_id(1)
    sources = ffn_ref.shape[0]
    capacity = x_ref.shape[1] // sources
    part = gate_ref.shape[3]
    tile = gate_tile_ref.shape[2]

    @pl.when((expert == 0) & (step == 0))
    def _():
        for source in range(sources):
            logits = dot_nt(router_ref[...], ffn_ref[source])
            shifted = jnp.exp(logits - jnp.max(logits, axis=0, keepdims=True))
            probs_ref[source] = shifted / jnp.sum(shifted, axis=0, keepdims=True)

    def fill(which):
        for source in range(sources):
            at = pl.ds(source * capacity, capacity)
            picked = picks(slot_ref, source, which, capacity)
            picked_low = picked.astype(bfloat)
            x_ref[0, at, :] = jnp.dot(
                picked_low, ffn_ref[source], preferred_element_type=single
            ).astype(bfloat)
            cot_rows = jnp.dot(picked_low, cot_ref[source], preferred_element_type=single)
            c_ref[0, at, :] = cot_rows.astype(bfloat)
            probs = probs_ref[source, pl.ds(2 * blk_ref[0] + which, 1), :]
            value = jnp.sum(jnp.where(picked, probs, 0.0), axis=1, keepdims=True)
            value_ref[0, at, :] = value
            grad_ref[at, :] = (value * cot_rows).astype(bfloat)

    for which in range(2):
        pl.when((expert == which) & (step == 0))(lambda which=which: fill(which))

    def hidden_part(index):
        w_both = jnp.concatenate([gate_ref[0, 0], up_ref[0, 0]], axis=1)
        both = jnp.dot(x_ref[0], w_both, preferred_element_type=single)
        gate_val, up_val = both[:, :part], both[:, part:]
        d_hidden = dot_nt(grad_ref[...], down_ref[0, 0])
        sigmoid = 1.0 / (1.0 + jnp.exp(-gate_val))
        silu = gate_val * sigmoid
        hidden_ref[0] = (silu * up_val).astype(bfloat)
        d_gate = (d_hidden * up_val * sigmoid * (1.0 + gate_val * (1.0 - sigmoid))).astype(bfloat)
        d_up = (d_hidden * silu).astype(bfloat)
        d_gate_ref[0] = d_gate
        d_up_ref[0] = d_up
        d_both_ref[:, pl.ds(2 * index * part, part)] = d_gate
        d_both_ref[:, pl.ds((2 * index + 1) * part, part)] = d_up

    for index in range(4):
        pl.when(step == index)(lambda index=index: hidden_part(index))

    def row_tile(index, which):
        weights = [ref[i, 0] for i in range(4) for ref in (gate_tile_ref, up_tile_ref)]
        d_rows = dot_nt(d_both_ref[...], jnp.concatenate(weights, axis=1)).astype(bfloat)
        at = pl.ds(index * tile, tile)
        if which == 0:
            first_ref[:, at] = d_rows
        else:
            spread_tokens(slot_ref, first_ref[:, at], d_rows, out_ref, capacity)

    for index in range(4):
        for which in range(2):
            pl.when((step == index + 4) & (expert == which))(
                lambda index=index, which=which: row_tile(index, which)
            )


def grads_kernel(
    slot_ref, x_ref, c_ref, value_ref, hidden_ref, d_gate_ref, d_up_ref, down_tile_ref,
    gate_sent_ref, up_sent_ref, down_sent_ref, gate_kept_ref, up_kept_ref, down_kept_ref,
    d_probs_ref, out_ref, grad_ref, xt_ref, dots_ref, first_ref,
):
    expert, step = pl.program_id(0), pl.program_id(1)
    sources = slot_ref.shape[0]
    capacity = x_ref.shape[1] // sources
    part = d_gate_ref.shape[2]
    tile = down_tile_ref.shape[3]

    @pl.when(step == 0)
    def _():
        grad_ref[...] = (value_ref[0] * c_ref[0].astype(single)).astype(bfloat)
        xt_ref[...] = jnp.transpose(x_ref[0])
        dots_ref[...] = jnp.zeros_like(dots_ref)

    def weight_part(index, gate_ref, up_ref, down_ref):
        d_both = jnp.concatenate([d_gate_ref[0], d_up_ref[0]], axis=1)
        both = jnp.dot(xt_ref[...], d_both, preferred_element_type=single)
        gate_ref[0, 0] = both[:, :part].astype(gate_ref.dtype)
        up_ref[0, 0] = both[:, part:].astype(up_ref.dtype)
        hidden = hidden_ref[0, :, pl.ds(index * part, part)]
        down_ref[0, 0] = dot_tn(hidden, grad_ref[...]).astype(down_ref.dtype)

    for index in range(4):
        refs = (
            (gate_sent_ref, up_sent_ref, down_sent_ref)
            if index < 2
            else (gate_kept_ref, up_kept_ref, down_kept_ref)
        )
        pl.when(step == index)(lambda index=index, refs=refs: weight_part(index, *refs))

    def out_tile(index, which):
        down = jnp.concatenate([down_tile_ref[i, 0] for i in range(4)], axis=0)
        expert_out = jnp.dot(hidden_ref[0], down, preferred_element_type=single)
        expert_out = expert_out.astype(bfloat).astype(single)
        at = pl.ds(index * tile, tile)
        dots_ref[...] += jnp.sum(
            c_ref[0, :, at].astype(single) * expert_out, axis=1, keepdims=True
        )
        weighted = (value_ref[0] * expert_out).astype(bfloat)
        if which == 0:
            first_ref[:, at] = weighted
        else:
            spread_tokens(slot_ref, first_ref[:, at], weighted, out_ref, capacity)
        if index == 3:
            for source in range(sources):
                picked = picks(slot_ref, source, which, capacity)
                row = dots_ref[source * capacity : (source + 1) * capacity]
                d_probs_ref[source, which : which + 1, :] = jnp.sum(
                    jnp.where(picked, row, 0.0), axis=0, keepdims=True
                )

    for index in range(4):
        for which in range(2):
            pl.when((step == index + 4) & (expert == which))(
                lambda index=index, which=which: out_tile(index, which)
            )


def rows_spec(rows, columns):
    return pl.BlockSpec((1, rows, columns), lambda e, k, *_: (e, 0, 0))


def first_half(k):
    return jnp.minimum(k, 3)


def second_half(k):
    return jnp.maximum(k - 4, 0)


def part_spec(rows, columns):
    return pl.BlockSpec((1, rows, columns), lambda e, k, *_: (e, 0, first_half(k)))


def weight_spec(shape, place=first_half):
    return pl.BlockSpec((1, 1) + shape[2:], lambda e, k, *_: (place(k), e, 0, 0))


def token_tile_spec(shape):
    block = shape[:2] + (shape[2] // 4,)
    return pl.BlockSpec(block, lambda e, k, *_: (0, 0, e * second_half(k)))


def expert_rows(blk, slot_map, ffn_all, cot_all, router_t, gate, up, down, capacity):
    sources, tokens, width = ffn_all.shape
    rows, experts, hidden = sources * capacity, router_t.shape[0], 4 * gate.shape[3]
    wide = jax.ShapeDtypeStruct((2, rows, width), bfloat)
    narrow = jax.ShapeDtypeStruct((2, rows, hidden), bfloat)
    probs = jax.ShapeDtypeStruct((sources, experts, tokens), single)
    tile_spec = pl.BlockSpec(
        (4, 1, width // 4, hidden // 4), lambda e, k, *_: (0, e, second_half(k), 0)
    )
    return pl.pallas_call(
        expert_kernel,
        grid_spec=pltpu.PrefetchScalarGridSpec(
            num_scalar_prefetch=1,
            grid=(2, 8),
            in_specs=[
                whole_spec(slot_map.shape), whole_spec(ffn_all.shape), whole_spec(cot_all.shape),
                whole_spec(router_t.shape), weight_spec(gate.shape), weight_spec(up.shape),
                weight_spec(down.shape), tile_spec, tile_spec,
            ],
            out_specs=[
                rows_spec(rows, width), rows_spec(rows, width), rows_spec(rows, 1),
                part_spec(rows, hidden // 4), part_spec(rows, hidden // 4),
                part_spec(rows, hidden // 4), whole_spec(probs.shape), token_tile_spec(ffn_all.shape),
            ],
            scratch_shapes=[
                pltpu.VMEM((rows, width), bfloat), pltpu.VMEM((rows, 2 * hidden), bfloat),
                pltpu.VMEM((rows, width), bfloat),
            ],
        ),
        out_shape=[
            wide, wide, jax.ShapeDtypeStruct((2, rows, 1), single), narrow, narrow, narrow,
            probs, jax.ShapeDtypeStruct(ffn_all.shape, bfloat),
        ],
        compiler_params=pltpu.CompilerParams(vmem_limit_bytes=60 << 20),
        name="expert_rows",
    )(blk[None], slot_map, ffn_all, cot_all, router_t, gate, up, down, gate, up)


def expert_grads(slot_map, x, c, value, hidden, d_gate, d_up, down, tokens):
    rows, width = x.shape[1:]
    part = down.shape[2]
    wide, tall = (2, 2, width, part), (2, 2, part, width)
    summed = (slot_map.shape[0], tokens, width)

    def sent(k):
        return jnp.minimum(k, 1)

    def kept(k):
        return jnp.clip(k - 2, 0, 1)

    shapes = (wide, wide, tall)
    return pl.pallas_call(
        grads_kernel,
        grid=(2, 8),
        in_specs=[
            whole_spec(slot_map.shape), rows_spec(rows, width), rows_spec(rows, width),
            rows_spec(rows, 1), rows_spec(rows, 4 * part), part_spec(rows, part),
            part_spec(rows, part),
            pl.BlockSpec((4, 1, part, width // 4), lambda e, k: (0, e, 0, second_half(k))),
        ],
        out_specs=[weight_spec(shape, sent) for shape in shapes]
        + [weight_spec(shape, kept) for shape in shapes]
        + [whole_spec(slot_map.shape), token_tile_spec(summed)],
        out_shape=[jax.ShapeDtypeStruct(shape, bfloat) for shape in shapes]
        + [jax.ShapeDtypeStruct(shape, single) for shape in shapes]
        + [
            jax.ShapeDtypeStruct(slot_map.shape, single),
            jax.ShapeDtypeStruct(summed, bfloat),
        ],
        scratch_shapes=[
            pltpu.VMEM((rows, width), bfloat), pltpu.VMEM((width, rows), bfloat),
            pltpu.VMEM((rows, 1), single), pltpu.VMEM((rows, width), bfloat),
        ],
        compiler_params=pltpu.CompilerParams(vmem_limit_bytes=60 << 20),
        name="expert_grads",
    )(slot_map, x, c, value, hidden, d_gate, d_up, down)


def plain_experts(blk, slot_map, ffn_all, cot_all, router_t, gate, up, down, capacity):
    sources, tokens, width = ffn_all.shape
    count = slot_map.shape[1]

    def joined(weights, axis):
        return jnp.concatenate([weights[i] for i in range(4)], axis=axis)

    gate, up, down = joined(gate, 2), joined(up, 2), joined(down, 1)
    slot_at = jnp.arange(1, capacity + 1, dtype=jnp.int32).astype(single)
    picked = jnp.transpose(slot_map, (1, 0, 2))[:, :, None, :] == slot_at[None, None, :, None]
    picked_low = picked.astype(bfloat)
    logits = jnp.einsum("ed,std->set", router_t, ffn_all, preferred_element_type=single)
    shifted = jnp.exp(logits - jnp.max(logits, axis=1, keepdims=True))
    probs = shifted / jnp.sum(shifted, axis=1, keepdims=True)
    local = jnp.transpose(lax.dynamic_slice_in_dim(probs, blk * count, count, 1), (1, 0, 2))
    value = jnp.sum(jnp.where(picked, local[:, :, None, :], 0.0), axis=3).reshape(count, -1, 1)

    def dispatch(rows):
        rows = jnp.einsum("esct,std->escd", picked_low, rows, preferred_element_type=single)
        return rows.astype(bfloat).reshape(count, -1, width)

    def combine(rows):
        rows = rows.astype(bfloat).reshape(count, sources, capacity, width)
        total = jnp.einsum("esct,escd->std", picked_low, rows, preferred_element_type=single)
        return total.astype(bfloat)

    def dots(spec, *arrays):
        return jnp.einsum(spec, *arrays, preferred_element_type=single)

    x, c = dispatch(ffn_all), dispatch(cot_all).astype(single)
    grad = (value * c).astype(bfloat)
    gate_val, up_val = dots("erd,edf->erf", x, gate), dots("erd,edf->erf", x, up)
    sigmoid = jax.nn.sigmoid(gate_val)
    hidden = (gate_val * sigmoid * up_val).astype(bfloat)
    d_hidden = dots("erd,efd->erf", grad, down)
    d_gate = (d_hidden * up_val * sigmoid * (1.0 + gate_val * (1.0 - sigmoid))).astype(bfloat)
    d_up = (d_hidden * gate_val * sigmoid).astype(bfloat)
    d_part = combine(dots("erf,edf->erd", d_gate, gate) + dots("erf,edf->erd", d_up, up))
    expert_out = dots("erf,efd->erd", hidden, down).astype(bfloat).astype(single)
    d_value = jnp.sum(c * expert_out, axis=2).reshape(count, sources, capacity, 1)
    d_probs = jnp.transpose(jnp.sum(jnp.where(picked, d_value, 0.0), axis=2), (1, 0, 2))
    mixed_part = combine(value * expert_out)

    def cut(total, axis):
        parts = jnp.stack(jnp.split(total, 4, axis=axis))
        return parts[:2].astype(bfloat), parts[2:]

    gate_sent, gate_kept = cut(dots("erd,erf->edf", x, d_gate), 2)
    up_sent, up_kept = cut(dots("erd,erf->edf", x, d_up), 2)
    down_sent, down_kept = cut(dots("erf,erd->efd", hidden, grad), 1)
    return probs, d_part, (
        gate_sent, up_sent, down_sent, gate_kept, up_kept, down_kept, d_probs, mixed_part
    )


def per_device(
    block_input, w_query, w_key, w_value, w_out, attn_gain, ffn_gain, query_gain, key_gain,
    router, w_gate, w_up, w_down, expert_ids, slot_ids, doc_starts, cotangent,
):
    ulysses_size = lax.axis_size("ulysses")
    blk_size = lax.axis_size(BLK)
    blk = lax.axis_index(BLK)
    uly = lax.axis_index("ulysses")
    core = uly % 2
    own_tokens, width = block_input.shape
    picks = expert_ids.shape[1]
    experts = router.shape[1]
    capacity = 5 * own_tokens * picks // (4 * experts)
    local_experts = experts // blk_size
    blk_tokens = ulysses_size * own_tokens
    far_size = blk_size // 2
    far_tokens = 2 * blk_tokens
    plane_size = 2 * ulysses_size
    local_width = width // ulysses_size
    plane_width = width // plane_size
    weight_rows = w_query.shape[0]
    groups = blk_size // 8
    plane = 2 * uly + blk % 2

    projections = jnp.concatenate(
        [
            weight.astype(bfloat).reshape(weight_rows, plane_size, plane_width)
            for weight in (w_query, w_key, w_value)
        ],
        axis=2,
    )
    projections = lax.all_to_all(
        jnp.transpose(projections, (1, 0, 2)), PLANE, split_axis=0, concat_axis=0, tiled=True
    )
    projections = projections.reshape(ulysses_size, 2 * weight_rows, 3 * plane_width)
    small = jnp.concatenate(
        [jnp.stack([attn_gain, ffn_gain, query_gain, key_gain]), router.T]
    ).astype(bfloat)
    w_qkv = gather_line(projections, 1).reshape(width, 3 * plane_width)
    small = gather_small(small)
    gate_mine, up_mine, down_mine = w_gate.astype(bfloat), w_up.astype(bfloat), w_down.astype(bfloat)
    plane_input = gather_plane(block_input).reshape(far_tokens, width)
    pair_beyond = swap(jnp.stack([gate_mine, up_mine]), 2)
    w_qkv, pair_beyond = tie(w_qkv, pair_beyond)
    attn_g = small[0].astype(single)
    ffn_g = small[1].astype(single)
    plane_gains = lax.dynamic_slice_in_dim(
        small[2:4], plane * plane_width, plane_width, 1
    ).astype(single)
    router_t = small[4:]

    def gather_expert(mine, beyond):
        return jnp.stack([swap(mine, 1), swap(beyond, 1), mine, beyond])

    named = expert_ids[:, :, None] == jnp.arange(experts, dtype=jnp.int32)[None, None, :]
    slot_map = jnp.sum(jnp.where(named, slot_ids[:, :, None] + 1, 0), axis=1)
    slot_map = slot_map.T.astype(single).reshape(blk_size, local_experts, own_tokens)
    slot_map = lax.all_to_all(slot_map, BLK, split_axis=0, concat_axis=0, tiled=True)

    inputs = block_input.astype(single)
    hat_one, recip_one = norm_parts(inputs)
    normed = (norm_parts(plane_input.astype(single))[0] * attn_g).astype(bfloat)
    lin, squares = projected(normed, w_qkv)
    w_o = lax.all_gather(w_out.astype(bfloat), BLK, axis=0, tiled=True)
    cot_all = lax.all_gather(cotangent, BLK, axis=0)
    squares, down_mine = tie(sum_plane(squares), down_mine)
    down_beyond = swap(down_mine, 2)
    recips = columns(lax.rsqrt(squares / width + NORM_EPSILON))
    far_at = blk // 2 * far_tokens + jnp.arange(far_tokens, dtype=jnp.int32)
    cosine, sine = angles(far_at - doc_begins(doc_starts, far_at), HEAD_DIM)
    split = rotated_heads(lin, recips, plane_gains, cosine, sine, groups)
    heads_in = line_to_heads(split, far_size)
    gate_beyond, up_beyond = pair_beyond[0], pair_beyond[1]
    part_rows = heads_in.shape[2]
    if groups == 1:
        query, mine = heads_in, heads_in
    else:
        query = heads_in[:, 0].reshape(-1, 1, QUERY_ROWS, HEAD_DIM)
        mine = lax.all_gather(
            heads_in[:, 1:], "far", axis=2, axis_index_groups=head_groups(far_size, groups)
        ).reshape(blk_size, 2, HALF_ROWS, HEAD_DIM)
    other = swap(mine[:, -2:], 1)
    query_at = (
        jnp.arange(blk_size, dtype=jnp.int32)[:, None] * blk_tokens
        + core * HALF_ROWS
        + blk // 2 % groups * part_rows
        + jnp.arange(part_rows, dtype=jnp.int32)[None, :]
    ).reshape(-1, QUERY_ROWS)
    query_begin = doc_begins(doc_starts, query_at)
    scalars = (core[None],) + block_bounds(query_at, query_begin)
    query_at, query_begin = query_at[:, None], query_begin[:, None]
    head_out, lse = attention_forward(scalars, query_at, query_begin, query, mine, other)
    attended = blk_from_heads(
        head_out.astype(bfloat).reshape(blk_size, part_rows, HEAD_DIM), blk_size
    )
    attended, down_beyond = tie(attended, down_beyond)
    expert_gate = gather_expert(gate_mine, gate_beyond)
    expert_up = gather_expert(up_mine, up_beyond)
    expert_down = gather_expert(down_mine, down_beyond)
    out_part = jnp.dot(attended, w_o, preferred_element_type=single)

    def token_rows(values):
        return lambda bits: lax.dynamic_slice_in_dim(
            values, (uly ^ bits) * own_tokens, own_tokens, 0
        )

    residual_mid = inputs + scatter_sum_ulysses(token_rows(out_part))
    hat_two, recip_two = norm_parts(residual_mid)
    ffn_in = (hat_two * ffn_g).astype(bfloat)

    ffn_all = lax.all_gather(ffn_in, BLK, axis=0)
    if capacity % 16 == 0:
        *kept_rows, probs_all, d_part = expert_rows(
            blk, slot_map, ffn_all, cot_all, router_t, expert_gate, expert_up, expert_down, capacity
        )
        *kept_rows, d_part = tie(*kept_rows, d_part)
        results = expert_grads(slot_map, *kept_rows, expert_down, own_tokens)
    else:
        probs_all, d_part, results = plain_experts(
            blk, slot_map, ffn_all, cot_all, router_t, expert_gate, expert_up, expert_down, capacity
        )
    d_ffn_in = lax.psum_scatter(d_part, BLK, scatter_dimension=0).astype(single)
    gate_sent, up_sent, down_sent, gate_kept, up_kept, down_kept, d_probs, mixed_part = results

    def add_core(sent, kept):
        got = swap(sent, 1).astype(single)
        return kept[0] + got[0], (kept[1] + got[1]).astype(bfloat)

    down_kept, down_sent = add_core(down_sent, down_kept)
    down_across = swap(down_sent, 2)
    d_probs = lax.all_to_all(d_probs, BLK, split_axis=0, concat_axis=0, tiled=True)
    d_probs = d_probs.reshape(experts, own_tokens)
    d_probs, gate_kept, up_kept = tie(d_probs, gate_kept, up_kept)
    gate_kept, gate_sent = add_core(gate_sent, gate_kept)
    up_kept, up_sent = add_core(up_sent, up_kept)
    d_ffn_in, mixed_part, gate_sent, up_sent, down_across = tie(
        d_ffn_in, mixed_part, gate_sent, up_sent, down_across
    )
    grad_w_down = down_kept + down_across.astype(single)
    mixed_sum = lax.psum_scatter(mixed_part, BLK, scatter_dimension=0)

    router_probs = lax.dynamic_index_in_dim(probs_all, blk, 0, keepdims=False)
    d_logits = (
        router_probs * (d_probs - jnp.sum(router_probs * d_probs, axis=0, keepdims=True))
    ).astype(bfloat)
    grad_router_part = jnp.dot(d_logits, ffn_in, preferred_element_type=single)
    d_ffn_in = d_ffn_in + dot_tn(d_logits, router_t)
    grad_ffn_part = jnp.sum(d_ffn_in * hat_two, axis=0)
    d_mid = cotangent.astype(single) + norm_back(d_ffn_in * ffn_g, hat_two, recip_two)

    d_attn_out = gather_ulysses(d_mid.astype(bfloat)).reshape(blk_tokens, width)
    d_attn_out, gate_sent = tie(d_attn_out, gate_sent)
    gate_across = swap(gate_sent, 2)
    d_attended = dot_nt(d_attn_out, w_o).astype(bfloat)
    grad_out_part = jnp.einsum("ti,to->io", attended, d_attn_out, preferred_element_type=single)
    grad_out_part = grad_out_part.astype(bfloat).reshape(blk_size, weight_rows, width)
    d_out = blk_to_heads(d_attended, blk_size).reshape(head_out.shape)
    d_out, grad_out_part, grad_w_down = tie(d_out, grad_out_part, grad_w_down)
    grad_w_out = lax.psum_scatter(grad_out_part, BLK, scatter_dimension=0)
    dq_head, keep, send = attention_backward(
        scalars, query_at, query_begin, lse, head_out, query, d_out, mine, other
    )
    dq_head, gate_across, up_sent = tie(dq_head, gate_across, up_sent)
    up_across = swap(up_sent, 2)
    grad_w_gate = gate_kept + gate_across.astype(single)
    d_keys = (keep + swap(send, 1).astype(single)).astype(bfloat)
    if groups > 1:
        moved = jnp.moveaxis(d_keys.reshape(blk_size, 2, groups, part_rows, HEAD_DIM), 2, 0)
        moved = lax.psum_scatter(
            moved, "far", scatter_dimension=0, axis_index_groups=head_groups(far_size, groups)
        )
        d_keys = moved
    d_stack = jnp.concatenate(
        [dq_head.reshape(blk_size, 1, part_rows, HEAD_DIM), d_keys], axis=1
    )
    d_split = line_from_heads(d_stack, far_size)
    narrow = scatter_sum_ulysses(
        lambda bits: lax.dynamic_slice_in_dim(
            jnp.concatenate([grad_ffn_part[None], grad_router_part]),
            (uly ^ bits) * local_width, local_width, 1,
        ),
        single,
    )
    d_split, narrow, up_across, mixed_sum, grad_w_gate = tie(
        d_split, narrow, up_across, mixed_sum, grad_w_gate
    )
    mixed = (residual_mid + mixed_sum.astype(single)).astype(bfloat)
    grad_w_up = up_kept + up_across.astype(single)
    gain_parts, means = rotated_sums(d_split, lin, recips, plane_gains, cosine, sine)
    means = columns(sum_plane(means) / width)
    means, grad_w_out = tie(means, grad_w_out)
    grad_w_out = grad_w_out.astype(single)
    d_lin = rotated_back(d_split, lin, recips, means, plane_gains, cosine, sine)
    grads = jnp.einsum("td,to->do", normed, d_lin, preferred_element_type=single)
    grads = grads.astype(bfloat).reshape(ulysses_size, far_size, 2 * weight_rows, 3 * plane_width)
    grads = jnp.transpose(grads, (1, 0, 2, 3)).reshape(-1, 3 * plane_width)
    grads = lax.psum_scatter(grads, "far", scatter_dimension=0, tiled=True)
    d_normed_part = dot_nt(d_lin, w_qkv)
    grad_attn_part = jnp.sum(d_normed_part * norm_parts(plane_input.astype(single))[0], axis=0)
    d_normed_part = d_normed_part.reshape(2, blk_tokens, width)
    side = blk % 2

    def near_rows(bits):
        mine, other = (
            lax.dynamic_slice(
                d_normed_part, (place, (uly ^ bits) * own_tokens, 0), (1, own_tokens, width)
            )[0]
            for place in (side, 1 - side)
        )
        return mine, other

    d_normed, grad_w_up = scatter_sum_plane(near_rows, grad_w_up)
    input_grad = d_mid + norm_back(d_normed * attn_g, hat_one, recip_one)

    def own_columns(values):
        return scatter_sum_ulysses(
            lambda bits: lax.dynamic_slice_in_dim(values, (uly ^ bits) * local_width, local_width, 1),
            single,
        )

    gain_parts = lax.dynamic_update_slice_in_dim(
        jnp.zeros((2, local_width), single), gain_parts, side * plane_width, 1
    )
    last = own_columns(grad_attn_part[None])
    gains = scatter_sum_blk_small(jnp.concatenate([last, narrow, gain_parts]))
    grads = grads.reshape(plane_size, weight_rows, 3 * plane_width)
    grads = lax.all_to_all(grads, PLANE, split_axis=0, concat_axis=0, tiled=True)
    grads = unpacked(grads)
    return (
        mixed,
        input_grad.astype(bfloat),
        grads[0],
        grads[1],
        grads[2],
        grad_w_out,
        gains[0],
        gains[1],
        gains[-2],
        gains[-1],
        gains[2:-2].T,
        grad_w_gate,
        grad_w_up,
        grad_w_down,
    )


def solution(mesh):
    in_specs = (
        P(("far", "near", "ulysses"), None),
        P(("ulysses", "far", "near"), None),
        P(("ulysses", "far", "near"), None),
        P(("ulysses", "far", "near"), None),
        P(("ulysses", "far", "near"), None),
        P(("ulysses", "far", "near")),
        P(("ulysses", "far", "near")),
        P(("ulysses", "far", "near")),
        P(("ulysses", "far", "near")),
        P(("ulysses", "far", "near"), None),
        P(BLK, None, "ulysses"),
        P(BLK, None, "ulysses"),
        P(BLK, "ulysses", None),
        P(("far", "near", "ulysses"), None),
        P(("far", "near", "ulysses"), None),
        P(),
        P(("far", "near", "ulysses"), None),
    )
    out_specs = (
        P(("far", "near", "ulysses"), None),
        P(("far", "near", "ulysses"), None),
        P(("ulysses", "far", "near"), None),
        P(("ulysses", "far", "near"), None),
        P(("ulysses", "far", "near"), None),
        P(("ulysses", "far", "near"), None),
        P(("ulysses", "far", "near")),
        P(("ulysses", "far", "near")),
        P(("ulysses", "far", "near")),
        P(("ulysses", "far", "near")),
        P(("ulysses", "far", "near"), None),
        P(BLK, None, "ulysses"),
        P(BLK, None, "ulysses"),
        P(BLK, "ulysses", None),
    )
    ulysses_size, blk_size = mesh.devices.shape
    shape = (ulysses_size, blk_size // 2, 2)
    split_mesh = jax.sharding.Mesh(mesh.devices.reshape(shape), ("ulysses", "far", "near"))
    return jax.shard_map(
        per_device, mesh=split_mesh, in_specs=in_specs, out_specs=out_specs, check_vma=False
    )
```

```python
import math

import jax
import jax.numpy as jnp
from jax import lax
from jax.experimental import pallas as pl
from jax.experimental.pallas import tpu as pltpu
from jax.sharding import PartitionSpec as P

HEAD_DIM = 128
NORM_EPSILON = 1e-05
ROPE_BASE = 10000.0
MASKED_SCORE = -1e30
SCORE_SCALE = HEAD_DIM ** (-0.5)
LOG2_SCALE = SCORE_SCALE * math.log2(math.e)
QUERY_ROWS = 256
HALF_ROWS = 256
KEY_ROWS = 512
BLK = ("far", "near")
PLANE = ("ulysses", "near")
bfloat = jnp.bfloat16
single = jnp.float32


def norm_parts(values):
    recip_factor = lax.rsqrt(jnp.mean(values * values, axis=-1, keepdims=True) + NORM_EPSILON)
    return (values * recip_factor, recip_factor)


def norm_back(grad_in, hat_values, recip_factor):
    return recip_factor * (
        grad_in - hat_values * jnp.mean(grad_in * hat_values, axis=-1, keepdims=True)
    )


def doc_begins(doc_starts, tokens_at):
    at_or_before = doc_starts[:, None] <= tokens_at.reshape(1, -1)
    begins = jnp.max(jnp.where(at_or_before, doc_starts[:, None], 0), axis=0)
    return begins.reshape(tokens_at.shape)


def angles(position, head_size):
    half_size = head_size // 2
    frequency = ROPE_BASE ** (-(jnp.arange(half_size, dtype=jnp.float32) * 2.0 / head_size))
    turn = position.astype(jnp.float32)[:, None] * frequency[None, :]
    cosine, sine = jnp.cos(turn), jnp.sin(turn)
    return jnp.concatenate([cosine, cosine], 1), jnp.concatenate([-sine, sine], 1)


def swap(values, bit, axis="ulysses"):
    size = lax.axis_size(axis)
    return lax.ppermute(values, axis, [(i, i ^ bit) for i in range(size)])


def gather_plane(values):
    me, side = lax.axis_index("ulysses"), lax.axis_index("near")
    near = swap(values, 1, "near")
    beyond = swap(values, 2)
    corner = swap(beyond, 1, "near")
    out = jnp.zeros((2, 4) + values.shape, values.dtype)
    for other, bit, part in ((0, 0, values), (0, 2, beyond), (1, 0, near), (1, 2, corner)):
        for core, piece in ((0, part), (1, swap(part, 1))):
            place = (side ^ other, me ^ bit ^ core) + (0,) * values.ndim
            out = lax.dynamic_update_slice(out, piece[None, None], place)
    return out


def line_steps(size):
    for step in range(1, size):
        up = [(i, i + 1) for i in range(step - 1, size - 1)]
        yield up, [(size - 1 - i, size - 1 - j) for i, j in up]


def gather_line(values, axis):
    size = lax.axis_size("far")
    if size > 4:
        return lax.all_gather(values, "far", axis=axis)
    at = lax.axis_index("far")
    below, above, parts = values, values, []
    for step, (up, down) in enumerate(line_steps(size), 1):
        below, above = lax.ppermute(below, "far", up), lax.ppermute(above, "far", down)
        parts = [(at - step, below), (at + step, above)] + parts
    shape = values.shape[:axis] + (size,) + values.shape[axis:]
    out = jnp.zeros(shape, values.dtype)
    for place, part in parts + [(at, values)]:
        out = lax.dynamic_update_index_in_dim(out, part, jnp.clip(place, 0, size - 1), axis)
    return out


def gather_ulysses(values):
    me = lax.axis_index("ulysses")
    beyond = swap(values, 2)
    core = swap(values, 1)
    beyond_core = swap(beyond, 1)
    out = jnp.zeros((4,) + values.shape, values.dtype)
    for bit, part in enumerate((values, core, beyond, beyond_core)):
        out = lax.dynamic_update_index_in_dim(out, part, me ^ bit, 0)
    return out


def scatter_sum_ulysses(parts, kind=bfloat):
    far = swap(parts(3).astype(kind), 1)
    near = swap(parts(1).astype(kind), 1)
    across = swap((parts(2) + far.astype(single)).astype(kind), 2)
    return parts(0) + near.astype(single) + across.astype(single)


def scatter_sum_plane(parts, beside):
    kept, sent = [], []
    for bits in (0, 2):
        mine, other = parts(bits)
        core_mine, core_other = parts(bits ^ 1)
        got = swap(jnp.stack([core_mine, core_other]).astype(bfloat), 1).astype(single)
        kept.append(mine + got[0])
        sent.append(other + got[1])
    got = swap(jnp.stack(sent).astype(bfloat), 1, "near")
    got, beside = tie(got, beside)
    got = got.astype(single)
    across = swap((kept[1] + got[1]).astype(bfloat), 2)
    return kept[0] + got[0] + across.astype(single), beside


def gather_blk_small(values):
    ulysses_size, count, size = values.shape
    blk_size = lax.axis_size(BLK)
    mine = jnp.transpose(values, (1, 0, 2)).reshape(count, -1)
    out = lax.all_to_all(
        jnp.broadcast_to(mine, (blk_size,) + mine.shape), BLK, split_axis=0, concat_axis=0, tiled=True
    )
    out = out.reshape(blk_size, count, ulysses_size, size)
    return jnp.transpose(out, (1, 2, 0, 3)).reshape(count, -1)


def scatter_sum_blk_small(values):
    count, blk_size = values.shape[0], lax.axis_size(BLK)
    parts = jnp.transpose(values.reshape(count, blk_size, -1), (1, 0, 2))
    parts = lax.all_to_all(parts, BLK, split_axis=0, concat_axis=0, tiled=True)
    return jnp.sum(parts, axis=0)


def tie(*values):
    return lax.optimization_barrier(values)


def sum_plane(values):
    values = values + swap(values, 1)
    values = values + swap(values, 2)
    return values + swap(values, 1, "near")


def swap_halves(values, core):
    got = swap(lax.dynamic_index_in_dim(values, 1 - core, 0, keepdims=False), 1)
    return lax.dynamic_update_index_in_dim(values, got, 1 - core, 0)


def line_to_heads(split, far_size):
    count, rows = split.shape[4:6]
    both = swap_halves(split, lax.axis_index("ulysses") % 2)
    both = both.reshape(far_size, 2, count, rows, HEAD_DIM)
    both = lax.all_to_all(both, "far", split_axis=0, concat_axis=0, tiled=True)
    return both.reshape(2 * far_size, count, rows, HEAD_DIM)


def line_from_heads(stacked, far_size):
    count, rows = stacked.shape[1:3]
    back = stacked.reshape(far_size, 2, count, rows, HEAD_DIM)
    back = lax.all_to_all(back, "far", split_axis=0, concat_axis=0, tiled=True)
    back = back.reshape(2, 2, far_size // 4, 2, count, rows, HEAD_DIM)
    return swap_halves(back, lax.axis_index("ulysses") % 2)


def blk_halves(values, blk_size):
    core = lax.axis_index("ulysses") % 2
    groups = blk_size // 8
    rows = values.shape[0] // (2 * groups)
    split = values.reshape(2, groups, rows, 2, 2, HEAD_DIM)
    split = jnp.transpose(split, (0, 4, 1, 3, 2, 5))
    return swap_halves(split, core).reshape(blk_size, rows, HEAD_DIM)


def blk_from_heads(stacked, blk_size):
    core = lax.axis_index("ulysses") % 2
    groups, rows = blk_size // 8, stacked.shape[1]
    back = lax.all_to_all(stacked, BLK, split_axis=0, concat_axis=0, tiled=True)
    whole = swap_halves(back.reshape(2, 2, groups, 2, rows, HEAD_DIM), core)
    whole = jnp.transpose(whole, (0, 2, 4, 3, 1, 5))
    return whole.reshape(2 * groups * rows, 4 * HEAD_DIM)


def head_groups(far_size, groups):
    return [[j * groups + p for p in range(groups)] for j in range(far_size // groups)]


def kernel_cost(micros):
    return pl.CostEstimate(flops=micros * 10**9, bytes_accessed=0, transcendentals=0)


def dot_nt(a, b):
    return lax.dot_general(a, b, (((1,), (1,)), ((), ())), preferred_element_type=single)


def key_loops(low_ref, open_ref, close_ref, high_ref, index, step, carry):
    low, opened = low_ref[index], open_ref[index]
    closed, high = close_ref[index], high_ref[index]
    carry = lax.fori_loop(low, opened, lambda kb, c: step(kb, c, True), carry)
    carry = lax.fori_loop(opened, closed, lambda kb, c: step(kb, c, False), carry)
    return lax.fori_loop(closed, high, lambda kb, c: step(kb, c, True), carry)


def allowed(start, pos, begin):
    key_at = start + lax.broadcasted_iota(jnp.int32, (KEY_ROWS, pos.shape[1]), 0)
    return (key_at <= pos) & (key_at >= begin)


def load_keys(core, mine_ref, other_ref, at, store):
    for blk in range(mine_ref.shape[0]):
        start = 2 * blk * HALF_ROWS
        store(pl.multiple_of(start + core * HALF_ROWS, HALF_ROWS), mine_ref[blk, at])
        store(pl.multiple_of(start + (1 - core) * HALF_ROWS, HALF_ROWS), other_ref[blk, at - mine_ref.shape[1] + 2])


def forward_kernel(
    core_ref, low_ref, open_ref, close_ref, high_ref,
    pos_ref, begin_ref, q_ref, mine_ref, other_ref, o_ref, lse_ref, k_ref, vt_ref,
):
    index = pl.program_id(0)

    @pl.when(index == 0)
    def _():
        core, last = core_ref[0], mine_ref.shape[1]

        def store_key(start, rows):
            k_ref[pl.ds(start, HALF_ROWS), :] = rows

        def store_value(start, rows):
            vt_ref[:, pl.ds(start, HALF_ROWS)] = jnp.transpose(rows)

        load_keys(core, mine_ref, other_ref, last - 2, store_key)
        load_keys(core, mine_ref, other_ref, last - 1, store_value)

    query = q_ref[0, 0]
    pos, begin = pos_ref[0], begin_ref[0]
    rows = query.shape[0]

    def step(block, carry, masked):
        top, total, acc = carry
        start = pl.multiple_of(block * KEY_ROWS, KEY_ROWS)
        scores = dot_nt(k_ref[pl.ds(start, KEY_ROWS), :], query) * LOG2_SCALE
        if masked:
            scores = jnp.where(allowed(start, pos, begin), scores, MASKED_SCORE)
        new_top = jnp.maximum(top, jnp.max(scores, axis=0, keepdims=True))
        probs = jnp.exp2(scores - new_top)
        shrink = jnp.exp2(top - new_top)
        total = total * shrink + jnp.sum(probs, axis=0, keepdims=True)
        acc = acc * shrink + jnp.dot(
            vt_ref[:, pl.ds(start, KEY_ROWS)], probs.astype(bfloat), preferred_element_type=single
        )
        return new_top, total, acc

    carry = (
        jnp.full((1, rows), MASKED_SCORE, single),
        jnp.zeros((1, rows), single),
        jnp.zeros((HEAD_DIM, rows), single),
    )
    top, total, acc = key_loops(low_ref, open_ref, close_ref, high_ref, index, step, carry)
    o_ref[0] = jnp.transpose(acc / total)
    lse_ref[0] = top + jnp.log2(total)


def backward_kernel(
    core_ref, low_ref, open_ref, close_ref, high_ref, pos_ref, begin_ref, lse_ref, o_ref,
    q_ref, do_ref, mine_ref, other_ref, dq_ref, keep_ref, send_ref, k_ref, v_ref, kt_ref, dk_ref, dv_ref,
):
    index = pl.program_id(0)
    core = core_ref[0]

    @pl.when(index == 0)
    def _():
        dk_ref[...] = jnp.zeros_like(dk_ref)
        dv_ref[...] = jnp.zeros_like(dv_ref)
        last = mine_ref.shape[1]

        def store_key(start, rows):
            k_ref[pl.ds(start, HALF_ROWS), :] = rows
            kt_ref[:, pl.ds(start, HALF_ROWS)] = jnp.transpose(rows)

        def store_value(start, rows):
            v_ref[pl.ds(start, HALF_ROWS), :] = rows

        load_keys(core, mine_ref, other_ref, last - 2, store_key)
        load_keys(core, mine_ref, other_ref, last - 1, store_value)

    query, d_out = q_ref[0, 0], do_ref[0]
    pos, begin = pos_ref[0], begin_ref[0]
    lse = lse_ref[0]
    products = d_out.astype(single) * o_ref[0]
    delta = jnp.sum(jnp.transpose(products), axis=0, keepdims=True)

    def step(block, acc, masked):
        start = pl.multiple_of(block * KEY_ROWS, KEY_ROWS)
        rows = pl.ds(start, KEY_ROWS)
        scores = dot_nt(k_ref[rows, :], query) * LOG2_SCALE
        probs = jnp.exp2(scores - lse)
        if masked:
            probs = jnp.where(allowed(start, pos, begin), probs, 0.0)
        d_probs = dot_nt(v_ref[rows, :], d_out)
        d_scores = (probs * (d_probs - delta)).astype(bfloat)
        dv_ref[rows, :] += jnp.dot(probs.astype(bfloat), d_out, preferred_element_type=single)
        dk_ref[rows, :] += jnp.dot(d_scores, query, preferred_element_type=single)
        return acc + jnp.dot(kt_ref[:, rows], d_scores, preferred_element_type=single)

    acc = jnp.zeros((HEAD_DIM, query.shape[0]), single)
    acc = key_loops(low_ref, open_ref, close_ref, high_ref, index, step, acc)
    dq_ref[0] = (jnp.transpose(acc) * SCORE_SCALE).astype(bfloat)

    @pl.when(index == pl.num_programs(0) - 1)
    def _():
        for blk in range(keep_ref.shape[0]):
            start = 2 * blk * HALF_ROWS
            mine = pl.ds(pl.multiple_of(start + core * HALF_ROWS, HALF_ROWS), HALF_ROWS)
            other = pl.ds(pl.multiple_of(start + (1 - core) * HALF_ROWS, HALF_ROWS), HALF_ROWS)
            keep_ref[blk, 0] = dk_ref[mine, :] * SCORE_SCALE
            keep_ref[blk, 1] = dv_ref[mine, :]
            send_ref[blk, 0] = (dk_ref[other, :] * SCORE_SCALE).astype(bfloat)
            send_ref[blk, 1] = dv_ref[other, :].astype(bfloat)


def block_bounds(pos, begin):
    first, last = jnp.min(begin, axis=1), jnp.max(begin, axis=1)
    low = first // KEY_ROWS
    high = jnp.max(pos, axis=1) // KEY_ROWS + 1
    opened = jnp.clip((last + KEY_ROWS - 1) // KEY_ROWS, low, high)
    closed = jnp.clip((jnp.min(pos, axis=1) + 1) // KEY_ROWS, opened, high)
    return low, opened, closed, high


def block_spec(shape):
    return pl.BlockSpec((1,) + shape[1:], lambda i, *_: (i,) + (0,) * (len(shape) - 1))


def first_spec(shape):
    return pl.BlockSpec((1, 1) + shape[2:], lambda i, *_: (i,) + (0,) * (len(shape) - 1))


def whole_spec(shape):
    return pl.BlockSpec(shape, lambda *_: (0,) * len(shape), pipeline_mode=pl.Buffered(1))


def attention_forward(scalars, pos, begin, query, mine, other):
    blocks, _, rows = pos.shape
    keys = 2 * mine.shape[0] * HALF_ROWS
    out_shape = [
        jax.ShapeDtypeStruct((blocks, rows, HEAD_DIM), single),
        jax.ShapeDtypeStruct(pos.shape, single),
    ]
    return pl.pallas_call(
        forward_kernel,
        grid_spec=pltpu.PrefetchScalarGridSpec(
            num_scalar_prefetch=5,
            grid=(blocks,),
            in_specs=[
                block_spec(pos.shape), block_spec(pos.shape), first_spec(query.shape),
                whole_spec(mine.shape), whole_spec(other.shape),
            ],
            out_specs=[block_spec(out.shape) for out in out_shape],
            scratch_shapes=[pltpu.VMEM((keys, HEAD_DIM), bfloat), pltpu.VMEM((HEAD_DIM, keys), bfloat)],
        ),
        out_shape=out_shape,
        compiler_params=pltpu.CompilerParams(vmem_limit_bytes=48 << 20),
        cost_estimate=kernel_cost(22),
        name="attention_forward",
    )(*scalars, pos, begin, query, mine, other)


def attention_backward(scalars, pos, begin, lse, head_out, query, d_out, mine, other):
    blocks, _, rows = pos.shape
    keys = 2 * mine.shape[0] * HALF_ROWS
    pair = (mine.shape[0], 2, HALF_ROWS, HEAD_DIM)
    out_shape = [
        jax.ShapeDtypeStruct(d_out.shape, bfloat),
        jax.ShapeDtypeStruct(pair, single),
        jax.ShapeDtypeStruct(pair, bfloat),
    ]
    return pl.pallas_call(
        backward_kernel,
        grid_spec=pltpu.PrefetchScalarGridSpec(
            num_scalar_prefetch=5,
            grid=(blocks,),
            in_specs=[
                block_spec(pos.shape), block_spec(pos.shape), block_spec(pos.shape),
                block_spec(head_out.shape), first_spec(query.shape), block_spec(d_out.shape),
                whole_spec(mine.shape), whole_spec(other.shape),
            ],
            out_specs=[block_spec(d_out.shape), whole_spec(pair), whole_spec(pair)],
            scratch_shapes=[
                pltpu.VMEM((keys, HEAD_DIM), bfloat), pltpu.VMEM((keys, HEAD_DIM), bfloat),
                pltpu.VMEM((HEAD_DIM, keys), bfloat),
                pltpu.VMEM((keys, HEAD_DIM), single), pltpu.VMEM((keys, HEAD_DIM), single),
            ],
        ),
        out_shape=out_shape,
        compiler_params=pltpu.CompilerParams(vmem_limit_bytes=60 << 20),
        cost_estimate=kernel_cost(26),
        name="attention_backward",
    )(*scalars, pos, begin, lse, head_out, query, d_out, mine, other)


def turned(values, cosine, sine):
    return values * cosine + pltpu.roll(values, HEAD_DIM // 2, 1) * sine


def rotate_kernel(lin_ref, recip_ref, gain_ref, cosine_ref, sine_ref, out_ref):
    groups, rows = out_ref.shape[2], out_ref.shape[5]
    cosine, sine = cosine_ref[...], sine_ref[...]
    for which in range(3):
        for head in range(2):
            at = head * HEAD_DIM
            values = lin_ref[:, pl.ds((2 * which + head) * HEAD_DIM, HEAD_DIM)]
            if which < 2:
                values = values * recip_ref[:, which : which + 1]
                values = values * gain_ref[which : which + 1, at : at + HEAD_DIM]
                values = turned(values, cosine, sine)
            values = values.astype(bfloat)
            for group in range(groups):
                out_ref[0, head, group, 0, which] = values[group * rows : (group + 1) * rows]


def back_parts(d_ref, lin_ref, recip_ref, gain_ref, cosine, sine, which, head):
    at = head * HEAD_DIM
    grad = d_ref[0, head, :, 0, which].reshape(-1, HEAD_DIM).astype(single)
    grad = turned(grad, cosine, -sine)
    hat = lin_ref[:, pl.ds((2 * which + head) * HEAD_DIM, HEAD_DIM)] * recip_ref[:, which : which + 1]
    return grad, grad * gain_ref[which : which + 1, at : at + HEAD_DIM], hat


def sums_kernel(d_ref, lin_ref, recip_ref, gain_ref, cosine_ref, sine_ref, gain_out_ref, sum_ref):
    first = (pl.program_id(0) == 0) & (pl.program_id(1) == 0)

    @pl.when(first)
    def _():
        gain_out_ref[...] = jnp.zeros_like(gain_out_ref)

    cosine, sine = cosine_ref[...], sine_ref[...]
    for which in range(2):
        total = None
        for head in range(2):
            grad, scaled, hat = back_parts(
                d_ref, lin_ref, recip_ref, gain_ref, cosine, sine, which, head
            )
            at = pl.ds(head * HEAD_DIM, HEAD_DIM)
            gain_out_ref[which : which + 1, at] += jnp.sum(grad * hat, axis=0, keepdims=True)
            product = jnp.transpose(scaled * hat)
            product = jnp.sum(product, axis=0, keepdims=True)
            total = product if total is None else total + product
        sum_ref[0, 0, which : which + 1, :] = total


def lin_kernel(d_ref, lin_ref, recip_ref, mean_ref, gain_ref, cosine_ref, sine_ref, out_ref):
    cosine, sine = cosine_ref[...], sine_ref[...]
    for head in range(2):
        for which in range(2):
            _, scaled, hat = back_parts(
                d_ref, lin_ref, recip_ref, gain_ref, cosine, sine, which, head
            )
            grad = recip_ref[:, which : which + 1] * (scaled - hat * mean_ref[:, which : which + 1])
            out_ref[:, pl.ds((2 * which + head) * HEAD_DIM, HEAD_DIM)] = grad.astype(bfloat)
        out_ref[:, pl.ds((4 + head) * HEAD_DIM, HEAD_DIM)] = d_ref[0, head, :, 0, 2].reshape(
            -1, HEAD_DIM
        )


def token_spec(columns):
    return pl.BlockSpec((HALF_ROWS, columns), lambda near, half: (2 * near + half, 0))


def split_spec(groups, rows):
    return pl.BlockSpec(
        (1, 2, groups, 1, 3, rows, HEAD_DIM), lambda near, half: (half, 0, 0, near, 0, 0, 0)
    )


def project_kernel(rows_ref, weight_ref, lin_ref, sum_ref):
    part = weight_ref.shape[1] // 3
    lin = jnp.dot(rows_ref[...], weight_ref[...], preferred_element_type=single)
    lin_ref[...] = lin
    for which in range(2):
        values = lin[:, which * part : (which + 1) * part]
        sum_ref[0, 0, which : which + 1, :] = jnp.sum(
            jnp.transpose(values * values), axis=0, keepdims=True
        )


def projected(rows, weight):
    return pl.pallas_call(
        project_kernel,
        grid=(2, 2),
        in_specs=[token_spec(rows.shape[1]), whole_spec(weight.shape)],
        out_specs=[
            token_spec(weight.shape[1]),
            pl.BlockSpec((1, 1, 2, HALF_ROWS), lambda near, half: (near, half, 0, 0)),
        ],
        out_shape=[
            jax.ShapeDtypeStruct((rows.shape[0], weight.shape[1]), single),
            jax.ShapeDtypeStruct((2, 2, 2, HALF_ROWS), single),
        ],
        compiler_params=pltpu.CompilerParams(vmem_limit_bytes=32 << 20),
        cost_estimate=kernel_cost(5),
        name="projected",
    )(rows, weight)


def columns(values):
    return jnp.transpose(values, (0, 1, 3, 2)).reshape(-1, 2)


def rotated_heads(lin, recips, gains, cosine, sine, groups):
    rows = HALF_ROWS // groups
    return pl.pallas_call(
        rotate_kernel,
        grid=(2, 2),
        in_specs=[
            token_spec(lin.shape[1]), token_spec(2), whole_spec(gains.shape),
            token_spec(HEAD_DIM), token_spec(HEAD_DIM),
        ],
        out_specs=split_spec(groups, rows),
        out_shape=jax.ShapeDtypeStruct((2, 2, groups, 2, 3, rows, HEAD_DIM), bfloat),
        cost_estimate=kernel_cost(5),
        name="rotated_heads",
    )(lin, recips, gains, cosine, sine)


def rotated_sums(d_split, lin, recips, gains, cosine, sine):
    groups, rows = d_split.shape[2], d_split.shape[5]
    return pl.pallas_call(
        sums_kernel,
        grid=(2, 2),
        in_specs=[
            split_spec(groups, rows), token_spec(lin.shape[1]), token_spec(2),
            whole_spec(gains.shape), token_spec(HEAD_DIM), token_spec(HEAD_DIM),
        ],
        out_specs=[
            pl.BlockSpec(gains.shape, lambda near, half: (0, 0)),
            pl.BlockSpec((1, 1, 2, HALF_ROWS), lambda near, half: (near, half, 0, 0)),
        ],
        out_shape=[
            jax.ShapeDtypeStruct(gains.shape, single),
            jax.ShapeDtypeStruct((2, 2, 2, HALF_ROWS), single),
        ],
        cost_estimate=kernel_cost(5),
        name="rotated_sums",
    )(d_split, lin, recips, gains, cosine, sine)


def rotated_back(d_split, lin, recips, means, gains, cosine, sine):
    groups, rows = d_split.shape[2], d_split.shape[5]
    return pl.pallas_call(
        lin_kernel,
        grid=(2, 2),
        in_specs=[
            split_spec(groups, rows), token_spec(lin.shape[1]), token_spec(2), token_spec(2),
            whole_spec(gains.shape), token_spec(HEAD_DIM), token_spec(HEAD_DIM),
        ],
        out_specs=token_spec(lin.shape[1]),
        out_shape=jax.ShapeDtypeStruct(lin.shape, bfloat),
        cost_estimate=kernel_cost(5),
        name="rotated_back",
    )(d_split, lin, recips, means, gains, cosine, sine)


def unpack_kernel(in_ref, *out_refs):
    count, rows, width = in_ref.shape
    part = width // 3
    for which in range(3):
        for piece in range(count):
            out_refs[which][:, pl.ds(piece * part, part)] = in_ref[
                piece, :, pl.ds(which * part, part)
            ].astype(single)


def unpacked(values):
    count, rows, width = values.shape
    return pl.pallas_call(
        unpack_kernel,
        out_shape=[jax.ShapeDtypeStruct((rows, count * width // 3), single)] * 3,
        name="unpacked",
    )(values)


def dot_tn(a, b):
    return lax.dot_general(a, b, (((0,), (0,)), ((), ())), preferred_element_type=single)


def picks(slot_ref, source, expert, capacity):
    slots = slot_ref[source, pl.ds(expert, 1), :]
    rows = lax.broadcasted_iota(jnp.int32, (capacity, slots.shape[1]), 0) + 1
    return slots == rows.astype(single)


def spread_tokens(slot_ref, first, second, out_ref, capacity):
    for source in range(slot_ref.shape[0]):
        at = slice(source * capacity, (source + 1) * capacity)
        total = dot_tn(picks(slot_ref, source, 0, capacity).astype(bfloat), first[at])
        total += dot_tn(picks(slot_ref, source, 1, capacity).astype(bfloat), second[at])
        out_ref[source] = total.astype(bfloat)


def expert_kernel(
    blk_ref, slot_ref, ffn_ref, cot_ref, router_ref, gate_ref, up_ref, down_ref, gate_tile_ref,
    up_tile_ref, x_ref, c_ref, value_ref, hidden_ref, d_gate_ref, d_up_ref, probs_ref, out_ref,
    grad_ref, d_both_ref, first_ref,
):
    expert, step = pl.program_id(0), pl.program_id(1)
    sources = ffn_ref.shape[0]
    capacity = x_ref.shape[1] // sources
    part = gate_ref.shape[-1]
    tile = gate_tile_ref.shape[-2]

    @pl.when((expert == 0) & (step == 0))
    def _():
        for source in range(sources):
            logits = dot_nt(router_ref[...], ffn_ref[source])
            shifted = jnp.exp(logits - jnp.max(logits, axis=0, keepdims=True))
            probs_ref[source] = shifted / jnp.sum(shifted, axis=0, keepdims=True)

    def fill(which):
        for source in range(sources):
            at = pl.ds(source * capacity, capacity)
            picked = picks(slot_ref, source, which, capacity)
            picked_low = picked.astype(bfloat)
            x_ref[0, at, :] = jnp.dot(
                picked_low, ffn_ref[source], preferred_element_type=single
            ).astype(bfloat)
            cot_rows = jnp.dot(picked_low, cot_ref[source], preferred_element_type=single)
            c_ref[0, at, :] = cot_rows.astype(bfloat)
            probs = probs_ref[source, pl.ds(2 * blk_ref[0] + which, 1), :]
            value = jnp.sum(jnp.where(picked, probs, 0.0), axis=1, keepdims=True)
            value_ref[0, at, :] = value
            grad_ref[at, :] = (value * cot_rows).astype(bfloat)

    pl.when(step == 0)(lambda: fill(expert))

    @pl.when(step < 4)
    def _():
        w_both = jnp.concatenate([gate_ref[0, 0, 0], up_ref[0, 0, 0]], axis=1)
        both = jnp.dot(x_ref[0], w_both, preferred_element_type=single)
        gate_val, up_val = both[:, :part], both[:, part:]
        d_hidden = dot_nt(grad_ref[...], down_ref[0, 0])
        sigmoid = 1.0 / (1.0 + jnp.exp(-gate_val))
        silu = gate_val * sigmoid
        hidden_ref[0] = (silu * up_val).astype(bfloat)
        d_gate = (d_hidden * up_val * sigmoid * (1.0 + gate_val * (1.0 - sigmoid))).astype(bfloat)
        d_up = (d_hidden * silu).astype(bfloat)
        d_gate_ref[0] = d_gate
        d_up_ref[0] = d_up
        at = pl.multiple_of(2 * step * part, part)
        d_both_ref[:, pl.ds(at, part)] = d_gate
        d_both_ref[:, pl.ds(pl.multiple_of(at + part, part), part)] = d_up

    @pl.when(step >= 4)
    def _():
        weights = [ref[i, 0, 0] for i in range(4) for ref in (gate_tile_ref, up_tile_ref)]
        d_rows = dot_nt(d_both_ref[...], jnp.concatenate(weights, axis=1)).astype(bfloat)
        at = pl.ds(pl.multiple_of((step - 4) * tile, tile), tile)

        @pl.when(expert == 0)
        def _():
            first_ref[:, at] = d_rows

        @pl.when(expert == 1)
        def _():
            spread_tokens(slot_ref, first_ref[:, at], d_rows, out_ref, capacity)


def down_grads_kernel(c_ref, value_ref, hidden_ref, sent_ref, kept_ref, grad_ref):
    step = pl.program_id(1)

    @pl.when(step == 0)
    def _():
        grad_ref[...] = (value_ref[0] * c_ref[0].astype(single)).astype(bfloat)

    down = dot_tn(hidden_ref[0], grad_ref[...])

    @pl.when(step < 2)
    def _():
        sent_ref[0, 0] = down.astype(bfloat)

    @pl.when(step >= 2)
    def _():
        kept_ref[0, 0] = down


def grads_kernel(
    slot_ref, x_ref, c_ref, value_ref, hidden_ref, d_gate_ref, d_up_ref, down_tile_ref,
    gate_sent_ref, up_sent_ref, gate_kept_ref, up_kept_ref,
    d_probs_ref, out_ref, xt_ref, dots_ref, first_ref,
):
    expert, step = pl.program_id(0), pl.program_id(1)
    sources = slot_ref.shape[0]
    capacity = x_ref.shape[1] // sources
    part = d_gate_ref.shape[2]
    tile = down_tile_ref.shape[3]

    @pl.when(step == 0)
    def _():
        xt_ref[...] = jnp.transpose(x_ref[0])
        dots_ref[...] = jnp.zeros_like(dots_ref)

    @pl.when(step < 4)
    def _():
        d_both = jnp.concatenate([d_gate_ref[0], d_up_ref[0]], axis=1)
        both = jnp.dot(xt_ref[...], d_both, preferred_element_type=single)

        @pl.when(step < 2)
        def _():
            gate_sent_ref[0, 0] = both[:, :part].astype(bfloat)
            up_sent_ref[0, 0] = both[:, part:].astype(bfloat)

        @pl.when(step >= 2)
        def _():
            gate_kept_ref[0, 0] = both[:, :part]
            up_kept_ref[0, 0] = both[:, part:]

    @pl.when(step >= 4)
    def _():
        down = jnp.concatenate([down_tile_ref[i, 0] for i in range(4)], axis=0)
        expert_out = jnp.dot(hidden_ref[0], down, preferred_element_type=single)
        expert_out = expert_out.astype(bfloat).astype(single)
        at = pl.ds(pl.multiple_of((step - 4) * tile, tile), tile)
        dots_ref[...] += jnp.sum(
            c_ref[0, :, at].astype(single) * expert_out, axis=1, keepdims=True
        )
        weighted = (value_ref[0] * expert_out).astype(bfloat)

        @pl.when(expert == 0)
        def _():
            first_ref[:, at] = weighted

        @pl.when(expert == 1)
        def _():
            spread_tokens(slot_ref, first_ref[:, at], weighted, out_ref, capacity)

    @pl.when(step == 7)
    def _():
        for source in range(sources):
            picked = picks(slot_ref, source, expert, capacity)
            row = dots_ref[source * capacity : (source + 1) * capacity]
            d_probs_ref[source, pl.ds(expert, 1), :] = jnp.sum(
                jnp.where(picked, row, 0.0), axis=0, keepdims=True
            )


def rows_spec(rows, columns):
    return pl.BlockSpec((1, rows, columns), lambda e, k, *_: (e, 0, 0))


def first_half(k):
    return jnp.minimum(k, 3)


def second_half(k):
    return jnp.maximum(k - 4, 0)


def part_spec(rows, columns):
    return pl.BlockSpec((1, rows, columns), lambda e, k, *_: (e, 0, first_half(k)))


def weight_spec(shape, place=first_half):
    return pl.BlockSpec((1, 1) + shape[2:], lambda e, k, *_: (place(k), e, 0, 0))


def token_tile_spec(shape):
    block = shape[:2] + (shape[2] // 4,)
    return pl.BlockSpec(block, lambda e, k, *_: (0, 0, e * second_half(k)))


def pair_spec(shape, which):
    return pl.BlockSpec(
        (1, 1, 1) + shape[3:], lambda e, k, *_: (first_half(k), which, e, 0, 0)
    )


def pair_tile_spec(shape, which):
    return pl.BlockSpec(
        (4, 1, 1, shape[3] // 4, shape[4]), lambda e, k, *_: (0, which, e, second_half(k), 0)
    )


def expert_rows(blk, slot_map, ffn_all, cot_all, router_t, pair, down, capacity):
    sources, tokens, width = ffn_all.shape
    rows, experts, hidden = sources * capacity, router_t.shape[0], 4 * down.shape[2]
    wide = jax.ShapeDtypeStruct((2, rows, width), bfloat)
    narrow = jax.ShapeDtypeStruct((2, rows, hidden), bfloat)
    probs = jax.ShapeDtypeStruct((sources, experts, tokens), single)
    return pl.pallas_call(
        expert_kernel,
        grid_spec=pltpu.PrefetchScalarGridSpec(
            num_scalar_prefetch=1,
            grid=(2, 8),
            in_specs=[
                whole_spec(slot_map.shape), whole_spec(ffn_all.shape), whole_spec(cot_all.shape),
                whole_spec(router_t.shape), pair_spec(pair.shape, 0), pair_spec(pair.shape, 1),
                weight_spec(down.shape), pair_tile_spec(pair.shape, 0), pair_tile_spec(pair.shape, 1),
            ],
            out_specs=[
                rows_spec(rows, width), rows_spec(rows, width), rows_spec(rows, 1),
                part_spec(rows, hidden // 4), part_spec(rows, hidden // 4),
                part_spec(rows, hidden // 4), whole_spec(probs.shape), token_tile_spec(ffn_all.shape),
            ],
            scratch_shapes=[
                pltpu.VMEM((rows, width), bfloat), pltpu.VMEM((rows, 2 * hidden), bfloat),
                pltpu.VMEM((rows, width), bfloat),
            ],
        ),
        out_shape=[
            wide, wide, jax.ShapeDtypeStruct((2, rows, 1), single), narrow, narrow, narrow,
            probs, jax.ShapeDtypeStruct(ffn_all.shape, bfloat),
        ],
        compiler_params=pltpu.CompilerParams(vmem_limit_bytes=60 << 20),
        cost_estimate=kernel_cost(55),
        name="expert_rows",
    )(blk[None], slot_map, ffn_all, cot_all, router_t, pair, pair, down, pair, pair)


def sent_place(k):
    return jnp.minimum(k, 1)


def kept_place(k):
    return jnp.clip(k - 2, 0, 1)


def expert_down_grads(c, value, hidden):
    rows, width = c.shape[1:]
    part = hidden.shape[2] // 4
    shape = (2, 2, part, width)
    return pl.pallas_call(
        down_grads_kernel,
        grid=(2, 4),
        in_specs=[rows_spec(rows, width), rows_spec(rows, 1), part_spec(rows, part)],
        out_specs=[weight_spec(shape, sent_place), weight_spec(shape, kept_place)],
        out_shape=[jax.ShapeDtypeStruct(shape, bfloat), jax.ShapeDtypeStruct(shape, single)],
        scratch_shapes=[pltpu.VMEM((rows, width), bfloat)],
        compiler_params=pltpu.CompilerParams(vmem_limit_bytes=40 << 20),
        cost_estimate=kernel_cost(12),
        name="expert_down_grads",
    )(c, value, hidden)


def expert_grads(slot_map, x, c, value, hidden, d_gate, d_up, down, tokens):
    rows, width = x.shape[1:]
    part = down.shape[2]
    wide = (2, 2, width, part)
    summed = (slot_map.shape[0], tokens, width)
    return pl.pallas_call(
        grads_kernel,
        grid=(2, 8),
        in_specs=[
            whole_spec(slot_map.shape), rows_spec(rows, width), rows_spec(rows, width),
            rows_spec(rows, 1), rows_spec(rows, 4 * part), part_spec(rows, part),
            part_spec(rows, part),
            pl.BlockSpec((4, 1, part, width // 4), lambda e, k: (0, e, 0, second_half(k))),
        ],
        out_specs=[weight_spec(wide, sent_place)] * 2
        + [weight_spec(wide, kept_place)] * 2
        + [whole_spec(slot_map.shape), token_tile_spec(summed)],
        out_shape=[jax.ShapeDtypeStruct(wide, bfloat)] * 2
        + [jax.ShapeDtypeStruct(wide, single)] * 2
        + [
            jax.ShapeDtypeStruct(slot_map.shape, single),
            jax.ShapeDtypeStruct(summed, bfloat),
        ],
        scratch_shapes=[
            pltpu.VMEM((width, rows), bfloat), pltpu.VMEM((rows, 1), single),
            pltpu.VMEM((rows, width), bfloat),
        ],
        compiler_params=pltpu.CompilerParams(vmem_limit_bytes=60 << 20),
        cost_estimate=kernel_cost(39),
        name="expert_grads",
    )(slot_map, x, c, value, hidden, d_gate, d_up, down)


def plain_experts(blk, slot_map, ffn_all, cot_all, router_t, pair, down, capacity):
    sources, tokens, width = ffn_all.shape
    count = slot_map.shape[1]

    def joined(weights, axis):
        return jnp.concatenate([weights[i] for i in range(4)], axis=axis)

    gate, up, down = joined(pair[:, 0], 2), joined(pair[:, 1], 2), joined(down, 1)
    slot_at = jnp.arange(1, capacity + 1, dtype=jnp.int32).astype(single)
    picked = jnp.transpose(slot_map, (1, 0, 2))[:, :, None, :] == slot_at[None, None, :, None]
    picked_low = picked.astype(bfloat)
    logits = jnp.einsum("ed,std->set", router_t, ffn_all, preferred_element_type=single)
    shifted = jnp.exp(logits - jnp.max(logits, axis=1, keepdims=True))
    probs = shifted / jnp.sum(shifted, axis=1, keepdims=True)
    local = jnp.transpose(lax.dynamic_slice_in_dim(probs, blk * count, count, 1), (1, 0, 2))
    value = jnp.sum(jnp.where(picked, local[:, :, None, :], 0.0), axis=3).reshape(count, -1, 1)

    def dispatch(rows):
        rows = jnp.einsum("esct,std->escd", picked_low, rows, preferred_element_type=single)
        return rows.astype(bfloat).reshape(count, -1, width)

    def combine(rows):
        rows = rows.astype(bfloat).reshape(count, sources, capacity, width)
        total = jnp.einsum("esct,escd->std", picked_low, rows, preferred_element_type=single)
        return total.astype(bfloat)

    def dots(spec, *arrays):
        return jnp.einsum(spec, *arrays, preferred_element_type=single)

    x, c = dispatch(ffn_all), dispatch(cot_all).astype(single)
    grad = (value * c).astype(bfloat)
    gate_val, up_val = dots("erd,edf->erf", x, gate), dots("erd,edf->erf", x, up)
    sigmoid = jax.nn.sigmoid(gate_val)
    hidden = (gate_val * sigmoid * up_val).astype(bfloat)
    d_hidden = dots("erd,efd->erf", grad, down)
    d_gate = (d_hidden * up_val * sigmoid * (1.0 + gate_val * (1.0 - sigmoid))).astype(bfloat)
    d_up = (d_hidden * gate_val * sigmoid).astype(bfloat)
    d_part = combine(dots("erf,edf->erd", d_gate, gate) + dots("erf,edf->erd", d_up, up))
    expert_out = dots("erf,efd->erd", hidden, down).astype(bfloat).astype(single)
    d_value = jnp.sum(c * expert_out, axis=2).reshape(count, sources, capacity, 1)
    d_probs = jnp.transpose(jnp.sum(jnp.where(picked, d_value, 0.0), axis=2), (1, 0, 2))
    mixed_part = combine(value * expert_out)

    def cut(total, axis):
        parts = jnp.stack(jnp.split(total, 4, axis=axis))
        return parts[:2].astype(bfloat), parts[2:]

    gate_sent, gate_kept = cut(dots("erd,erf->edf", x, d_gate), 2)
    up_sent, up_kept = cut(dots("erd,erf->edf", x, d_up), 2)
    down_sent, down_kept = cut(dots("erf,erd->efd", hidden, grad), 1)
    return probs, d_part, (down_sent, down_kept), (
        gate_sent, up_sent, gate_kept, up_kept, d_probs, mixed_part
    )


def per_device(
    block_input, w_query, w_key, w_value, w_out, attn_gain, ffn_gain, query_gain, key_gain,
    router, w_gate, w_up, w_down, expert_ids, slot_ids, doc_starts, cotangent,
):
    ulysses_size = lax.axis_size("ulysses")
    blk_size = lax.axis_size(BLK)
    blk = lax.axis_index(BLK)
    uly = lax.axis_index("ulysses")
    core = uly % 2
    own_tokens, width = block_input.shape
    picks = expert_ids.shape[1]
    experts = router.shape[1]
    capacity = 5 * own_tokens * picks // (4 * experts)
    local_experts = experts // blk_size
    blk_tokens = ulysses_size * own_tokens
    far_size = blk_size // 2
    far_tokens = 2 * blk_tokens
    plane_size = 2 * ulysses_size
    local_width = width // ulysses_size
    plane_width = width // plane_size
    weight_rows = w_query.shape[0]
    groups = blk_size // 8
    plane = 2 * uly + blk % 2

    projections = jnp.concatenate(
        [
            weight.astype(bfloat).reshape(weight_rows, plane_size, plane_width)
            for weight in (w_query, w_key, w_value)
        ],
        axis=2,
    )
    projections = lax.all_to_all(
        jnp.transpose(projections, (1, 0, 2)), PLANE, split_axis=0, concat_axis=0, tiled=True
    )
    projections = projections.reshape(ulysses_size, 2 * weight_rows, 3 * plane_width)
    small = jnp.concatenate(
        [jnp.stack([attn_gain, ffn_gain, query_gain, key_gain]), router.T]
    ).astype(bfloat)
    projections, small = tie(projections, gather_ulysses(small))
    w_qkv = gather_line(projections, 1).reshape(width, 3 * plane_width)
    small = gather_blk_small(small)
    gate_mine, up_mine, down_mine = w_gate.astype(bfloat), w_up.astype(bfloat), w_down.astype(bfloat)
    plane_input = gather_plane(block_input).reshape(far_tokens, width)
    pair_mine = jnp.stack([gate_mine, up_mine])
    pair_beyond = swap(pair_mine, 2)
    attn_g = small[0].astype(single)
    ffn_g = small[1].astype(single)
    plane_gains = lax.dynamic_slice_in_dim(
        small[2:4], plane * plane_width, plane_width, 1
    ).astype(single)
    router_t = small[4:]

    inputs = block_input.astype(single)
    hat_one, recip_one = norm_parts(inputs)
    normed = (norm_parts(plane_input.astype(single))[0] * attn_g).astype(bfloat)
    lin, squares = projected(normed, w_qkv)
    w_o = lax.all_gather(w_out.astype(bfloat), BLK, axis=0, tiled=True)
    named = expert_ids[:, :, None] == jnp.arange(experts, dtype=jnp.int32)[None, None, :]
    slot_map = jnp.sum(jnp.where(named, slot_ids[:, :, None] + 1, 0), axis=1)
    slot_map = slot_map.T.astype(single).reshape(blk_size, local_experts, own_tokens)
    squares, pair_beyond, w_o = tie(squares, pair_beyond, w_o)
    squares, down_mine = tie(sum_plane(squares), down_mine)
    down_beyond = swap(down_mine, 2)
    recips = columns(lax.rsqrt(squares / width + NORM_EPSILON))
    far_at = blk // 2 * far_tokens + jnp.arange(far_tokens, dtype=jnp.int32)
    cosine, sine = angles(far_at - doc_begins(doc_starts, far_at), HEAD_DIM)
    split = rotated_heads(lin, recips, plane_gains, cosine, sine, groups)
    heads_in = line_to_heads(split, far_size)
    heads_in, cotangent_sent, slot_map = tie(heads_in, cotangent, slot_map)
    slot_map = lax.all_to_all(slot_map, BLK, split_axis=0, concat_axis=0, tiled=True)
    cot_all = lax.all_gather(cotangent_sent, BLK, axis=0)
    part_rows = heads_in.shape[2]
    if groups == 1:
        query, mine = heads_in, heads_in
    else:
        query = heads_in[:, 0].reshape(-1, 1, QUERY_ROWS, HEAD_DIM)
        mine = lax.all_gather(
            heads_in[:, 1:], "far", axis=2, axis_index_groups=head_groups(far_size, groups)
        ).reshape(blk_size, 2, HALF_ROWS, HEAD_DIM)
    other, pair_mine, pair_beyond, down_mine = tie(
        swap(mine[:, -2:], 1), pair_mine, pair_beyond, down_mine
    )
    pair_near, pair_far, down_near = swap(pair_mine, 1), swap(pair_beyond, 1), swap(down_mine, 1)
    query_at = (
        jnp.arange(blk_size, dtype=jnp.int32)[:, None] * blk_tokens
        + core * HALF_ROWS
        + blk // 2 % groups * part_rows
        + jnp.arange(part_rows, dtype=jnp.int32)[None, :]
    ).reshape(-1, QUERY_ROWS)
    query_begin = doc_begins(doc_starts, query_at)
    scalars = (core[None],) + block_bounds(query_at, query_begin)
    query_at, query_begin = query_at[:, None], query_begin[:, None]
    head_out, lse = attention_forward(scalars, query_at, query_begin, query, mine, other)
    attended = blk_from_heads(
        head_out.astype(bfloat).reshape(blk_size, part_rows, HEAD_DIM), blk_size
    )
    attended, down_beyond, pair_near, pair_far, down_near = tie(
        attended, down_beyond, pair_near, pair_far, down_near
    )
    down_far = swap(down_beyond, 1)
    out_part = jnp.dot(attended, w_o, preferred_element_type=single)

    def token_rows(values):
        return lambda bits: lax.dynamic_slice_in_dim(
            values, (uly ^ bits) * own_tokens, own_tokens, 0
        )

    residual_mid = inputs + scatter_sum_ulysses(token_rows(out_part))
    hat_two, recip_two = norm_parts(residual_mid)
    ffn_in = (hat_two * ffn_g).astype(bfloat)

    ffn_in, pair_near, pair_far, pair_mine, pair_beyond = tie(
        ffn_in, pair_near, pair_far, pair_mine, pair_beyond
    )
    ffn_all = lax.all_gather(ffn_in, BLK, axis=0)
    expert_pair = jnp.stack([pair_near, pair_far, pair_mine, pair_beyond])
    expert_down = jnp.stack([down_near, down_far, down_mine, down_beyond])
    if capacity % 16 == 0:
        *kept_rows, probs_all, d_part = expert_rows(
            blk, slot_map, ffn_all, cot_all, router_t, expert_pair, expert_down, capacity
        )
        *kept_rows, d_part = tie(*kept_rows, d_part)
        x, c, value, hidden, d_gate, d_up = kept_rows
        down_results = expert_down_grads(c, value, hidden)
        x, *down_results = tie(x, *down_results)
        results = expert_grads(
            slot_map, x, c, value, hidden, d_gate, d_up, expert_down, own_tokens
        )
    else:
        probs_all, d_part, down_results, results = plain_experts(
            blk, slot_map, ffn_all, cot_all, router_t, expert_pair, expert_down, capacity
        )
    d_ffn_in = lax.psum_scatter(d_part, BLK, scatter_dimension=0).astype(single)
    down_sent, down_kept = down_results
    gate_sent, up_sent, gate_kept, up_kept, d_probs, mixed_part = results

    d_probs = lax.all_to_all(d_probs, BLK, split_axis=0, concat_axis=0, tiled=True)
    d_probs = d_probs.reshape(experts, own_tokens)
    gate_sent, up_sent, down_got = tie(gate_sent, up_sent, swap(down_sent, 1))
    gate_got, up_got = swap(gate_sent, 1), swap(up_sent, 1)

    def onward(got, kept):
        return (kept[1] + got[1].astype(single)).astype(bfloat)

    down_sent = onward(down_got, down_kept)
    gate_sent = onward(gate_got, gate_kept)
    d_ffn_in, mixed_part, up_got, gate_sent = tie(d_ffn_in, mixed_part, up_got, gate_sent)
    mixed_sum = lax.psum_scatter(mixed_part, BLK, scatter_dimension=0)

    router_probs = lax.dynamic_index_in_dim(probs_all, blk, 0, keepdims=False)
    d_logits = (
        router_probs * (d_probs - jnp.sum(router_probs * d_probs, axis=0, keepdims=True))
    ).astype(bfloat)
    grad_router_part = jnp.dot(d_logits, ffn_in, preferred_element_type=single)
    d_ffn_in = d_ffn_in + dot_tn(d_logits, router_t)
    grad_ffn_part = jnp.sum(d_ffn_in * hat_two, axis=0)
    d_mid = cotangent.astype(single) + norm_back(d_ffn_in * ffn_g, hat_two, recip_two)

    d_attn_out = gather_ulysses(d_mid.astype(bfloat)).reshape(blk_tokens, width)
    narrow = scatter_sum_ulysses(
        lambda bits: lax.dynamic_slice_in_dim(
            jnp.concatenate([grad_ffn_part[None], grad_router_part]),
            (uly ^ bits) * local_width, local_width, 1,
        ),
        single,
    )
    d_attn_out, gate_sent, narrow = tie(d_attn_out, gate_sent, narrow)
    gate_across = swap(gate_sent, 2)
    d_attended = dot_nt(d_attn_out, w_o).astype(bfloat)
    grad_out_part = jnp.einsum("ti,to->io", attended, d_attn_out, preferred_element_type=single)
    grad_out_part = grad_out_part.astype(bfloat).reshape(blk_size, weight_rows, width)
    d_halves, up_got = tie(blk_halves(d_attended, blk_size), up_got)
    up_sent = onward(up_got, up_kept)
    d_out = lax.all_to_all(d_halves, BLK, split_axis=0, concat_axis=0, tiled=True)
    d_out = d_out.reshape(head_out.shape)
    d_out, grad_out_part, up_sent = tie(d_out, grad_out_part, up_sent)
    up_across = swap(up_sent, 2)
    grad_w_out = lax.psum_scatter(grad_out_part, BLK, scatter_dimension=0)
    dq_head, keep, send = attention_backward(
        scalars, query_at, query_begin, lse, head_out, query, d_out, mine, other
    )
    dq_head, gate_across = tie(dq_head, gate_across)
    d_keys = (keep + swap(send, 1).astype(single)).astype(bfloat)
    if groups > 1:
        moved = jnp.moveaxis(d_keys.reshape(blk_size, 2, groups, part_rows, HEAD_DIM), 2, 0)
        moved = lax.psum_scatter(
            moved, "far", scatter_dimension=0, axis_index_groups=head_groups(far_size, groups)
        )
        d_keys = moved
    d_stack = jnp.concatenate(
        [dq_head.reshape(blk_size, 1, part_rows, HEAD_DIM), d_keys], axis=1
    )
    d_split = line_from_heads(d_stack, far_size)
    d_split, up_across, mixed_sum = tie(d_split, up_across, mixed_sum)
    mixed = (residual_mid + mixed_sum.astype(single)).astype(bfloat)
    gain_parts, means = rotated_sums(d_split, lin, recips, plane_gains, cosine, sine)
    means, down_sent = tie(sum_plane(means), down_sent)
    down_across = swap(down_sent, 2)
    means = columns(means / width)
    d_lin = rotated_back(d_split, lin, recips, means, plane_gains, cosine, sine)
    grads = jnp.einsum("td,to->do", normed, d_lin, preferred_element_type=single)
    grads = grads.astype(bfloat).reshape(ulysses_size, far_size, 2 * weight_rows, 3 * plane_width)
    grads = jnp.transpose(grads, (1, 0, 2, 3)).reshape(-1, 3 * plane_width)
    grads = lax.psum_scatter(grads, "far", scatter_dimension=0, tiled=True)
    d_normed_part = dot_nt(d_lin, w_qkv)
    grad_attn_part = jnp.sum(d_normed_part * norm_parts(plane_input.astype(single))[0], axis=0)
    d_normed_part = d_normed_part.reshape(2, blk_tokens, width)
    side = blk % 2

    def near_rows(bits):
        mine, other = (
            lax.dynamic_slice(
                d_normed_part, (place, (uly ^ bits) * own_tokens, 0), (1, own_tokens, width)
            )[0]
            for place in (side, 1 - side)
        )
        return mine, other


    def whole_sum(kept, got, across):
        return kept[0] + got[0].astype(single) + across.astype(single)

    grad_w_gate = whole_sum(gate_kept, gate_got, gate_across)
    grad_w_up = whole_sum(up_kept, up_got, up_across)
    d_normed, (grad_w_gate, grad_w_up, grad_attn_part, grad_w_out) = scatter_sum_plane(
        near_rows, (grad_w_gate, grad_w_up, grad_attn_part, grad_w_out)
    )
    grad_w_out = grad_w_out.astype(single)
    grad_w_down = whole_sum(down_kept, down_got, down_across)
    input_grad = d_mid + norm_back(d_normed * attn_g, hat_one, recip_one)

    def own_columns(values):
        return scatter_sum_ulysses(
            lambda bits: lax.dynamic_slice_in_dim(values, (uly ^ bits) * local_width, local_width, 1),
            single,
        )

    gain_parts = lax.dynamic_update_slice_in_dim(
        jnp.zeros((2, local_width), single), gain_parts, side * plane_width, 1
    )
    last = own_columns(grad_attn_part[None])
    gains = scatter_sum_blk_small(jnp.concatenate([last, narrow, gain_parts]))
    grads = grads.reshape(plane_size, weight_rows, 3 * plane_width)
    grads = lax.all_to_all(grads, PLANE, split_axis=0, concat_axis=0, tiled=True)
    grads = unpacked(grads)
    return (
        mixed,
        input_grad.astype(bfloat),
        grads[0],
        grads[1],
        grads[2],
        grad_w_out,
        gains[0],
        gains[1],
        gains[-2],
        gains[-1],
        gains[2:-2].T,
        grad_w_gate,
        grad_w_up,
        grad_w_down,
    )


def solution(mesh):
    in_specs = (
        P(("far", "near", "ulysses"), None),
        P(("ulysses", "far", "near"), None),
        P(("ulysses", "far", "near"), None),
        P(("ulysses", "far", "near"), None),
        P(("ulysses", "far", "near"), None),
        P(("ulysses", "far", "near")),
        P(("ulysses", "far", "near")),
        P(("ulysses", "far", "near")),
        P(("ulysses", "far", "near")),
        P(("ulysses", "far", "near"), None),
        P(BLK, None, "ulysses"),
        P(BLK, None, "ulysses"),
        P(BLK, "ulysses", None),
        P(("far", "near", "ulysses"), None),
        P(("far", "near", "ulysses"), None),
        P(),
        P(("far", "near", "ulysses"), None),
    )
    out_specs = (
        P(("far", "near", "ulysses"), None),
        P(("far", "near", "ulysses"), None),
        P(("ulysses", "far", "near"), None),
        P(("ulysses", "far", "near"), None),
        P(("ulysses", "far", "near"), None),
        P(("ulysses", "far", "near"), None),
        P(("ulysses", "far", "near")),
        P(("ulysses", "far", "near")),
        P(("ulysses", "far", "near")),
        P(("ulysses", "far", "near")),
        P(("ulysses", "far", "near"), None),
        P(BLK, None, "ulysses"),
        P(BLK, None, "ulysses"),
        P(BLK, "ulysses", None),
    )
    ulysses_size, blk_size = mesh.devices.shape
    shape = (ulysses_size, blk_size // 2, 2)
    split_mesh = jax.sharding.Mesh(mesh.devices.reshape(shape), ("ulysses", "far", "near"))
    return jax.shard_map(
        per_device, mesh=split_mesh, in_specs=in_specs, out_specs=out_specs, check_vma=False
    )
```

```python
import math

import jax
import jax.numpy as jnp
from jax import lax
from jax.experimental import pallas as pl
from jax.experimental.pallas import tpu as pltpu
from jax.sharding import PartitionSpec as P

HEAD_DIM = 128
NORM_EPSILON = 1e-05
ROPE_BASE = 10000.0
MASKED_SCORE = -1e30
SCORE_SCALE = HEAD_DIM ** (-0.5)
LOG2_SCALE = SCORE_SCALE * math.log2(math.e)
QUERY_ROWS = 256
HALF_ROWS = 256
KEY_ROWS = 512
BLK = ("far", "near")
PLANE = ("ulysses", "near")
bfloat = jnp.bfloat16
single = jnp.float32


def norm_parts(values):
    recip_factor = lax.rsqrt(jnp.mean(values * values, axis=-1, keepdims=True) + NORM_EPSILON)
    return (values * recip_factor, recip_factor)


def norm_back(grad_in, hat_values, recip_factor):
    return recip_factor * (
        grad_in - hat_values * jnp.mean(grad_in * hat_values, axis=-1, keepdims=True)
    )


def doc_begins(doc_starts, tokens_at):
    at_or_before = doc_starts[:, None] <= tokens_at.reshape(1, -1)
    begins = jnp.max(jnp.where(at_or_before, doc_starts[:, None], 0), axis=0)
    return begins.reshape(tokens_at.shape)


def angles(position, head_size):
    half_size = head_size // 2
    frequency = ROPE_BASE ** (-(jnp.arange(half_size, dtype=jnp.float32) * 2.0 / head_size))
    turn = position.astype(jnp.float32)[:, None] * frequency[None, :]
    cosine, sine = jnp.cos(turn), jnp.sin(turn)
    return jnp.concatenate([cosine, cosine], 1), jnp.concatenate([-sine, sine], 1)


def swap(values, bit, axis="ulysses"):
    size = lax.axis_size(axis)
    return lax.ppermute(values, axis, [(i, i ^ bit) for i in range(size)])


def gather_plane(values):
    me, side = lax.axis_index("ulysses"), lax.axis_index("near")
    near = swap(values, 1, "near")
    beyond = swap(values, 2)
    corner = swap(beyond, 1, "near")
    out = jnp.zeros((2, 4) + values.shape, values.dtype)
    for other, bit, part in ((0, 0, values), (0, 2, beyond), (1, 0, near), (1, 2, corner)):
        for core, piece in ((0, part), (1, swap(part, 1))):
            place = (side ^ other, me ^ bit ^ core) + (0,) * values.ndim
            out = lax.dynamic_update_slice(out, piece[None, None], place)
    return out


def line_steps(size):
    for step in range(1, size):
        up = [(i, i + 1) for i in range(step - 1, size - 1)]
        yield up, [(size - 1 - i, size - 1 - j) for i, j in up]


def gather_line(values, axis):
    size = lax.axis_size("far")
    if size > 4:
        return lax.all_gather(values, "far", axis=axis)
    at = lax.axis_index("far")
    below, above, parts = values, values, []
    for step, (up, down) in enumerate(line_steps(size), 1):
        below, above = lax.ppermute(below, "far", up), lax.ppermute(above, "far", down)
        parts = [(at - step, below), (at + step, above)] + parts
    shape = values.shape[:axis] + (size,) + values.shape[axis:]
    out = jnp.zeros(shape, values.dtype)
    for place, part in parts + [(at, values)]:
        out = lax.dynamic_update_index_in_dim(out, part, jnp.clip(place, 0, size - 1), axis)
    return out


def gather_ulysses(values):
    me = lax.axis_index("ulysses")
    beyond = swap(values, 2)
    core = swap(values, 1)
    beyond_core = swap(beyond, 1)
    out = jnp.zeros((4,) + values.shape, values.dtype)
    for bit, part in enumerate((values, core, beyond, beyond_core)):
        out = lax.dynamic_update_index_in_dim(out, part, me ^ bit, 0)
    return out


def scatter_sum_ulysses(parts, kind=bfloat):
    far = swap(parts(3).astype(kind), 1)
    near = swap(parts(1).astype(kind), 1)
    across = swap((parts(2) + far.astype(single)).astype(kind), 2)
    return parts(0) + near.astype(single) + across.astype(single)


def scatter_sum_plane(parts, beside):
    kept, sent = [], []
    for bits in (0, 2):
        mine, other = parts(bits)
        core_mine, core_other = parts(bits ^ 1)
        got = swap(jnp.stack([core_mine, core_other]).astype(bfloat), 1).astype(single)
        kept.append(mine + got[0])
        sent.append(other + got[1])
    got = swap(jnp.stack(sent).astype(bfloat), 1, "near")
    got, beside = tie(got, beside)
    got = got.astype(single)
    across = swap((kept[1] + got[1]).astype(bfloat), 2)
    return kept[0] + got[0] + across.astype(single), beside


def gather_blk_small(values):
    ulysses_size, count, size = values.shape
    blk_size = lax.axis_size(BLK)
    mine = jnp.transpose(values, (1, 0, 2)).reshape(count, -1)
    out = lax.all_to_all(
        jnp.broadcast_to(mine, (blk_size,) + mine.shape), BLK, split_axis=0, concat_axis=0, tiled=True
    )
    out = out.reshape(blk_size, count, ulysses_size, size)
    return jnp.transpose(out, (1, 2, 0, 3)).reshape(count, -1)


def scatter_sum_blk_small(values):
    count, blk_size = values.shape[0], lax.axis_size(BLK)
    parts = jnp.transpose(values.reshape(count, blk_size, -1), (1, 0, 2))
    parts = lax.all_to_all(parts, BLK, split_axis=0, concat_axis=0, tiled=True)
    return jnp.sum(parts, axis=0)


def tie(*values):
    return lax.optimization_barrier(values)


def sum_plane(values):
    values = values + swap(values, 1)
    values = values + swap(values, 2)
    return values + swap(values, 1, "near")


def swap_halves(values, core):
    got = swap(lax.dynamic_index_in_dim(values, 1 - core, 0, keepdims=False), 1)
    return lax.dynamic_update_index_in_dim(values, got, 1 - core, 0)


def line_to_heads(split, far_size):
    count, rows = split.shape[4:6]
    both = swap_halves(split, lax.axis_index("ulysses") % 2)
    both = both.reshape(far_size, 2, count, rows, HEAD_DIM)
    both = lax.all_to_all(both, "far", split_axis=0, concat_axis=0, tiled=True)
    return both.reshape(2 * far_size, count, rows, HEAD_DIM)


def line_from_heads(stacked, far_size):
    count, rows = stacked.shape[1:3]
    back = stacked.reshape(far_size, 2, count, rows, HEAD_DIM)
    back = lax.all_to_all(back, "far", split_axis=0, concat_axis=0, tiled=True)
    back = back.reshape(2, 2, far_size // 4, 2, count, rows, HEAD_DIM)
    return swap_halves(back, lax.axis_index("ulysses") % 2)


def blk_halves(values, blk_size):
    core = lax.axis_index("ulysses") % 2
    groups = blk_size // 8
    rows = values.shape[0] // (2 * groups)
    split = values.reshape(2, groups, rows, 2, 2, HEAD_DIM)
    split = jnp.transpose(split, (0, 4, 1, 3, 2, 5))
    return swap_halves(split, core).reshape(blk_size, rows, HEAD_DIM)


def blk_from_heads(stacked, blk_size):
    core = lax.axis_index("ulysses") % 2
    groups, rows = blk_size // 8, stacked.shape[1]
    back = lax.all_to_all(stacked, BLK, split_axis=0, concat_axis=0, tiled=True)
    whole = swap_halves(back.reshape(2, 2, groups, 2, rows, HEAD_DIM), core)
    whole = jnp.transpose(whole, (0, 2, 4, 3, 1, 5))
    return whole.reshape(2 * groups * rows, 4 * HEAD_DIM)


def head_groups(far_size, groups):
    return [[j * groups + p for p in range(groups)] for j in range(far_size // groups)]


def kernel_cost(micros):
    return pl.CostEstimate(flops=micros * 10**9, bytes_accessed=0, transcendentals=0)


def dot_nt(a, b):
    return lax.dot_general(a, b, (((1,), (1,)), ((), ())), preferred_element_type=single)


def key_loops(low_ref, open_ref, close_ref, high_ref, index, step, carry):
    low, opened = low_ref[index], open_ref[index]
    closed, high = close_ref[index], high_ref[index]
    pairs = (closed - opened) // 2
    paired = opened + 2 * pairs

    def two(pair, carry):
        return step(opened + 2 * pair, carry, False, 2 * KEY_ROWS)

    carry = lax.fori_loop(low, opened, lambda kb, c: step(kb, c, True, KEY_ROWS), carry)
    carry = lax.fori_loop(0, pairs, two, carry)
    carry = lax.fori_loop(paired, closed, lambda kb, c: step(kb, c, False, KEY_ROWS), carry)
    return lax.fori_loop(closed, high, lambda kb, c: step(kb, c, True, KEY_ROWS), carry)


def allowed(start, pos, begin):
    key_at = start + lax.broadcasted_iota(jnp.int32, (KEY_ROWS, pos.shape[1]), 0)
    return (key_at <= pos) & (key_at >= begin)


def load_keys(core, mine_ref, other_ref, at, store):
    for blk in range(mine_ref.shape[0]):
        start = 2 * blk * HALF_ROWS
        store(pl.multiple_of(start + core * HALF_ROWS, HALF_ROWS), mine_ref[blk, at])
        store(pl.multiple_of(start + (1 - core) * HALF_ROWS, HALF_ROWS), other_ref[blk, at - mine_ref.shape[1] + 2])


def forward_kernel(
    core_ref, low_ref, open_ref, close_ref, high_ref,
    pos_ref, begin_ref, q_ref, mine_ref, other_ref, o_ref, lse_ref, k_ref, vt_ref,
):
    index = pl.program_id(0)

    @pl.when(index == 0)
    def _():
        core, last = core_ref[0], mine_ref.shape[1]

        def store_key(start, rows):
            k_ref[pl.ds(start, HALF_ROWS), :] = rows

        def store_value(start, rows):
            vt_ref[:, pl.ds(start, HALF_ROWS)] = jnp.transpose(rows)

        load_keys(core, mine_ref, other_ref, last - 2, store_key)
        load_keys(core, mine_ref, other_ref, last - 1, store_value)

    query = q_ref[0, 0]
    pos, begin = pos_ref[0], begin_ref[0]
    rows = query.shape[0]

    def step(block, carry, masked, size):
        top, total, acc = carry
        start = pl.multiple_of(block * KEY_ROWS, KEY_ROWS)
        scores = dot_nt(k_ref[pl.ds(start, size), :], query) * LOG2_SCALE
        if masked:
            scores = jnp.where(allowed(start, pos, begin), scores, MASKED_SCORE)
        new_top = jnp.maximum(top, jnp.max(scores, axis=0, keepdims=True))
        probs = jnp.exp2(scores - new_top)
        shrink = jnp.exp2(top - new_top)
        total = total * shrink + jnp.sum(probs, axis=0, keepdims=True)
        acc = acc * shrink + jnp.dot(
            vt_ref[:, pl.ds(start, size)], probs.astype(bfloat), preferred_element_type=single
        )
        return new_top, total, acc

    carry = (
        jnp.full((1, rows), MASKED_SCORE, single),
        jnp.zeros((1, rows), single),
        jnp.zeros((HEAD_DIM, rows), single),
    )
    top, total, acc = key_loops(low_ref, open_ref, close_ref, high_ref, index, step, carry)
    o_ref[0] = jnp.transpose(acc / total)
    lse_ref[0] = top + jnp.log2(total)


def backward_kernel(
    core_ref, low_ref, open_ref, close_ref, high_ref, pos_ref, begin_ref, lse_ref, o_ref,
    q_ref, do_ref, mine_ref, other_ref, dq_ref, keep_ref, send_ref, k_ref, v_ref, kt_ref, dk_ref, dv_ref,
):
    index = pl.program_id(0)
    core = core_ref[0]

    @pl.when(index == 0)
    def _():
        dk_ref[...] = jnp.zeros_like(dk_ref)
        dv_ref[...] = jnp.zeros_like(dv_ref)
        last = mine_ref.shape[1]

        def store_key(start, rows):
            k_ref[pl.ds(start, HALF_ROWS), :] = rows
            kt_ref[:, pl.ds(start, HALF_ROWS)] = jnp.transpose(rows)

        def store_value(start, rows):
            v_ref[pl.ds(start, HALF_ROWS), :] = rows

        load_keys(core, mine_ref, other_ref, last - 2, store_key)
        load_keys(core, mine_ref, other_ref, last - 1, store_value)

    query, d_out = q_ref[0, 0], do_ref[0]
    pos, begin = pos_ref[0], begin_ref[0]
    lse = lse_ref[0]
    products = d_out.astype(single) * o_ref[0]
    delta = jnp.sum(jnp.transpose(products), axis=0, keepdims=True)

    def step(block, acc, masked, size):
        start = pl.multiple_of(block * KEY_ROWS, KEY_ROWS)
        rows = pl.ds(start, size)
        scores = dot_nt(k_ref[rows, :], query) * LOG2_SCALE
        probs = jnp.exp2(scores - lse)
        if masked:
            probs = jnp.where(allowed(start, pos, begin), probs, 0.0)
        d_probs = dot_nt(v_ref[rows, :], d_out)
        d_scores = (probs * (d_probs - delta)).astype(bfloat)
        dv_ref[rows, :] += jnp.dot(probs.astype(bfloat), d_out, preferred_element_type=single)
        dk_ref[rows, :] += jnp.dot(d_scores, query, preferred_element_type=single)
        return acc + jnp.dot(kt_ref[:, rows], d_scores, preferred_element_type=single)

    acc = jnp.zeros((HEAD_DIM, query.shape[0]), single)
    acc = key_loops(low_ref, open_ref, close_ref, high_ref, index, step, acc)
    dq_ref[0] = (jnp.transpose(acc) * SCORE_SCALE).astype(bfloat)

    @pl.when(index == pl.num_programs(0) - 1)
    def _():
        for blk in range(keep_ref.shape[0]):
            start = 2 * blk * HALF_ROWS
            mine = pl.ds(pl.multiple_of(start + core * HALF_ROWS, HALF_ROWS), HALF_ROWS)
            other = pl.ds(pl.multiple_of(start + (1 - core) * HALF_ROWS, HALF_ROWS), HALF_ROWS)
            keep_ref[blk, 0] = dk_ref[mine, :] * SCORE_SCALE
            keep_ref[blk, 1] = dv_ref[mine, :]
            send_ref[blk, 0] = (dk_ref[other, :] * SCORE_SCALE).astype(bfloat)
            send_ref[blk, 1] = dv_ref[other, :].astype(bfloat)


def block_bounds(pos, begin):
    first, last = jnp.min(begin, axis=1), jnp.max(begin, axis=1)
    low = first // KEY_ROWS
    high = jnp.max(pos, axis=1) // KEY_ROWS + 1
    opened = jnp.clip((last + KEY_ROWS - 1) // KEY_ROWS, low, high)
    closed = jnp.clip((jnp.min(pos, axis=1) + 1) // KEY_ROWS, opened, high)
    return low, opened, closed, high


def block_spec(shape):
    return pl.BlockSpec((1,) + shape[1:], lambda i, *_: (i,) + (0,) * (len(shape) - 1))


def first_spec(shape):
    return pl.BlockSpec((1, 1) + shape[2:], lambda i, *_: (i,) + (0,) * (len(shape) - 1))


def whole_spec(shape):
    return pl.BlockSpec(shape, lambda *_: (0,) * len(shape), pipeline_mode=pl.Buffered(1))


def attention_forward(scalars, pos, begin, query, mine, other):
    blocks, _, rows = pos.shape
    keys = 2 * mine.shape[0] * HALF_ROWS
    out_shape = [
        jax.ShapeDtypeStruct((blocks, rows, HEAD_DIM), single),
        jax.ShapeDtypeStruct(pos.shape, single),
    ]
    return pl.pallas_call(
        forward_kernel,
        grid_spec=pltpu.PrefetchScalarGridSpec(
            num_scalar_prefetch=5,
            grid=(blocks,),
            in_specs=[
                block_spec(pos.shape), block_spec(pos.shape), first_spec(query.shape),
                whole_spec(mine.shape), whole_spec(other.shape),
            ],
            out_specs=[block_spec(out.shape) for out in out_shape],
            scratch_shapes=[pltpu.VMEM((keys, HEAD_DIM), bfloat), pltpu.VMEM((HEAD_DIM, keys), bfloat)],
        ),
        out_shape=out_shape,
        compiler_params=pltpu.CompilerParams(vmem_limit_bytes=48 << 20),
        cost_estimate=kernel_cost(22),
        name="attention_forward",
    )(*scalars, pos, begin, query, mine, other)


def attention_backward(scalars, pos, begin, lse, head_out, query, d_out, mine, other):
    blocks, _, rows = pos.shape
    keys = 2 * mine.shape[0] * HALF_ROWS
    pair = (mine.shape[0], 2, HALF_ROWS, HEAD_DIM)
    out_shape = [
        jax.ShapeDtypeStruct(d_out.shape, bfloat),
        jax.ShapeDtypeStruct(pair, single),
        jax.ShapeDtypeStruct(pair, bfloat),
    ]
    return pl.pallas_call(
        backward_kernel,
        grid_spec=pltpu.PrefetchScalarGridSpec(
            num_scalar_prefetch=5,
            grid=(blocks,),
            in_specs=[
                block_spec(pos.shape), block_spec(pos.shape), block_spec(pos.shape),
                block_spec(head_out.shape), first_spec(query.shape), block_spec(d_out.shape),
                whole_spec(mine.shape), whole_spec(other.shape),
            ],
            out_specs=[block_spec(d_out.shape), whole_spec(pair), whole_spec(pair)],
            scratch_shapes=[
                pltpu.VMEM((keys, HEAD_DIM), bfloat), pltpu.VMEM((keys, HEAD_DIM), bfloat),
                pltpu.VMEM((HEAD_DIM, keys), bfloat),
                pltpu.VMEM((keys, HEAD_DIM), single), pltpu.VMEM((keys, HEAD_DIM), single),
            ],
        ),
        out_shape=out_shape,
        compiler_params=pltpu.CompilerParams(vmem_limit_bytes=60 << 20),
        cost_estimate=kernel_cost(1),
        name="attention_backward",
    )(*scalars, pos, begin, lse, head_out, query, d_out, mine, other)


def turned(values, cosine, sine):
    return values * cosine + pltpu.roll(values, HEAD_DIM // 2, 1) * sine


def rotate_kernel(lin_ref, recip_ref, gain_ref, cosine_ref, sine_ref, out_ref):
    groups, rows = out_ref.shape[2], out_ref.shape[5]
    cosine, sine = cosine_ref[...], sine_ref[...]
    for which in range(3):
        for head in range(2):
            at = head * HEAD_DIM
            values = lin_ref[:, pl.ds((2 * which + head) * HEAD_DIM, HEAD_DIM)]
            if which < 2:
                values = values * recip_ref[:, which : which + 1]
                values = values * gain_ref[which : which + 1, at : at + HEAD_DIM]
                values = turned(values, cosine, sine)
            values = values.astype(bfloat)
            for group in range(groups):
                out_ref[0, head, group, 0, which] = values[group * rows : (group + 1) * rows]


def back_parts(d_ref, lin_ref, recip_ref, gain_ref, cosine, sine, which, head):
    at = head * HEAD_DIM
    grad = d_ref[0, head, :, 0, which].reshape(-1, HEAD_DIM).astype(single)
    grad = turned(grad, cosine, -sine)
    hat = lin_ref[:, pl.ds((2 * which + head) * HEAD_DIM, HEAD_DIM)] * recip_ref[:, which : which + 1]
    return grad, grad * gain_ref[which : which + 1, at : at + HEAD_DIM], hat


def sums_kernel(d_ref, lin_ref, recip_ref, gain_ref, cosine_ref, sine_ref, gain_out_ref, sum_ref):
    first = (pl.program_id(0) == 0) & (pl.program_id(1) == 0)

    @pl.when(first)
    def _():
        gain_out_ref[...] = jnp.zeros_like(gain_out_ref)

    cosine, sine = cosine_ref[...], sine_ref[...]
    for which in range(2):
        total = None
        for head in range(2):
            grad, scaled, hat = back_parts(
                d_ref, lin_ref, recip_ref, gain_ref, cosine, sine, which, head
            )
            at = pl.ds(head * HEAD_DIM, HEAD_DIM)
            gain_out_ref[which : which + 1, at] += jnp.sum(grad * hat, axis=0, keepdims=True)
            product = jnp.transpose(scaled * hat)
            product = jnp.sum(product, axis=0, keepdims=True)
            total = product if total is None else total + product
        sum_ref[0, 0, which : which + 1, :] = total


def lin_kernel(d_ref, lin_ref, recip_ref, mean_ref, gain_ref, cosine_ref, sine_ref, out_ref):
    cosine, sine = cosine_ref[...], sine_ref[...]
    for head in range(2):
        for which in range(2):
            _, scaled, hat = back_parts(
                d_ref, lin_ref, recip_ref, gain_ref, cosine, sine, which, head
            )
            grad = recip_ref[:, which : which + 1] * (scaled - hat * mean_ref[:, which : which + 1])
            out_ref[:, pl.ds((2 * which + head) * HEAD_DIM, HEAD_DIM)] = grad.astype(bfloat)
        out_ref[:, pl.ds((4 + head) * HEAD_DIM, HEAD_DIM)] = d_ref[0, head, :, 0, 2].reshape(
            -1, HEAD_DIM
        )


def token_spec(columns):
    return pl.BlockSpec((HALF_ROWS, columns), lambda near, half: (2 * near + half, 0))


def split_spec(groups, rows):
    return pl.BlockSpec(
        (1, 2, groups, 1, 3, rows, HEAD_DIM), lambda near, half: (half, 0, 0, near, 0, 0, 0)
    )


def project_kernel(rows_ref, weight_ref, lin_ref, sum_ref):
    part = weight_ref.shape[1] // 3
    lin = jnp.dot(rows_ref[...], weight_ref[...], preferred_element_type=single)
    lin_ref[...] = lin
    for which in range(2):
        values = lin[:, which * part : (which + 1) * part]
        sum_ref[0, 0, which : which + 1, :] = jnp.sum(
            jnp.transpose(values * values), axis=0, keepdims=True
        )


def projected(rows, weight):
    return pl.pallas_call(
        project_kernel,
        grid=(2, 2),
        in_specs=[token_spec(rows.shape[1]), whole_spec(weight.shape)],
        out_specs=[
            token_spec(weight.shape[1]),
            pl.BlockSpec((1, 1, 2, HALF_ROWS), lambda near, half: (near, half, 0, 0)),
        ],
        out_shape=[
            jax.ShapeDtypeStruct((rows.shape[0], weight.shape[1]), single),
            jax.ShapeDtypeStruct((2, 2, 2, HALF_ROWS), single),
        ],
        compiler_params=pltpu.CompilerParams(vmem_limit_bytes=32 << 20),
        cost_estimate=kernel_cost(5),
        name="projected",
    )(rows, weight)


def columns(values):
    return jnp.transpose(values, (0, 1, 3, 2)).reshape(-1, 2)


def rotated_heads(lin, recips, gains, cosine, sine, groups):
    rows = HALF_ROWS // groups
    return pl.pallas_call(
        rotate_kernel,
        grid=(2, 2),
        in_specs=[
            token_spec(lin.shape[1]), token_spec(2), whole_spec(gains.shape),
            token_spec(HEAD_DIM), token_spec(HEAD_DIM),
        ],
        out_specs=split_spec(groups, rows),
        out_shape=jax.ShapeDtypeStruct((2, 2, groups, 2, 3, rows, HEAD_DIM), bfloat),
        cost_estimate=kernel_cost(5),
        name="rotated_heads",
    )(lin, recips, gains, cosine, sine)


def rotated_sums(d_split, lin, recips, gains, cosine, sine):
    groups, rows = d_split.shape[2], d_split.shape[5]
    return pl.pallas_call(
        sums_kernel,
        grid=(2, 2),
        in_specs=[
            split_spec(groups, rows), token_spec(lin.shape[1]), token_spec(2),
            whole_spec(gains.shape), token_spec(HEAD_DIM), token_spec(HEAD_DIM),
        ],
        out_specs=[
            pl.BlockSpec(gains.shape, lambda near, half: (0, 0)),
            pl.BlockSpec((1, 1, 2, HALF_ROWS), lambda near, half: (near, half, 0, 0)),
        ],
        out_shape=[
            jax.ShapeDtypeStruct(gains.shape, single),
            jax.ShapeDtypeStruct((2, 2, 2, HALF_ROWS), single),
        ],
        cost_estimate=kernel_cost(5),
        name="rotated_sums",
    )(d_split, lin, recips, gains, cosine, sine)


def rotated_back(d_split, lin, recips, means, gains, cosine, sine):
    groups, rows = d_split.shape[2], d_split.shape[5]
    return pl.pallas_call(
        lin_kernel,
        grid=(2, 2),
        in_specs=[
            split_spec(groups, rows), token_spec(lin.shape[1]), token_spec(2), token_spec(2),
            whole_spec(gains.shape), token_spec(HEAD_DIM), token_spec(HEAD_DIM),
        ],
        out_specs=token_spec(lin.shape[1]),
        out_shape=jax.ShapeDtypeStruct(lin.shape, bfloat),
        cost_estimate=kernel_cost(5),
        name="rotated_back",
    )(d_split, lin, recips, means, gains, cosine, sine)


def unpack_kernel(in_ref, *out_refs):
    count, rows, width = in_ref.shape
    part = width // 3
    for which in range(3):
        for piece in range(count):
            out_refs[which][:, pl.ds(piece * part, part)] = in_ref[
                piece, :, pl.ds(which * part, part)
            ].astype(single)


def unpacked(values):
    count, rows, width = values.shape
    return pl.pallas_call(
        unpack_kernel,
        out_shape=[jax.ShapeDtypeStruct((rows, count * width // 3), single)] * 3,
        name="unpacked",
    )(values)


def dot_tn(a, b):
    return lax.dot_general(a, b, (((0,), (0,)), ((), ())), preferred_element_type=single)


def picks(slot_ref, source, expert, capacity):
    slots = slot_ref[source, pl.ds(expert, 1), :]
    rows = lax.broadcasted_iota(jnp.int32, (capacity, slots.shape[1]), 0) + 1
    return slots == rows.astype(single)


def spread_tokens(slot_ref, first, second, out_ref, capacity):
    for source in range(slot_ref.shape[0]):
        at = slice(source * capacity, (source + 1) * capacity)
        total = dot_tn(picks(slot_ref, source, 0, capacity).astype(bfloat), first[at])
        total += dot_tn(picks(slot_ref, source, 1, capacity).astype(bfloat), second[at])
        out_ref[source] = total.astype(bfloat)


def expert_kernel(
    blk_ref, slot_ref, ffn_ref, cot_ref, router_ref, gate_ref, up_ref, down_ref, gate_tile_ref,
    up_tile_ref, x_ref, c_ref, value_ref, hidden_ref, d_gate_ref, d_up_ref, probs_ref, out_ref,
    grad_ref, d_both_ref, first_ref,
):
    expert, step = pl.program_id(0), pl.program_id(1)
    sources = ffn_ref.shape[0]
    capacity = x_ref.shape[1] // sources
    part = gate_ref.shape[-1]
    tile = gate_tile_ref.shape[-2]

    @pl.when((expert == 0) & (step == 0))
    def _():
        for source in range(sources):
            logits = dot_nt(router_ref[...], ffn_ref[source])
            shifted = jnp.exp(logits - jnp.max(logits, axis=0, keepdims=True))
            probs_ref[source] = shifted / jnp.sum(shifted, axis=0, keepdims=True)

    def fill(which):
        for source in range(sources):
            at = pl.ds(source * capacity, capacity)
            picked = picks(slot_ref, source, which, capacity)
            picked_low = picked.astype(bfloat)
            x_ref[0, at, :] = jnp.dot(
                picked_low, ffn_ref[source], preferred_element_type=single
            ).astype(bfloat)
            cot_rows = jnp.dot(picked_low, cot_ref[source], preferred_element_type=single)
            c_ref[0, at, :] = cot_rows.astype(bfloat)
            probs = probs_ref[source, pl.ds(2 * blk_ref[0] + which, 1), :]
            value = jnp.sum(jnp.where(picked, probs, 0.0), axis=1, keepdims=True)
            value_ref[0, at, :] = value
            grad_ref[at, :] = (value * cot_rows).astype(bfloat)

    pl.when(step == 0)(lambda: fill(expert))

    @pl.when(step < 4)
    def _():
        w_both = jnp.concatenate([gate_ref[0, 0, 0], up_ref[0, 0, 0]], axis=1)
        both = jnp.dot(x_ref[0], w_both, preferred_element_type=single)
        gate_val, up_val = both[:, :part], both[:, part:]
        d_hidden = dot_nt(grad_ref[...], down_ref[0, 0])
        sigmoid = 1.0 / (1.0 + jnp.exp(-gate_val))
        silu = gate_val * sigmoid
        hidden_ref[0] = (silu * up_val).astype(bfloat)
        d_gate = (d_hidden * up_val * sigmoid * (1.0 + gate_val * (1.0 - sigmoid))).astype(bfloat)
        d_up = (d_hidden * silu).astype(bfloat)
        d_gate_ref[0] = d_gate
        d_up_ref[0] = d_up
        at = pl.multiple_of(2 * step * part, part)
        d_both_ref[:, pl.ds(at, part)] = d_gate
        d_both_ref[:, pl.ds(pl.multiple_of(at + part, part), part)] = d_up

    @pl.when(step >= 4)
    def _():
        weights = [ref[i, 0, 0] for i in range(4) for ref in (gate_tile_ref, up_tile_ref)]
        d_rows = dot_nt(d_both_ref[...], jnp.concatenate(weights, axis=1)).astype(bfloat)
        at = pl.ds(pl.multiple_of((step - 4) * tile, tile), tile)

        @pl.when(expert == 0)
        def _():
            first_ref[:, at] = d_rows

        @pl.when(expert == 1)
        def _():
            spread_tokens(slot_ref, first_ref[:, at], d_rows, out_ref, capacity)


def down_grads_kernel(c_ref, value_ref, hidden_ref, sent_ref, kept_ref, grad_ref):
    step = pl.program_id(1)

    @pl.when(step == 0)
    def _():
        grad_ref[...] = (value_ref[0] * c_ref[0].astype(single)).astype(bfloat)

    down = dot_tn(hidden_ref[0], grad_ref[...])

    @pl.when(step < 2)
    def _():
        sent_ref[0, 0] = down.astype(bfloat)

    @pl.when(step >= 2)
    def _():
        kept_ref[0, 0] = down


def grads_kernel(
    slot_ref, x_ref, c_ref, value_ref, hidden_ref, d_gate_ref, d_up_ref, down_tile_ref,
    gate_sent_ref, up_sent_ref, gate_kept_ref, up_kept_ref,
    d_probs_ref, out_ref, xt_ref, dots_ref, first_ref,
):
    expert, step = pl.program_id(0), pl.program_id(1)
    sources = slot_ref.shape[0]
    capacity = x_ref.shape[1] // sources
    part = d_gate_ref.shape[2]
    tile = down_tile_ref.shape[3]

    @pl.when(step == 0)
    def _():
        xt_ref[...] = jnp.transpose(x_ref[0])
        dots_ref[...] = jnp.zeros_like(dots_ref)

    @pl.when(step < 4)
    def _():
        d_both = jnp.concatenate([d_gate_ref[0], d_up_ref[0]], axis=1)
        both = jnp.dot(xt_ref[...], d_both, preferred_element_type=single)

        @pl.when(step < 2)
        def _():
            gate_sent_ref[0, 0] = both[:, :part].astype(bfloat)
            up_sent_ref[0, 0] = both[:, part:].astype(bfloat)

        @pl.when(step >= 2)
        def _():
            gate_kept_ref[0, 0] = both[:, :part]
            up_kept_ref[0, 0] = both[:, part:]

    @pl.when(step >= 4)
    def _():
        down = jnp.concatenate([down_tile_ref[i, 0] for i in range(4)], axis=0)
        expert_out = jnp.dot(hidden_ref[0], down, preferred_element_type=single)
        expert_out = expert_out.astype(bfloat).astype(single)
        at = pl.ds(pl.multiple_of((step - 4) * tile, tile), tile)
        dots_ref[...] += jnp.sum(
            c_ref[0, :, at].astype(single) * expert_out, axis=1, keepdims=True
        )
        weighted = (value_ref[0] * expert_out).astype(bfloat)

        @pl.when(expert == 0)
        def _():
            first_ref[:, at] = weighted

        @pl.when(expert == 1)
        def _():
            spread_tokens(slot_ref, first_ref[:, at], weighted, out_ref, capacity)

    @pl.when(step == 7)
    def _():
        for source in range(sources):
            picked = picks(slot_ref, source, expert, capacity)
            row = dots_ref[source * capacity : (source + 1) * capacity]
            d_probs_ref[source, pl.ds(expert, 1), :] = jnp.sum(
                jnp.where(picked, row, 0.0), axis=0, keepdims=True
            )


def rows_spec(rows, columns):
    return pl.BlockSpec((1, rows, columns), lambda e, k, *_: (e, 0, 0))


def first_half(k):
    return jnp.minimum(k, 3)


def second_half(k):
    return jnp.maximum(k - 4, 0)


def part_spec(rows, columns):
    return pl.BlockSpec((1, rows, columns), lambda e, k, *_: (e, 0, first_half(k)))


def weight_spec(shape, place=first_half):
    return pl.BlockSpec((1, 1) + shape[2:], lambda e, k, *_: (place(k), e, 0, 0))


def token_tile_spec(shape):
    block = shape[:2] + (shape[2] // 4,)
    return pl.BlockSpec(block, lambda e, k, *_: (0, 0, e * second_half(k)))


def pair_spec(shape, which):
    return pl.BlockSpec(
        (1, 1, 1) + shape[3:], lambda e, k, *_: (first_half(k), which, e, 0, 0)
    )


def pair_tile_spec(shape, which):
    return pl.BlockSpec(
        (4, 1, 1, shape[3] // 4, shape[4]), lambda e, k, *_: (0, which, e, second_half(k), 0)
    )


def expert_rows(blk, slot_map, ffn_all, cot_all, router_t, pair, down, capacity):
    sources, tokens, width = ffn_all.shape
    rows, experts, hidden = sources * capacity, router_t.shape[0], 4 * down.shape[2]
    wide = jax.ShapeDtypeStruct((2, rows, width), bfloat)
    narrow = jax.ShapeDtypeStruct((2, rows, hidden), bfloat)
    probs = jax.ShapeDtypeStruct((sources, experts, tokens), single)
    return pl.pallas_call(
        expert_kernel,
        grid_spec=pltpu.PrefetchScalarGridSpec(
            num_scalar_prefetch=1,
            grid=(2, 8),
            in_specs=[
                whole_spec(slot_map.shape), whole_spec(ffn_all.shape), whole_spec(cot_all.shape),
                whole_spec(router_t.shape), pair_spec(pair.shape, 0), pair_spec(pair.shape, 1),
                weight_spec(down.shape), pair_tile_spec(pair.shape, 0), pair_tile_spec(pair.shape, 1),
            ],
            out_specs=[
                rows_spec(rows, width), rows_spec(rows, width), rows_spec(rows, 1),
                part_spec(rows, hidden // 4), part_spec(rows, hidden // 4),
                part_spec(rows, hidden // 4), whole_spec(probs.shape), token_tile_spec(ffn_all.shape),
            ],
            scratch_shapes=[
                pltpu.VMEM((rows, width), bfloat), pltpu.VMEM((rows, 2 * hidden), bfloat),
                pltpu.VMEM((rows, width), bfloat),
            ],
        ),
        out_shape=[
            wide, wide, jax.ShapeDtypeStruct((2, rows, 1), single), narrow, narrow, narrow,
            probs, jax.ShapeDtypeStruct(ffn_all.shape, bfloat),
        ],
        compiler_params=pltpu.CompilerParams(vmem_limit_bytes=60 << 20),
        cost_estimate=kernel_cost(55),
        name="expert_rows",
    )(blk[None], slot_map, ffn_all, cot_all, router_t, pair, pair, down, pair, pair)


def sent_place(k):
    return jnp.minimum(k, 1)


def kept_place(k):
    return jnp.clip(k - 2, 0, 1)


def expert_down_grads(c, value, hidden):
    rows, width = c.shape[1:]
    part = hidden.shape[2] // 4
    shape = (2, 2, part, width)
    return pl.pallas_call(
        down_grads_kernel,
        grid=(2, 4),
        in_specs=[rows_spec(rows, width), rows_spec(rows, 1), part_spec(rows, part)],
        out_specs=[weight_spec(shape, sent_place), weight_spec(shape, kept_place)],
        out_shape=[jax.ShapeDtypeStruct(shape, bfloat), jax.ShapeDtypeStruct(shape, single)],
        scratch_shapes=[pltpu.VMEM((rows, width), bfloat)],
        compiler_params=pltpu.CompilerParams(vmem_limit_bytes=40 << 20),
        cost_estimate=kernel_cost(12),
        name="expert_down_grads",
    )(c, value, hidden)


def expert_grads(slot_map, x, c, value, hidden, d_gate, d_up, down, tokens):
    rows, width = x.shape[1:]
    part = down.shape[2]
    wide = (2, 2, width, part)
    summed = (slot_map.shape[0], tokens, width)
    return pl.pallas_call(
        grads_kernel,
        grid=(2, 8),
        in_specs=[
            whole_spec(slot_map.shape), rows_spec(rows, width), rows_spec(rows, width),
            rows_spec(rows, 1), rows_spec(rows, 4 * part), part_spec(rows, part),
            part_spec(rows, part),
            pl.BlockSpec((4, 1, part, width // 4), lambda e, k: (0, e, 0, second_half(k))),
        ],
        out_specs=[weight_spec(wide, sent_place)] * 2
        + [weight_spec(wide, kept_place)] * 2
        + [whole_spec(slot_map.shape), token_tile_spec(summed)],
        out_shape=[jax.ShapeDtypeStruct(wide, bfloat)] * 2
        + [jax.ShapeDtypeStruct(wide, single)] * 2
        + [
            jax.ShapeDtypeStruct(slot_map.shape, single),
            jax.ShapeDtypeStruct(summed, bfloat),
        ],
        scratch_shapes=[
            pltpu.VMEM((width, rows), bfloat), pltpu.VMEM((rows, 1), single),
            pltpu.VMEM((rows, width), bfloat),
        ],
        compiler_params=pltpu.CompilerParams(vmem_limit_bytes=60 << 20),
        cost_estimate=kernel_cost(39),
        name="expert_grads",
    )(slot_map, x, c, value, hidden, d_gate, d_up, down)


def plain_experts(blk, slot_map, ffn_all, cot_all, router_t, pair, down, capacity):
    sources, tokens, width = ffn_all.shape
    count = slot_map.shape[1]

    def joined(weights, axis):
        return jnp.concatenate([weights[i] for i in range(4)], axis=axis)

    gate, up, down = joined(pair[:, 0], 2), joined(pair[:, 1], 2), joined(down, 1)
    slot_at = jnp.arange(1, capacity + 1, dtype=jnp.int32).astype(single)
    picked = jnp.transpose(slot_map, (1, 0, 2))[:, :, None, :] == slot_at[None, None, :, None]
    picked_low = picked.astype(bfloat)
    logits = jnp.einsum("ed,std->set", router_t, ffn_all, preferred_element_type=single)
    shifted = jnp.exp(logits - jnp.max(logits, axis=1, keepdims=True))
    probs = shifted / jnp.sum(shifted, axis=1, keepdims=True)
    local = jnp.transpose(lax.dynamic_slice_in_dim(probs, blk * count, count, 1), (1, 0, 2))
    value = jnp.sum(jnp.where(picked, local[:, :, None, :], 0.0), axis=3).reshape(count, -1, 1)

    def dispatch(rows):
        rows = jnp.einsum("esct,std->escd", picked_low, rows, preferred_element_type=single)
        return rows.astype(bfloat).reshape(count, -1, width)

    def combine(rows):
        rows = rows.astype(bfloat).reshape(count, sources, capacity, width)
        total = jnp.einsum("esct,escd->std", picked_low, rows, preferred_element_type=single)
        return total.astype(bfloat)

    def dots(spec, *arrays):
        return jnp.einsum(spec, *arrays, preferred_element_type=single)

    x, c = dispatch(ffn_all), dispatch(cot_all).astype(single)
    grad = (value * c).astype(bfloat)
    gate_val, up_val = dots("erd,edf->erf", x, gate), dots("erd,edf->erf", x, up)
    sigmoid = jax.nn.sigmoid(gate_val)
    hidden = (gate_val * sigmoid * up_val).astype(bfloat)
    d_hidden = dots("erd,efd->erf", grad, down)
    d_gate = (d_hidden * up_val * sigmoid * (1.0 + gate_val * (1.0 - sigmoid))).astype(bfloat)
    d_up = (d_hidden * gate_val * sigmoid).astype(bfloat)
    d_part = combine(dots("erf,edf->erd", d_gate, gate) + dots("erf,edf->erd", d_up, up))
    expert_out = dots("erf,efd->erd", hidden, down).astype(bfloat).astype(single)
    d_value = jnp.sum(c * expert_out, axis=2).reshape(count, sources, capacity, 1)
    d_probs = jnp.transpose(jnp.sum(jnp.where(picked, d_value, 0.0), axis=2), (1, 0, 2))
    mixed_part = combine(value * expert_out)

    def cut(total, axis):
        parts = jnp.stack(jnp.split(total, 4, axis=axis))
        return parts[:2].astype(bfloat), parts[2:]

    gate_sent, gate_kept = cut(dots("erd,erf->edf", x, d_gate), 2)
    up_sent, up_kept = cut(dots("erd,erf->edf", x, d_up), 2)
    down_sent, down_kept = cut(dots("erf,erd->efd", hidden, grad), 1)
    return probs, d_part, (down_sent, down_kept), (
        gate_sent, up_sent, gate_kept, up_kept, d_probs, mixed_part
    )


def per_device(
    block_input, w_query, w_key, w_value, w_out, attn_gain, ffn_gain, query_gain, key_gain,
    router, w_gate, w_up, w_down, expert_ids, slot_ids, doc_starts, cotangent,
):
    ulysses_size = lax.axis_size("ulysses")
    blk_size = lax.axis_size(BLK)
    blk = lax.axis_index(BLK)
    uly = lax.axis_index("ulysses")
    core = uly % 2
    own_tokens, width = block_input.shape
    picks = expert_ids.shape[1]
    experts = router.shape[1]
    capacity = 5 * own_tokens * picks // (4 * experts)
    local_experts = experts // blk_size
    blk_tokens = ulysses_size * own_tokens
    far_size = blk_size // 2
    far_tokens = 2 * blk_tokens
    plane_size = 2 * ulysses_size
    local_width = width // ulysses_size
    plane_width = width // plane_size
    weight_rows = w_query.shape[0]
    groups = blk_size // 8
    plane = 2 * uly + blk % 2

    projections = jnp.concatenate(
        [
            weight.astype(bfloat).reshape(weight_rows, plane_size, plane_width)
            for weight in (w_query, w_key, w_value)
        ],
        axis=2,
    )
    projections = lax.all_to_all(
        jnp.transpose(projections, (1, 0, 2)), PLANE, split_axis=0, concat_axis=0, tiled=True
    )
    projections = projections.reshape(ulysses_size, 2 * weight_rows, 3 * plane_width)
    small = jnp.concatenate(
        [jnp.stack([attn_gain, ffn_gain, query_gain, key_gain]), router.T]
    ).astype(bfloat)
    projections, small = tie(projections, gather_ulysses(small))
    w_qkv = gather_line(projections, 1).reshape(width, 3 * plane_width)
    small = gather_blk_small(small)
    gate_mine, up_mine, down_mine = w_gate.astype(bfloat), w_up.astype(bfloat), w_down.astype(bfloat)
    plane_input = gather_plane(block_input).reshape(far_tokens, width)
    pair_mine = jnp.stack([gate_mine, up_mine])
    pair_beyond = swap(pair_mine, 2)
    attn_g = small[0].astype(single)
    ffn_g = small[1].astype(single)
    plane_gains = lax.dynamic_slice_in_dim(
        small[2:4], plane * plane_width, plane_width, 1
    ).astype(single)
    router_t = small[4:]

    inputs = block_input.astype(single)
    hat_one, recip_one = norm_parts(inputs)
    normed = (norm_parts(plane_input.astype(single))[0] * attn_g).astype(bfloat)
    lin, squares = projected(normed, w_qkv)
    w_o = lax.all_gather(w_out.astype(bfloat), BLK, axis=0, tiled=True)
    named = expert_ids[:, :, None] == jnp.arange(experts, dtype=jnp.int32)[None, None, :]
    slot_map = jnp.sum(jnp.where(named, slot_ids[:, :, None] + 1, 0), axis=1)
    slot_map = slot_map.T.astype(single).reshape(blk_size, local_experts, own_tokens)
    squares, pair_beyond, w_o = tie(squares, pair_beyond, w_o)
    squares, down_mine = tie(sum_plane(squares), down_mine)
    down_beyond = swap(down_mine, 2)
    recips = columns(lax.rsqrt(squares / width + NORM_EPSILON))
    far_at = blk // 2 * far_tokens + jnp.arange(far_tokens, dtype=jnp.int32)
    cosine, sine = angles(far_at - doc_begins(doc_starts, far_at), HEAD_DIM)
    split = rotated_heads(lin, recips, plane_gains, cosine, sine, groups)
    heads_in = line_to_heads(split, far_size)
    heads_in, cotangent_sent, slot_map = tie(heads_in, cotangent, slot_map)
    slot_map = lax.all_to_all(slot_map, BLK, split_axis=0, concat_axis=0, tiled=True)
    cot_all = lax.all_gather(cotangent_sent, BLK, axis=0)
    part_rows = heads_in.shape[2]
    if groups == 1:
        query, mine = heads_in, heads_in
    else:
        query = heads_in[:, 0].reshape(-1, 1, QUERY_ROWS, HEAD_DIM)
        mine = lax.all_gather(
            heads_in[:, 1:], "far", axis=2, axis_index_groups=head_groups(far_size, groups)
        ).reshape(blk_size, 2, HALF_ROWS, HEAD_DIM)
    other, pair_mine, pair_beyond, down_mine = tie(
        swap(mine[:, -2:], 1), pair_mine, pair_beyond, down_mine
    )
    pair_near, pair_far, down_near = swap(pair_mine, 1), swap(pair_beyond, 1), swap(down_mine, 1)
    query_at = (
        jnp.arange(blk_size, dtype=jnp.int32)[:, None] * blk_tokens
        + core * HALF_ROWS
        + blk // 2 % groups * part_rows
        + jnp.arange(part_rows, dtype=jnp.int32)[None, :]
    ).reshape(-1, QUERY_ROWS)
    query_begin = doc_begins(doc_starts, query_at)
    scalars = (core[None],) + block_bounds(query_at, query_begin)
    query_at, query_begin = query_at[:, None], query_begin[:, None]
    head_out, lse = attention_forward(scalars, query_at, query_begin, query, mine, other)
    attended = blk_from_heads(
        head_out.astype(bfloat).reshape(blk_size, part_rows, HEAD_DIM), blk_size
    )
    attended, down_beyond, pair_near, pair_far, down_near = tie(
        attended, down_beyond, pair_near, pair_far, down_near
    )
    down_far = swap(down_beyond, 1)
    out_part = jnp.dot(attended, w_o, preferred_element_type=single)

    def token_rows(values):
        return lambda bits: lax.dynamic_slice_in_dim(
            values, (uly ^ bits) * own_tokens, own_tokens, 0
        )

    residual_mid = inputs + scatter_sum_ulysses(token_rows(out_part))
    hat_two, recip_two = norm_parts(residual_mid)
    ffn_in = (hat_two * ffn_g).astype(bfloat)

    ffn_in, pair_near, pair_far, pair_mine, pair_beyond = tie(
        ffn_in, pair_near, pair_far, pair_mine, pair_beyond
    )
    ffn_all = lax.all_gather(ffn_in, BLK, axis=0)
    expert_pair = jnp.stack([pair_near, pair_far, pair_mine, pair_beyond])
    expert_down = jnp.stack([down_near, down_far, down_mine, down_beyond])
    if capacity % 16 == 0:
        *kept_rows, probs_all, d_part = expert_rows(
            blk, slot_map, ffn_all, cot_all, router_t, expert_pair, expert_down, capacity
        )
        *kept_rows, d_part = tie(*kept_rows, d_part)
        x, c, value, hidden, d_gate, d_up = kept_rows
        down_results = expert_down_grads(c, value, hidden)
        x, *down_results = tie(x, *down_results)
        results = expert_grads(
            slot_map, x, c, value, hidden, d_gate, d_up, expert_down, own_tokens
        )
    else:
        probs_all, d_part, down_results, results = plain_experts(
            blk, slot_map, ffn_all, cot_all, router_t, expert_pair, expert_down, capacity
        )
    d_ffn_in = lax.psum_scatter(d_part, BLK, scatter_dimension=0).astype(single)
    down_sent, down_kept = down_results
    gate_sent, up_sent, gate_kept, up_kept, d_probs, mixed_part = results

    d_probs = lax.all_to_all(d_probs, BLK, split_axis=0, concat_axis=0, tiled=True)
    d_probs = d_probs.reshape(experts, own_tokens)
    gate_sent, up_sent, down_got = tie(gate_sent, up_sent, swap(down_sent, 1))
    gate_got, up_got = swap(gate_sent, 1), swap(up_sent, 1)

    def onward(got, kept):
        return (kept[1] + got[1].astype(single)).astype(bfloat)

    down_sent = onward(down_got, down_kept)
    gate_sent = onward(gate_got, gate_kept)
    summed = lax.dynamic_update_slice(
        jnp.zeros((blk_size, weight_rows + own_tokens, width), bfloat), mixed_part, (0, weight_rows, 0)
    )
    d_ffn_in, summed, up_got, gate_sent = tie(d_ffn_in, summed, up_got, gate_sent)

    router_probs = lax.dynamic_index_in_dim(probs_all, blk, 0, keepdims=False)
    d_logits = (
        router_probs * (d_probs - jnp.sum(router_probs * d_probs, axis=0, keepdims=True))
    ).astype(bfloat)
    grad_router_part = jnp.dot(d_logits, ffn_in, preferred_element_type=single)
    d_ffn_in = d_ffn_in + dot_tn(d_logits, router_t)
    grad_ffn_part = jnp.sum(d_ffn_in * hat_two, axis=0)
    d_mid = cotangent.astype(single) + norm_back(d_ffn_in * ffn_g, hat_two, recip_two)

    d_attn_out = gather_ulysses(d_mid.astype(bfloat)).reshape(blk_tokens, width)
    narrow = scatter_sum_ulysses(
        lambda bits: lax.dynamic_slice_in_dim(
            jnp.concatenate([grad_ffn_part[None], grad_router_part]),
            (uly ^ bits) * local_width, local_width, 1,
        ),
        single,
    )
    d_attn_out, gate_sent, narrow = tie(d_attn_out, gate_sent, narrow)
    gate_across = swap(gate_sent, 2)
    d_attended = dot_nt(d_attn_out, w_o).astype(bfloat)
    grad_out_part = jnp.einsum("ti,to->io", attended, d_attn_out, preferred_element_type=single)
    grad_out_part = grad_out_part.astype(bfloat).reshape(blk_size, weight_rows, width)
    d_halves, up_got = tie(blk_halves(d_attended, blk_size), up_got)
    up_sent = onward(up_got, up_kept)
    d_out = lax.all_to_all(d_halves, BLK, split_axis=0, concat_axis=0, tiled=True)
    d_out = d_out.reshape(head_out.shape)
    d_out, grad_out_part, up_sent = tie(d_out, grad_out_part, up_sent)
    up_across = swap(up_sent, 2)
    summed = lax.dynamic_update_slice(summed, grad_out_part, (0, 0, 0))
    summed = lax.psum_scatter(summed, BLK, scatter_dimension=0)
    dq_head, keep, send = attention_backward(
        scalars, query_at, query_begin, lse, head_out, query, d_out, mine, other
    )
    d_keys = (keep + swap(send, 1).astype(single)).astype(bfloat)
    if groups > 1:
        moved = jnp.moveaxis(d_keys.reshape(blk_size, 2, groups, part_rows, HEAD_DIM), 2, 0)
        moved = lax.psum_scatter(
            moved, "far", scatter_dimension=0, axis_index_groups=head_groups(far_size, groups)
        )
        d_keys = moved
    d_keys, gate_across = tie(d_keys, gate_across)
    d_stack = jnp.concatenate(
        [dq_head.reshape(blk_size, 1, part_rows, HEAD_DIM), d_keys], axis=1
    )
    d_split = line_from_heads(d_stack, far_size)
    d_split, up_across = tie(d_split, up_across)
    gain_parts, means = rotated_sums(d_split, lin, recips, plane_gains, cosine, sine)
    means, first_down = tie(sum_plane(means), down_sent[0])
    first_down = swap(first_down, 2)
    means = columns(means / width)
    d_lin = rotated_back(d_split, lin, recips, means, plane_gains, cosine, sine)
    grads = jnp.einsum("td,to->do", normed, d_lin, preferred_element_type=single)
    grads = grads.astype(bfloat).reshape(ulysses_size, far_size, 2 * weight_rows, 3 * plane_width)
    grads = jnp.transpose(grads, (1, 0, 2, 3)).reshape(-1, 3 * plane_width)
    grads, d_lin, summed = tie(grads, d_lin, summed)
    grads = lax.psum_scatter(grads, "far", scatter_dimension=0, tiled=True)
    d_normed_part = dot_nt(d_lin, w_qkv)
    grad_attn_part = jnp.sum(d_normed_part * norm_parts(plane_input.astype(single))[0], axis=0)
    d_normed_part = d_normed_part.reshape(2, blk_tokens, width)
    side = blk % 2

    def near_rows(bits):
        mine, other = (
            lax.dynamic_slice(
                d_normed_part, (place, (uly ^ bits) * own_tokens, 0), (1, own_tokens, width)
            )[0]
            for place in (side, 1 - side)
        )
        return mine, other


    def whole_sum(kept, got, across):
        return kept[0] + got[0].astype(single) + across.astype(single)

    grad_w_gate = whole_sum(gate_kept, gate_got, gate_across)
    grad_w_up = whole_sum(up_kept, up_got, up_across)
    d_normed, beside = scatter_sum_plane(
        near_rows,
        (grad_w_gate, grad_w_up, grad_attn_part, summed, first_down, down_sent[1]),
    )
    grad_w_gate, grad_w_up, grad_attn_part, summed, first_down, second_down = beside
    d_normed, second_down = tie(d_normed, swap(second_down, 2))
    down_across = jnp.stack([first_down, second_down])
    grad_w_out = summed[:weight_rows].astype(single)
    mixed = (residual_mid + summed[weight_rows:].astype(single)).astype(bfloat)
    grad_w_down = whole_sum(down_kept, down_got, down_across)
    input_grad = d_mid + norm_back(d_normed * attn_g, hat_one, recip_one)

    def own_columns(values):
        return scatter_sum_ulysses(
            lambda bits: lax.dynamic_slice_in_dim(values, (uly ^ bits) * local_width, local_width, 1),
            single,
        )

    gain_parts = lax.dynamic_update_slice_in_dim(
        jnp.zeros((2, local_width), single), gain_parts, side * plane_width, 1
    )
    last = own_columns(grad_attn_part[None])
    gains = scatter_sum_blk_small(jnp.concatenate([last, narrow, gain_parts]))
    grads = grads.reshape(plane_size, weight_rows, 3 * plane_width)
    grads = lax.all_to_all(grads, PLANE, split_axis=0, concat_axis=0, tiled=True)
    grads = unpacked(grads)
    return (
        mixed,
        input_grad.astype(bfloat),
        grads[0],
        grads[1],
        grads[2],
        grad_w_out,
        gains[0],
        gains[1],
        gains[-2],
        gains[-1],
        gains[2:-2].T,
        grad_w_gate,
        grad_w_up,
        grad_w_down,
    )


def solution(mesh):
    in_specs = (
        P(("far", "near", "ulysses"), None),
        P(("ulysses", "far", "near"), None),
        P(("ulysses", "far", "near"), None),
        P(("ulysses", "far", "near"), None),
        P(("ulysses", "far", "near"), None),
        P(("ulysses", "far", "near")),
        P(("ulysses", "far", "near")),
        P(("ulysses", "far", "near")),
        P(("ulysses", "far", "near")),
        P(("ulysses", "far", "near"), None),
        P(BLK, None, "ulysses"),
        P(BLK, None, "ulysses"),
        P(BLK, "ulysses", None),
        P(("far", "near", "ulysses"), None),
        P(("far", "near", "ulysses"), None),
        P(),
        P(("far", "near", "ulysses"), None),
    )
    out_specs = (
        P(("far", "near", "ulysses"), None),
        P(("far", "near", "ulysses"), None),
        P(("ulysses", "far", "near"), None),
        P(("ulysses", "far", "near"), None),
        P(("ulysses", "far", "near"), None),
        P(("ulysses", "far", "near"), None),
        P(("ulysses", "far", "near")),
        P(("ulysses", "far", "near")),
        P(("ulysses", "far", "near")),
        P(("ulysses", "far", "near")),
        P(("ulysses", "far", "near"), None),
        P(BLK, None, "ulysses"),
        P(BLK, None, "ulysses"),
        P(BLK, "ulysses", None),
    )
    ulysses_size, blk_size = mesh.devices.shape
    shape = (ulysses_size, blk_size // 2, 2)
    split_mesh = jax.sharding.Mesh(mesh.devices.reshape(shape), ("ulysses", "far", "near"))
    return jax.shard_map(
        per_device, mesh=split_mesh, in_specs=in_specs, out_specs=out_specs, check_vma=False
    )
```

```python
import math

import jax
import jax.numpy as jnp
from jax import lax
from jax.experimental import pallas as pl
from jax.experimental.pallas import tpu as pltpu
from jax.sharding import PartitionSpec as P

HEAD_DIM = 128
NORM_EPSILON = 1e-05
ROPE_BASE = 10000.0
MASKED_SCORE = -1e30
SCORE_SCALE = HEAD_DIM ** (-0.5)
LOG2_SCALE = SCORE_SCALE * math.log2(math.e)
QUERY_ROWS = 256
HALF_ROWS = 256
KEY_ROWS = 512
BLK = ("far", "near")
PLANE = ("ulysses", "near")
bfloat = jnp.bfloat16
single = jnp.float32


def norm_parts(values):
    recip_factor = lax.rsqrt(jnp.mean(values * values, axis=-1, keepdims=True) + NORM_EPSILON)
    return (values * recip_factor, recip_factor)


def norm_back(grad_in, hat_values, recip_factor):
    return recip_factor * (
        grad_in - hat_values * jnp.mean(grad_in * hat_values, axis=-1, keepdims=True)
    )


def doc_begins(doc_starts, tokens_at):
    at_or_before = doc_starts[:, None] <= tokens_at.reshape(1, -1)
    begins = jnp.max(jnp.where(at_or_before, doc_starts[:, None], 0), axis=0)
    return begins.reshape(tokens_at.shape)


def angles(position, head_size):
    half_size = head_size // 2
    frequency = ROPE_BASE ** (-(jnp.arange(half_size, dtype=jnp.float32) * 2.0 / head_size))
    turn = position.astype(jnp.float32)[:, None] * frequency[None, :]
    cosine, sine = jnp.cos(turn), jnp.sin(turn)
    return jnp.concatenate([cosine, cosine], 1), jnp.concatenate([-sine, sine], 1)


def swap(values, bit, axis="ulysses"):
    size = lax.axis_size(axis)
    return lax.ppermute(values, axis, [(i, i ^ bit) for i in range(size)])


def gather_plane(values):
    me, side = lax.axis_index("ulysses"), lax.axis_index("near")
    near = swap(values, 1, "near")
    beyond = swap(values, 2)
    corner = swap(beyond, 1, "near")
    out = jnp.zeros((2, 4) + values.shape, values.dtype)
    for other, bit, part in ((0, 0, values), (0, 2, beyond), (1, 0, near), (1, 2, corner)):
        for core, piece in ((0, part), (1, swap(part, 1))):
            place = (side ^ other, me ^ bit ^ core) + (0,) * values.ndim
            out = lax.dynamic_update_slice(out, piece[None, None], place)
    return out


def line_steps(size):
    for step in range(1, size):
        up = [(i, i + 1) for i in range(step - 1, size - 1)]
        yield up, [(size - 1 - i, size - 1 - j) for i, j in up]


def gather_line(values, axis):
    size = lax.axis_size("far")
    if size > 4:
        return lax.all_gather(values, "far", axis=axis)
    at = lax.axis_index("far")
    below, above, parts = values, values, []
    for step, (up, down) in enumerate(line_steps(size), 1):
        below, above = lax.ppermute(below, "far", up), lax.ppermute(above, "far", down)
        parts = [(at - step, below), (at + step, above)] + parts
    shape = values.shape[:axis] + (size,) + values.shape[axis:]
    out = jnp.zeros(shape, values.dtype)
    for place, part in parts + [(at, values)]:
        out = lax.dynamic_update_index_in_dim(out, part, jnp.clip(place, 0, size - 1), axis)
    return out


def gather_ulysses(values):
    me = lax.axis_index("ulysses")
    beyond = swap(values, 2)
    core = swap(values, 1)
    beyond_core = swap(beyond, 1)
    out = jnp.zeros((4,) + values.shape, values.dtype)
    for bit, part in enumerate((values, core, beyond, beyond_core)):
        out = lax.dynamic_update_index_in_dim(out, part, me ^ bit, 0)
    return out


def scatter_sum_ulysses(parts, kind=bfloat):
    far = swap(parts(3).astype(kind), 1)
    near = swap(parts(1).astype(kind), 1)
    across = swap((parts(2) + far.astype(single)).astype(kind), 2)
    return parts(0) + near.astype(single) + across.astype(single)


def scatter_sum_plane(parts, beside):
    kept, sent = [], []
    for bits in (0, 2):
        mine, other = parts(bits)
        core_mine, core_other = parts(bits ^ 1)
        got = swap(jnp.stack([core_mine, core_other]).astype(bfloat), 1).astype(single)
        kept.append(mine + got[0])
        sent.append(other + got[1])
    got = swap(jnp.stack(sent).astype(bfloat), 1, "near")
    got, beside = tie(got, beside)
    got = got.astype(single)
    across = swap((kept[1] + got[1]).astype(bfloat), 2)
    return kept[0] + got[0] + across.astype(single), beside


def gather_blk_small(values):
    ulysses_size, count, size = values.shape
    blk_size = lax.axis_size(BLK)
    mine = jnp.transpose(values, (1, 0, 2)).reshape(count, -1)
    out = lax.all_to_all(
        jnp.broadcast_to(mine, (blk_size,) + mine.shape), BLK, split_axis=0, concat_axis=0, tiled=True
    )
    out = out.reshape(blk_size, count, ulysses_size, size)
    return jnp.transpose(out, (1, 2, 0, 3)).reshape(count, -1)


def scatter_sum_blk_small(values):
    count, blk_size = values.shape[0], lax.axis_size(BLK)
    parts = jnp.transpose(values.reshape(count, blk_size, -1), (1, 0, 2))
    parts = lax.all_to_all(parts, BLK, split_axis=0, concat_axis=0, tiled=True)
    return jnp.sum(parts, axis=0)


def tie(*values):
    return lax.optimization_barrier(values)


def sum_plane(values):
    values = values + swap(values, 1)
    values = values + swap(values, 2)
    return values + swap(values, 1, "near")


def swap_halves(values, core):
    got = swap(lax.dynamic_index_in_dim(values, 1 - core, 0, keepdims=False), 1)
    return lax.dynamic_update_index_in_dim(values, got, 1 - core, 0)


def line_to_heads(split, far_size):
    count, rows = split.shape[4:6]
    both = swap_halves(split, lax.axis_index("ulysses") % 2)
    both = both.reshape(far_size, 2, count, rows, HEAD_DIM)
    both = lax.all_to_all(both, "far", split_axis=0, concat_axis=0, tiled=True)
    return both.reshape(2 * far_size, count, rows, HEAD_DIM)


def line_from_heads(stacked, far_size):
    count, rows = stacked.shape[1:3]
    back = stacked.reshape(far_size, 2, count, rows, HEAD_DIM)
    back = lax.all_to_all(back, "far", split_axis=0, concat_axis=0, tiled=True)
    back = back.reshape(2, 2, far_size // 4, 2, count, rows, HEAD_DIM)
    return swap_halves(back, lax.axis_index("ulysses") % 2)


def blk_halves(values, blk_size):
    core = lax.axis_index("ulysses") % 2
    groups = blk_size // 8
    rows = values.shape[0] // (2 * groups)
    split = values.reshape(2, groups, rows, 2, 2, HEAD_DIM)
    split = jnp.transpose(split, (0, 4, 1, 3, 2, 5))
    return swap_halves(split, core).reshape(blk_size, rows, HEAD_DIM)


def blk_from_heads(stacked, blk_size):
    core = lax.axis_index("ulysses") % 2
    groups, rows = blk_size // 8, stacked.shape[1]
    back = lax.all_to_all(stacked, BLK, split_axis=0, concat_axis=0, tiled=True)
    whole = swap_halves(back.reshape(2, 2, groups, 2, rows, HEAD_DIM), core)
    whole = jnp.transpose(whole, (0, 2, 4, 3, 1, 5))
    return whole.reshape(2 * groups * rows, 4 * HEAD_DIM)


def head_groups(far_size, groups):
    return [[j * groups + p for p in range(groups)] for j in range(far_size // groups)]


def kernel_cost(micros):
    return pl.CostEstimate(flops=micros * 10**9, bytes_accessed=0, transcendentals=0)


def dot_nt(a, b):
    return lax.dot_general(a, b, (((1,), (1,)), ((), ())), preferred_element_type=single)


def key_loops(low_ref, open_ref, close_ref, high_ref, index, step, carry):
    low, opened = low_ref[index], open_ref[index]
    closed, high = close_ref[index], high_ref[index]
    pairs = (closed - opened) // 2
    paired = opened + 2 * pairs

    def two(pair, carry):
        return step(opened + 2 * pair, carry, False, 2 * KEY_ROWS)

    carry = lax.fori_loop(low, opened, lambda kb, c: step(kb, c, True, KEY_ROWS), carry)
    carry = lax.fori_loop(0, pairs, two, carry)
    carry = lax.fori_loop(paired, closed, lambda kb, c: step(kb, c, False, KEY_ROWS), carry)
    return lax.fori_loop(closed, high, lambda kb, c: step(kb, c, True, KEY_ROWS), carry)


def allowed(start, pos, begin):
    key_at = start + lax.broadcasted_iota(jnp.int32, (KEY_ROWS, pos.shape[1]), 0)
    return (key_at <= pos) & (key_at >= begin)


def load_keys(core, mine_ref, other_ref, at, store):
    for blk in range(mine_ref.shape[0]):
        start = 2 * blk * HALF_ROWS
        store(pl.multiple_of(start + core * HALF_ROWS, HALF_ROWS), mine_ref[blk, at])
        store(pl.multiple_of(start + (1 - core) * HALF_ROWS, HALF_ROWS), other_ref[blk, at - mine_ref.shape[1] + 2])


def forward_kernel(
    core_ref, low_ref, open_ref, close_ref, high_ref,
    pos_ref, begin_ref, q_ref, mine_ref, other_ref, o_ref, lse_ref, k_ref, vt_ref,
):
    index = pl.program_id(0)

    @pl.when(index == 0)
    def _():
        core, last = core_ref[0], mine_ref.shape[1]

        def store_key(start, rows):
            k_ref[pl.ds(start, HALF_ROWS), :] = rows

        def store_value(start, rows):
            vt_ref[:, pl.ds(start, HALF_ROWS)] = jnp.transpose(rows)

        load_keys(core, mine_ref, other_ref, last - 2, store_key)
        load_keys(core, mine_ref, other_ref, last - 1, store_value)

    query = q_ref[0, 0]
    pos, begin = pos_ref[0], begin_ref[0]
    rows = query.shape[0]

    def step(block, carry, masked, size):
        top, total, acc = carry
        start = pl.multiple_of(block * KEY_ROWS, KEY_ROWS)
        scores = dot_nt(k_ref[pl.ds(start, size), :], query) * LOG2_SCALE
        if masked:
            scores = jnp.where(allowed(start, pos, begin), scores, MASKED_SCORE)
        new_top = jnp.maximum(top, jnp.max(scores, axis=0, keepdims=True))
        probs = jnp.exp2(scores - new_top)
        shrink = jnp.exp2(top - new_top)
        total = total * shrink + jnp.sum(probs, axis=0, keepdims=True)
        acc = acc * shrink + jnp.dot(
            vt_ref[:, pl.ds(start, size)], probs.astype(bfloat), preferred_element_type=single
        )
        return new_top, total, acc

    carry = (
        jnp.full((1, rows), MASKED_SCORE, single),
        jnp.zeros((1, rows), single),
        jnp.zeros((HEAD_DIM, rows), single),
    )
    top, total, acc = key_loops(low_ref, open_ref, close_ref, high_ref, index, step, carry)
    o_ref[0] = jnp.transpose(acc / total)
    lse_ref[0] = top + jnp.log2(total)


def backward_kernel(
    core_ref, low_ref, open_ref, close_ref, high_ref, pos_ref, begin_ref, lse_ref, o_ref,
    q_ref, do_ref, mine_ref, other_ref, dq_ref, keep_ref, send_ref, k_ref, v_ref, kt_ref, dk_ref, dv_ref,
):
    index = pl.program_id(0)
    core = core_ref[0]

    @pl.when(index == 0)
    def _():
        dk_ref[...] = jnp.zeros_like(dk_ref)
        dv_ref[...] = jnp.zeros_like(dv_ref)
        last = mine_ref.shape[1]

        def store_key(start, rows):
            k_ref[pl.ds(start, HALF_ROWS), :] = rows
            kt_ref[:, pl.ds(start, HALF_ROWS)] = jnp.transpose(rows)

        def store_value(start, rows):
            v_ref[pl.ds(start, HALF_ROWS), :] = rows

        load_keys(core, mine_ref, other_ref, last - 2, store_key)
        load_keys(core, mine_ref, other_ref, last - 1, store_value)

    query, d_out = q_ref[0, 0], do_ref[0]
    pos, begin = pos_ref[0], begin_ref[0]
    lse = lse_ref[0]
    products = d_out.astype(single) * o_ref[0]
    delta = jnp.sum(jnp.transpose(products), axis=0, keepdims=True)

    def step(block, acc, masked, size):
        start = pl.multiple_of(block * KEY_ROWS, KEY_ROWS)
        rows = pl.ds(start, size)
        scores = dot_nt(k_ref[rows, :], query) * LOG2_SCALE
        probs = jnp.exp2(scores - lse)
        if masked:
            probs = jnp.where(allowed(start, pos, begin), probs, 0.0)
        d_probs = dot_nt(v_ref[rows, :], d_out)
        d_scores = (probs * (d_probs - delta)).astype(bfloat)
        dv_ref[rows, :] += jnp.dot(probs.astype(bfloat), d_out, preferred_element_type=single)
        dk_ref[rows, :] += jnp.dot(d_scores, query, preferred_element_type=single)
        return acc + jnp.dot(kt_ref[:, rows], d_scores, preferred_element_type=single)

    acc = jnp.zeros((HEAD_DIM, query.shape[0]), single)
    acc = key_loops(low_ref, open_ref, close_ref, high_ref, index, step, acc)
    dq_ref[0] = (jnp.transpose(acc) * SCORE_SCALE).astype(bfloat)

    @pl.when(index == pl.num_programs(0) - 1)
    def _():
        for blk in range(keep_ref.shape[0]):
            start = 2 * blk * HALF_ROWS
            mine = pl.ds(pl.multiple_of(start + core * HALF_ROWS, HALF_ROWS), HALF_ROWS)
            other = pl.ds(pl.multiple_of(start + (1 - core) * HALF_ROWS, HALF_ROWS), HALF_ROWS)
            keep_ref[blk, 0] = dk_ref[mine, :] * SCORE_SCALE
            keep_ref[blk, 1] = dv_ref[mine, :]
            send_ref[blk, 0] = (dk_ref[other, :] * SCORE_SCALE).astype(bfloat)
            send_ref[blk, 1] = dv_ref[other, :].astype(bfloat)


def block_bounds(pos, begin):
    first, last = jnp.min(begin, axis=1), jnp.max(begin, axis=1)
    low = first // KEY_ROWS
    high = jnp.max(pos, axis=1) // KEY_ROWS + 1
    opened = jnp.clip((last + KEY_ROWS - 1) // KEY_ROWS, low, high)
    closed = jnp.clip((jnp.min(pos, axis=1) + 1) // KEY_ROWS, opened, high)
    return low, opened, closed, high


def block_spec(shape):
    return pl.BlockSpec((1,) + shape[1:], lambda i, *_: (i,) + (0,) * (len(shape) - 1))


def first_spec(shape):
    return pl.BlockSpec((1, 1) + shape[2:], lambda i, *_: (i,) + (0,) * (len(shape) - 1))


def whole_spec(shape):
    return pl.BlockSpec(shape, lambda *_: (0,) * len(shape), pipeline_mode=pl.Buffered(1))


def attention_forward(scalars, pos, begin, query, mine, other):
    blocks, _, rows = pos.shape
    keys = 2 * mine.shape[0] * HALF_ROWS
    out_shape = [
        jax.ShapeDtypeStruct((blocks, rows, HEAD_DIM), single),
        jax.ShapeDtypeStruct(pos.shape, single),
    ]
    return pl.pallas_call(
        forward_kernel,
        grid_spec=pltpu.PrefetchScalarGridSpec(
            num_scalar_prefetch=5,
            grid=(blocks,),
            in_specs=[
                block_spec(pos.shape), block_spec(pos.shape), first_spec(query.shape),
                whole_spec(mine.shape), whole_spec(other.shape),
            ],
            out_specs=[block_spec(out.shape) for out in out_shape],
            scratch_shapes=[pltpu.VMEM((keys, HEAD_DIM), bfloat), pltpu.VMEM((HEAD_DIM, keys), bfloat)],
        ),
        out_shape=out_shape,
        compiler_params=pltpu.CompilerParams(vmem_limit_bytes=48 << 20),
        cost_estimate=kernel_cost(22),
        name="attention_forward",
    )(*scalars, pos, begin, query, mine, other)


def attention_backward(scalars, pos, begin, lse, head_out, query, d_out, mine, other):
    blocks, _, rows = pos.shape
    keys = 2 * mine.shape[0] * HALF_ROWS
    pair = (mine.shape[0], 2, HALF_ROWS, HEAD_DIM)
    out_shape = [
        jax.ShapeDtypeStruct(d_out.shape, bfloat),
        jax.ShapeDtypeStruct(pair, single),
        jax.ShapeDtypeStruct(pair, bfloat),
    ]
    return pl.pallas_call(
        backward_kernel,
        grid_spec=pltpu.PrefetchScalarGridSpec(
            num_scalar_prefetch=5,
            grid=(blocks,),
            in_specs=[
                block_spec(pos.shape), block_spec(pos.shape), block_spec(pos.shape),
                block_spec(head_out.shape), first_spec(query.shape), block_spec(d_out.shape),
                whole_spec(mine.shape), whole_spec(other.shape),
            ],
            out_specs=[block_spec(d_out.shape), whole_spec(pair), whole_spec(pair)],
            scratch_shapes=[
                pltpu.VMEM((keys, HEAD_DIM), bfloat), pltpu.VMEM((keys, HEAD_DIM), bfloat),
                pltpu.VMEM((HEAD_DIM, keys), bfloat),
                pltpu.VMEM((keys, HEAD_DIM), single), pltpu.VMEM((keys, HEAD_DIM), single),
            ],
        ),
        out_shape=out_shape,
        compiler_params=pltpu.CompilerParams(vmem_limit_bytes=60 << 20),
        cost_estimate=kernel_cost(1),
        name="attention_backward",
    )(*scalars, pos, begin, lse, head_out, query, d_out, mine, other)


def turned(values, cosine, sine):
    return values * cosine + pltpu.roll(values, HEAD_DIM // 2, 1) * sine


def rotate_kernel(lin_ref, recip_ref, gain_ref, cosine_ref, sine_ref, out_ref):
    groups, rows = out_ref.shape[2], out_ref.shape[5]
    cosine, sine = cosine_ref[...], sine_ref[...]
    for which in range(3):
        for head in range(2):
            at = head * HEAD_DIM
            values = lin_ref[:, pl.ds((2 * which + head) * HEAD_DIM, HEAD_DIM)]
            if which < 2:
                values = values * recip_ref[:, which : which + 1]
                values = values * gain_ref[which : which + 1, at : at + HEAD_DIM]
                values = turned(values, cosine, sine)
            values = values.astype(bfloat)
            for group in range(groups):
                out_ref[0, head, group, 0, which] = values[group * rows : (group + 1) * rows]


def back_parts(d_ref, lin_ref, recip_ref, gain_ref, cosine, sine, which, head):
    at = head * HEAD_DIM
    grad = d_ref[0, head, :, 0, which].reshape(-1, HEAD_DIM).astype(single)
    grad = turned(grad, cosine, -sine)
    hat = lin_ref[:, pl.ds((2 * which + head) * HEAD_DIM, HEAD_DIM)] * recip_ref[:, which : which + 1]
    return grad, grad * gain_ref[which : which + 1, at : at + HEAD_DIM], hat


def sums_kernel(d_ref, lin_ref, recip_ref, gain_ref, cosine_ref, sine_ref, gain_out_ref, sum_ref):
    first = (pl.program_id(0) == 0) & (pl.program_id(1) == 0)

    @pl.when(first)
    def _():
        gain_out_ref[...] = jnp.zeros_like(gain_out_ref)

    cosine, sine = cosine_ref[...], sine_ref[...]
    for which in range(2):
        total = None
        for head in range(2):
            grad, scaled, hat = back_parts(
                d_ref, lin_ref, recip_ref, gain_ref, cosine, sine, which, head
            )
            at = pl.ds(head * HEAD_DIM, HEAD_DIM)
            gain_out_ref[which : which + 1, at] += jnp.sum(grad * hat, axis=0, keepdims=True)
            product = jnp.transpose(scaled * hat)
            product = jnp.sum(product, axis=0, keepdims=True)
            total = product if total is None else total + product
        sum_ref[0, 0, which : which + 1, :] = total


def lin_kernel(d_ref, lin_ref, recip_ref, mean_ref, gain_ref, cosine_ref, sine_ref, out_ref):
    cosine, sine = cosine_ref[...], sine_ref[...]
    for head in range(2):
        for which in range(2):
            _, scaled, hat = back_parts(
                d_ref, lin_ref, recip_ref, gain_ref, cosine, sine, which, head
            )
            grad = recip_ref[:, which : which + 1] * (scaled - hat * mean_ref[:, which : which + 1])
            out_ref[:, pl.ds((2 * which + head) * HEAD_DIM, HEAD_DIM)] = grad.astype(bfloat)
        out_ref[:, pl.ds((4 + head) * HEAD_DIM, HEAD_DIM)] = d_ref[0, head, :, 0, 2].reshape(
            -1, HEAD_DIM
        )


def token_spec(columns):
    return pl.BlockSpec((HALF_ROWS, columns), lambda near, half: (2 * near + half, 0))


def split_spec(groups, rows):
    return pl.BlockSpec(
        (1, 2, groups, 1, 3, rows, HEAD_DIM), lambda near, half: (half, 0, 0, near, 0, 0, 0)
    )


def project_kernel(rows_ref, weight_ref, lin_ref, sum_ref):
    part = weight_ref.shape[1] // 3
    lin = jnp.dot(rows_ref[...], weight_ref[...], preferred_element_type=single)
    lin_ref[...] = lin
    for which in range(2):
        values = lin[:, which * part : (which + 1) * part]
        sum_ref[0, 0, which : which + 1, :] = jnp.sum(
            jnp.transpose(values * values), axis=0, keepdims=True
        )


def projected(rows, weight):
    return pl.pallas_call(
        project_kernel,
        grid=(2, 2),
        in_specs=[token_spec(rows.shape[1]), whole_spec(weight.shape)],
        out_specs=[
            token_spec(weight.shape[1]),
            pl.BlockSpec((1, 1, 2, HALF_ROWS), lambda near, half: (near, half, 0, 0)),
        ],
        out_shape=[
            jax.ShapeDtypeStruct((rows.shape[0], weight.shape[1]), single),
            jax.ShapeDtypeStruct((2, 2, 2, HALF_ROWS), single),
        ],
        compiler_params=pltpu.CompilerParams(vmem_limit_bytes=32 << 20),
        cost_estimate=kernel_cost(5),
        name="projected",
    )(rows, weight)


def columns(values):
    return jnp.transpose(values, (0, 1, 3, 2)).reshape(-1, 2)


def rotated_heads(lin, recips, gains, cosine, sine, groups):
    rows = HALF_ROWS // groups
    return pl.pallas_call(
        rotate_kernel,
        grid=(2, 2),
        in_specs=[
            token_spec(lin.shape[1]), token_spec(2), whole_spec(gains.shape),
            token_spec(HEAD_DIM), token_spec(HEAD_DIM),
        ],
        out_specs=split_spec(groups, rows),
        out_shape=jax.ShapeDtypeStruct((2, 2, groups, 2, 3, rows, HEAD_DIM), bfloat),
        cost_estimate=kernel_cost(5),
        name="rotated_heads",
    )(lin, recips, gains, cosine, sine)


def rotated_sums(d_split, lin, recips, gains, cosine, sine):
    groups, rows = d_split.shape[2], d_split.shape[5]
    return pl.pallas_call(
        sums_kernel,
        grid=(2, 2),
        in_specs=[
            split_spec(groups, rows), token_spec(lin.shape[1]), token_spec(2),
            whole_spec(gains.shape), token_spec(HEAD_DIM), token_spec(HEAD_DIM),
        ],
        out_specs=[
            pl.BlockSpec(gains.shape, lambda near, half: (0, 0)),
            pl.BlockSpec((1, 1, 2, HALF_ROWS), lambda near, half: (near, half, 0, 0)),
        ],
        out_shape=[
            jax.ShapeDtypeStruct(gains.shape, single),
            jax.ShapeDtypeStruct((2, 2, 2, HALF_ROWS), single),
        ],
        cost_estimate=kernel_cost(5),
        name="rotated_sums",
    )(d_split, lin, recips, gains, cosine, sine)


def rotated_back(d_split, lin, recips, means, gains, cosine, sine):
    groups, rows = d_split.shape[2], d_split.shape[5]
    return pl.pallas_call(
        lin_kernel,
        grid=(2, 2),
        in_specs=[
            split_spec(groups, rows), token_spec(lin.shape[1]), token_spec(2), token_spec(2),
            whole_spec(gains.shape), token_spec(HEAD_DIM), token_spec(HEAD_DIM),
        ],
        out_specs=token_spec(lin.shape[1]),
        out_shape=jax.ShapeDtypeStruct(lin.shape, bfloat),
        cost_estimate=kernel_cost(5),
        name="rotated_back",
    )(d_split, lin, recips, means, gains, cosine, sine)


def unpack_kernel(in_ref, *out_refs):
    count, rows, width = in_ref.shape
    part = width // 3
    for which in range(3):
        for piece in range(count):
            out_refs[which][:, pl.ds(piece * part, part)] = in_ref[
                piece, :, pl.ds(which * part, part)
            ].astype(single)


def unpacked(values):
    count, rows, width = values.shape
    return pl.pallas_call(
        unpack_kernel,
        out_shape=[jax.ShapeDtypeStruct((rows, count * width // 3), single)] * 3,
        name="unpacked",
    )(values)


def dot_tn(a, b):
    return lax.dot_general(a, b, (((0,), (0,)), ((), ())), preferred_element_type=single)


def picks(slot_ref, source, expert, capacity):
    slots = slot_ref[source, pl.ds(expert, 1), :]
    rows = lax.broadcasted_iota(jnp.int32, (capacity, slots.shape[1]), 0) + 1
    return slots == rows.astype(single)


def spread_tokens(slot_ref, first, second, out_ref, capacity):
    for source in range(slot_ref.shape[0]):
        at = slice(source * capacity, (source + 1) * capacity)
        total = dot_tn(picks(slot_ref, source, 0, capacity).astype(bfloat), first[at])
        total += dot_tn(picks(slot_ref, source, 1, capacity).astype(bfloat), second[at])
        out_ref[source] = total.astype(bfloat)


def expert_kernel(
    blk_ref, slot_ref, ffn_ref, cot_ref, router_ref, gate_ref, up_ref, down_ref, gate_tile_ref,
    up_tile_ref, x_ref, c_ref, value_ref, hidden_ref, d_gate_ref, d_up_ref, probs_ref, out_ref,
    grad_ref, d_both_ref, first_ref,
):
    expert, step = pl.program_id(0), pl.program_id(1)
    sources = ffn_ref.shape[0]
    capacity = x_ref.shape[1] // sources
    part = gate_ref.shape[-1]
    tile = gate_tile_ref.shape[-2]

    @pl.when((expert == 0) & (step == 0))
    def _():
        for source in range(sources):
            logits = dot_nt(router_ref[...], ffn_ref[source])
            shifted = jnp.exp(logits - jnp.max(logits, axis=0, keepdims=True))
            probs_ref[source] = shifted / jnp.sum(shifted, axis=0, keepdims=True)

    def fill(which):
        for source in range(sources):
            at = pl.ds(source * capacity, capacity)
            picked = picks(slot_ref, source, which, capacity)
            picked_low = picked.astype(bfloat)
            x_ref[0, at, :] = jnp.dot(
                picked_low, ffn_ref[source], preferred_element_type=single
            ).astype(bfloat)
            cot_rows = jnp.dot(picked_low, cot_ref[source], preferred_element_type=single)
            c_ref[0, at, :] = cot_rows.astype(bfloat)
            probs = probs_ref[source, pl.ds(2 * blk_ref[0] + which, 1), :]
            value = jnp.sum(jnp.where(picked, probs, 0.0), axis=1, keepdims=True)
            value_ref[0, at, :] = value
            grad_ref[at, :] = (value * cot_rows).astype(bfloat)

    pl.when(step == 0)(lambda: fill(expert))

    @pl.when(step < 4)
    def _():
        w_both = jnp.concatenate([gate_ref[0, 0, 0], up_ref[0, 0, 0]], axis=1)
        both = jnp.dot(x_ref[0], w_both, preferred_element_type=single)
        gate_val, up_val = both[:, :part], both[:, part:]
        d_hidden = dot_nt(grad_ref[...], down_ref[0, 0])
        sigmoid = 1.0 / (1.0 + jnp.exp(-gate_val))
        silu = gate_val * sigmoid
        hidden_ref[0] = (silu * up_val).astype(bfloat)
        d_gate = (d_hidden * up_val * sigmoid * (1.0 + gate_val * (1.0 - sigmoid))).astype(bfloat)
        d_up = (d_hidden * silu).astype(bfloat)
        d_gate_ref[0] = d_gate
        d_up_ref[0] = d_up
        at = pl.multiple_of(2 * step * part, part)
        d_both_ref[:, pl.ds(at, part)] = d_gate
        d_both_ref[:, pl.ds(pl.multiple_of(at + part, part), part)] = d_up

    @pl.when(step >= 4)
    def _():
        weights = [ref[i, 0, 0] for i in range(4) for ref in (gate_tile_ref, up_tile_ref)]
        d_rows = dot_nt(d_both_ref[...], jnp.concatenate(weights, axis=1)).astype(bfloat)
        at = pl.ds(pl.multiple_of((step - 4) * tile, tile), tile)

        @pl.when(expert == 0)
        def _():
            first_ref[:, at] = d_rows

        @pl.when(expert == 1)
        def _():
            spread_tokens(slot_ref, first_ref[:, at], d_rows, out_ref, capacity)


def down_grads_kernel(c_ref, value_ref, hidden_ref, sent_ref, kept_ref, grad_ref):
    step = pl.program_id(1)

    @pl.when(step == 0)
    def _():
        grad_ref[...] = (value_ref[0] * c_ref[0].astype(single)).astype(bfloat)

    down = dot_tn(hidden_ref[0], grad_ref[...])

    @pl.when(step < 2)
    def _():
        sent_ref[0, 0] = down.astype(bfloat)

    @pl.when(step >= 2)
    def _():
        kept_ref[0, 0] = down


def grads_kernel(
    slot_ref, x_ref, c_ref, value_ref, hidden_ref, d_gate_ref, d_up_ref, down_tile_ref,
    gate_sent_ref, up_sent_ref, gate_kept_ref, up_kept_ref,
    d_probs_ref, out_ref, xt_ref, dots_ref, first_ref,
):
    expert, step = pl.program_id(0), pl.program_id(1)
    sources = slot_ref.shape[0]
    capacity = x_ref.shape[1] // sources
    part = d_gate_ref.shape[2]
    tile = down_tile_ref.shape[3]

    @pl.when(step == 0)
    def _():
        xt_ref[...] = jnp.transpose(x_ref[0])
        dots_ref[...] = jnp.zeros_like(dots_ref)

    @pl.when(step < 4)
    def _():
        d_both = jnp.concatenate([d_gate_ref[0], d_up_ref[0]], axis=1)
        both = jnp.dot(xt_ref[...], d_both, preferred_element_type=single)

        @pl.when(step < 2)
        def _():
            gate_sent_ref[0, 0] = both[:, :part].astype(bfloat)
            up_sent_ref[0, 0] = both[:, part:].astype(bfloat)

        @pl.when(step >= 2)
        def _():
            gate_kept_ref[0, 0] = both[:, :part]
            up_kept_ref[0, 0] = both[:, part:]

    @pl.when(step >= 4)
    def _():
        down = jnp.concatenate([down_tile_ref[i, 0] for i in range(4)], axis=0)
        expert_out = jnp.dot(hidden_ref[0], down, preferred_element_type=single)
        expert_out = expert_out.astype(bfloat).astype(single)
        at = pl.ds(pl.multiple_of((step - 4) * tile, tile), tile)
        dots_ref[...] += jnp.sum(
            c_ref[0, :, at].astype(single) * expert_out, axis=1, keepdims=True
        )
        weighted = (value_ref[0] * expert_out).astype(bfloat)

        @pl.when(expert == 0)
        def _():
            first_ref[:, at] = weighted

        @pl.when(expert == 1)
        def _():
            spread_tokens(slot_ref, first_ref[:, at], weighted, out_ref, capacity)

    @pl.when(step == 7)
    def _():
        for source in range(sources):
            picked = picks(slot_ref, source, expert, capacity)
            row = dots_ref[source * capacity : (source + 1) * capacity]
            d_probs_ref[source, pl.ds(expert, 1), :] = jnp.sum(
                jnp.where(picked, row, 0.0), axis=0, keepdims=True
            )


def rows_spec(rows, columns):
    return pl.BlockSpec((1, rows, columns), lambda e, k, *_: (e, 0, 0))


def first_half(k):
    return jnp.minimum(k, 3)


def second_half(k):
    return jnp.maximum(k - 4, 0)


def part_spec(rows, columns):
    return pl.BlockSpec((1, rows, columns), lambda e, k, *_: (e, 0, first_half(k)))


def weight_spec(shape, place=first_half):
    return pl.BlockSpec((1, 1) + shape[2:], lambda e, k, *_: (place(k), e, 0, 0))


def token_tile_spec(shape):
    block = shape[:2] + (shape[2] // 4,)
    return pl.BlockSpec(block, lambda e, k, *_: (0, 0, e * second_half(k)))


def pair_spec(shape, which):
    return pl.BlockSpec(
        (1, 1, 1) + shape[3:], lambda e, k, *_: (first_half(k), which, e, 0, 0)
    )


def pair_tile_spec(shape, which):
    return pl.BlockSpec(
        (4, 1, 1, shape[3] // 4, shape[4]), lambda e, k, *_: (0, which, e, second_half(k), 0)
    )


def expert_rows(blk, slot_map, ffn_all, cot_all, router_t, pair, down, capacity):
    sources, tokens, width = ffn_all.shape
    rows, experts, hidden = sources * capacity, router_t.shape[0], 4 * down.shape[2]
    wide = jax.ShapeDtypeStruct((2, rows, width), bfloat)
    narrow = jax.ShapeDtypeStruct((2, rows, hidden), bfloat)
    probs = jax.ShapeDtypeStruct((sources, experts, tokens), single)
    return pl.pallas_call(
        expert_kernel,
        grid_spec=pltpu.PrefetchScalarGridSpec(
            num_scalar_prefetch=1,
            grid=(2, 8),
            in_specs=[
                whole_spec(slot_map.shape), whole_spec(ffn_all.shape), whole_spec(cot_all.shape),
                whole_spec(router_t.shape), pair_spec(pair.shape, 0), pair_spec(pair.shape, 1),
                weight_spec(down.shape), pair_tile_spec(pair.shape, 0), pair_tile_spec(pair.shape, 1),
            ],
            out_specs=[
                rows_spec(rows, width), rows_spec(rows, width), rows_spec(rows, 1),
                part_spec(rows, hidden // 4), part_spec(rows, hidden // 4),
                part_spec(rows, hidden // 4), whole_spec(probs.shape), token_tile_spec(ffn_all.shape),
            ],
            scratch_shapes=[
                pltpu.VMEM((rows, width), bfloat), pltpu.VMEM((rows, 2 * hidden), bfloat),
                pltpu.VMEM((rows, width), bfloat),
            ],
        ),
        out_shape=[
            wide, wide, jax.ShapeDtypeStruct((2, rows, 1), single), narrow, narrow, narrow,
            probs, jax.ShapeDtypeStruct(ffn_all.shape, bfloat),
        ],
        compiler_params=pltpu.CompilerParams(vmem_limit_bytes=60 << 20),
        cost_estimate=kernel_cost(55),
        name="expert_rows",
    )(blk[None], slot_map, ffn_all, cot_all, router_t, pair, pair, down, pair, pair)


def sent_place(k):
    return jnp.minimum(k, 1)


def kept_place(k):
    return jnp.clip(k - 2, 0, 1)


def expert_down_grads(c, value, hidden):
    rows, width = c.shape[1:]
    part = hidden.shape[2] // 4
    shape = (2, 2, part, width)
    return pl.pallas_call(
        down_grads_kernel,
        grid=(2, 4),
        in_specs=[rows_spec(rows, width), rows_spec(rows, 1), part_spec(rows, part)],
        out_specs=[weight_spec(shape, sent_place), weight_spec(shape, kept_place)],
        out_shape=[jax.ShapeDtypeStruct(shape, bfloat), jax.ShapeDtypeStruct(shape, single)],
        scratch_shapes=[pltpu.VMEM((rows, width), bfloat)],
        compiler_params=pltpu.CompilerParams(vmem_limit_bytes=40 << 20),
        cost_estimate=kernel_cost(12),
        name="expert_down_grads",
    )(c, value, hidden)


def expert_grads(slot_map, x, c, value, hidden, d_gate, d_up, down, tokens):
    rows, width = x.shape[1:]
    part = down.shape[2]
    wide = (2, 2, width, part)
    summed = (slot_map.shape[0], tokens, width)
    return pl.pallas_call(
        grads_kernel,
        grid=(2, 8),
        in_specs=[
            whole_spec(slot_map.shape), rows_spec(rows, width), rows_spec(rows, width),
            rows_spec(rows, 1), rows_spec(rows, 4 * part), part_spec(rows, part),
            part_spec(rows, part),
            pl.BlockSpec((4, 1, part, width // 4), lambda e, k: (0, e, 0, second_half(k))),
        ],
        out_specs=[weight_spec(wide, sent_place)] * 2
        + [weight_spec(wide, kept_place)] * 2
        + [whole_spec(slot_map.shape), token_tile_spec(summed)],
        out_shape=[jax.ShapeDtypeStruct(wide, bfloat)] * 2
        + [jax.ShapeDtypeStruct(wide, single)] * 2
        + [
            jax.ShapeDtypeStruct(slot_map.shape, single),
            jax.ShapeDtypeStruct(summed, bfloat),
        ],
        scratch_shapes=[
            pltpu.VMEM((width, rows), bfloat), pltpu.VMEM((rows, 1), single),
            pltpu.VMEM((rows, width), bfloat),
        ],
        compiler_params=pltpu.CompilerParams(vmem_limit_bytes=60 << 20),
        cost_estimate=kernel_cost(39),
        name="expert_grads",
    )(slot_map, x, c, value, hidden, d_gate, d_up, down)


def plain_experts(blk, slot_map, ffn_all, cot_all, router_t, pair, down, capacity):
    sources, tokens, width = ffn_all.shape
    count = slot_map.shape[1]

    def joined(weights, axis):
        return jnp.concatenate([weights[i] for i in range(4)], axis=axis)

    gate, up, down = joined(pair[:, 0], 2), joined(pair[:, 1], 2), joined(down, 1)
    slot_at = jnp.arange(1, capacity + 1, dtype=jnp.int32).astype(single)
    picked = jnp.transpose(slot_map, (1, 0, 2))[:, :, None, :] == slot_at[None, None, :, None]
    picked_low = picked.astype(bfloat)
    logits = jnp.einsum("ed,std->set", router_t, ffn_all, preferred_element_type=single)
    shifted = jnp.exp(logits - jnp.max(logits, axis=1, keepdims=True))
    probs = shifted / jnp.sum(shifted, axis=1, keepdims=True)
    local = jnp.transpose(lax.dynamic_slice_in_dim(probs, blk * count, count, 1), (1, 0, 2))
    value = jnp.sum(jnp.where(picked, local[:, :, None, :], 0.0), axis=3).reshape(count, -1, 1)

    def dispatch(rows):
        rows = jnp.einsum("esct,std->escd", picked_low, rows, preferred_element_type=single)
        return rows.astype(bfloat).reshape(count, -1, width)

    def combine(rows):
        rows = rows.astype(bfloat).reshape(count, sources, capacity, width)
        total = jnp.einsum("esct,escd->std", picked_low, rows, preferred_element_type=single)
        return total.astype(bfloat)

    def dots(spec, *arrays):
        return jnp.einsum(spec, *arrays, preferred_element_type=single)

    x, c = dispatch(ffn_all), dispatch(cot_all).astype(single)
    grad = (value * c).astype(bfloat)
    gate_val, up_val = dots("erd,edf->erf", x, gate), dots("erd,edf->erf", x, up)
    sigmoid = jax.nn.sigmoid(gate_val)
    hidden = (gate_val * sigmoid * up_val).astype(bfloat)
    d_hidden = dots("erd,efd->erf", grad, down)
    d_gate = (d_hidden * up_val * sigmoid * (1.0 + gate_val * (1.0 - sigmoid))).astype(bfloat)
    d_up = (d_hidden * gate_val * sigmoid).astype(bfloat)
    d_part = combine(dots("erf,edf->erd", d_gate, gate) + dots("erf,edf->erd", d_up, up))
    expert_out = dots("erf,efd->erd", hidden, down).astype(bfloat).astype(single)
    d_value = jnp.sum(c * expert_out, axis=2).reshape(count, sources, capacity, 1)
    d_probs = jnp.transpose(jnp.sum(jnp.where(picked, d_value, 0.0), axis=2), (1, 0, 2))
    mixed_part = combine(value * expert_out)

    def cut(total, axis):
        parts = jnp.stack(jnp.split(total, 4, axis=axis))
        return parts[:2].astype(bfloat), parts[2:]

    gate_sent, gate_kept = cut(dots("erd,erf->edf", x, d_gate), 2)
    up_sent, up_kept = cut(dots("erd,erf->edf", x, d_up), 2)
    down_sent, down_kept = cut(dots("erf,erd->efd", hidden, grad), 1)
    return probs, d_part, (down_sent, down_kept), (
        gate_sent, up_sent, gate_kept, up_kept, d_probs, mixed_part
    )


def per_device(
    block_input, w_query, w_key, w_value, w_out, attn_gain, ffn_gain, query_gain, key_gain,
    router, w_gate, w_up, w_down, expert_ids, slot_ids, doc_starts, cotangent,
):
    ulysses_size = lax.axis_size("ulysses")
    blk_size = lax.axis_size(BLK)
    blk = lax.axis_index(BLK)
    uly = lax.axis_index("ulysses")
    core = uly % 2
    own_tokens, width = block_input.shape
    picks = expert_ids.shape[1]
    experts = router.shape[1]
    capacity = 5 * own_tokens * picks // (4 * experts)
    local_experts = experts // blk_size
    blk_tokens = ulysses_size * own_tokens
    far_size = blk_size // 2
    far_tokens = 2 * blk_tokens
    plane_size = 2 * ulysses_size
    local_width = width // ulysses_size
    plane_width = width // plane_size
    weight_rows = w_query.shape[0]
    groups = blk_size // 8
    plane = 2 * uly + blk % 2

    projections = jnp.concatenate(
        [
            weight.astype(bfloat).reshape(weight_rows, plane_size, plane_width)
            for weight in (w_query, w_key, w_value)
        ],
        axis=2,
    )
    projections = lax.all_to_all(
        jnp.transpose(projections, (1, 0, 2)), PLANE, split_axis=0, concat_axis=0, tiled=True
    )
    projections = projections.reshape(ulysses_size, 2 * weight_rows, 3 * plane_width)
    small = jnp.concatenate(
        [jnp.stack([attn_gain, ffn_gain, query_gain, key_gain]), router.T]
    ).astype(bfloat)
    projections, small = tie(projections, gather_ulysses(small))
    w_qkv = gather_line(projections, 1).reshape(width, 3 * plane_width)
    small = gather_blk_small(small)
    gate_mine, up_mine, down_mine = w_gate.astype(bfloat), w_up.astype(bfloat), w_down.astype(bfloat)
    plane_input = gather_plane(block_input).reshape(far_tokens, width)
    pair_mine = jnp.stack([gate_mine, up_mine])
    pair_beyond = swap(pair_mine, 2)
    attn_g = small[0].astype(single)
    ffn_g = small[1].astype(single)
    plane_gains = lax.dynamic_slice_in_dim(
        small[2:4], plane * plane_width, plane_width, 1
    ).astype(single)
    router_t = small[4:]

    inputs = block_input.astype(single)
    hat_one, recip_one = norm_parts(inputs)
    normed = (norm_parts(plane_input.astype(single))[0] * attn_g).astype(bfloat)
    lin, squares = projected(normed, w_qkv)
    w_o = lax.all_gather(w_out.astype(bfloat), BLK, axis=0, tiled=True)
    named = expert_ids[:, :, None] == jnp.arange(experts, dtype=jnp.int32)[None, None, :]
    slot_map = jnp.sum(jnp.where(named, slot_ids[:, :, None] + 1, 0), axis=1)
    slot_map = slot_map.T.astype(single).reshape(blk_size, local_experts, own_tokens)
    squares, pair_beyond, w_o = tie(squares, pair_beyond, w_o)
    squares, down_mine = tie(sum_plane(squares), down_mine)
    down_beyond = swap(down_mine, 2)
    recips = columns(lax.rsqrt(squares / width + NORM_EPSILON))
    far_at = blk // 2 * far_tokens + jnp.arange(far_tokens, dtype=jnp.int32)
    cosine, sine = angles(far_at - doc_begins(doc_starts, far_at), HEAD_DIM)
    split = rotated_heads(lin, recips, plane_gains, cosine, sine, groups)
    heads_in = line_to_heads(split, far_size)
    heads_in, cotangent_sent, slot_map = tie(heads_in, cotangent, slot_map)
    slot_map = lax.all_to_all(slot_map, BLK, split_axis=0, concat_axis=0, tiled=True)
    cot_all = lax.all_gather(cotangent_sent, BLK, axis=0)
    part_rows = heads_in.shape[2]
    if groups == 1:
        query, mine = heads_in, heads_in
    else:
        query = heads_in[:, 0].reshape(-1, 1, QUERY_ROWS, HEAD_DIM)
        mine = lax.all_gather(
            heads_in[:, 1:], "far", axis=2, axis_index_groups=head_groups(far_size, groups)
        ).reshape(blk_size, 2, HALF_ROWS, HEAD_DIM)
    other, pair_mine, pair_beyond, down_mine = tie(
        swap(mine[:, -2:], 1), pair_mine, pair_beyond, down_mine
    )
    pair_near, pair_far, down_near = swap(pair_mine, 1), swap(pair_beyond, 1), swap(down_mine, 1)
    query_at = (
        jnp.arange(blk_size, dtype=jnp.int32)[:, None] * blk_tokens
        + core * HALF_ROWS
        + blk // 2 % groups * part_rows
        + jnp.arange(part_rows, dtype=jnp.int32)[None, :]
    ).reshape(-1, QUERY_ROWS)
    query_begin = doc_begins(doc_starts, query_at)
    scalars = (core[None],) + block_bounds(query_at, query_begin)
    query_at, query_begin = query_at[:, None], query_begin[:, None]
    head_out, lse = attention_forward(scalars, query_at, query_begin, query, mine, other)
    attended = blk_from_heads(
        head_out.astype(bfloat).reshape(blk_size, part_rows, HEAD_DIM), blk_size
    )
    attended, down_beyond, pair_near, pair_far, down_near = tie(
        attended, down_beyond, pair_near, pair_far, down_near
    )
    down_far = swap(down_beyond, 1)
    out_part = jnp.dot(attended, w_o, preferred_element_type=single)

    def token_rows(values):
        return lambda bits: lax.dynamic_slice_in_dim(
            values, (uly ^ bits) * own_tokens, own_tokens, 0
        )

    residual_mid = inputs + scatter_sum_ulysses(token_rows(out_part))
    hat_two, recip_two = norm_parts(residual_mid)
    ffn_in = (hat_two * ffn_g).astype(bfloat)

    ffn_in, pair_near, pair_far, pair_mine, pair_beyond = tie(
        ffn_in, pair_near, pair_far, pair_mine, pair_beyond
    )
    ffn_all = lax.all_gather(ffn_in, BLK, axis=0)
    expert_pair = jnp.stack([pair_near, pair_far, pair_mine, pair_beyond])
    expert_down = jnp.stack([down_near, down_far, down_mine, down_beyond])
    if capacity % 16 == 0:
        *kept_rows, probs_all, d_part = expert_rows(
            blk, slot_map, ffn_all, cot_all, router_t, expert_pair, expert_down, capacity
        )
        *kept_rows, d_part = tie(*kept_rows, d_part)
        x, c, value, hidden, d_gate, d_up = kept_rows
        down_results = expert_down_grads(c, value, hidden)
        x, *down_results = tie(x, *down_results)
        results = expert_grads(
            slot_map, x, c, value, hidden, d_gate, d_up, expert_down, own_tokens
        )
    else:
        probs_all, d_part, down_results, results = plain_experts(
            blk, slot_map, ffn_all, cot_all, router_t, expert_pair, expert_down, capacity
        )
    d_ffn_in = lax.psum_scatter(d_part, BLK, scatter_dimension=0).astype(single)
    down_sent, down_kept = down_results
    gate_sent, up_sent, gate_kept, up_kept, d_probs, mixed_part = results

    d_probs = lax.all_to_all(d_probs, BLK, split_axis=0, concat_axis=0, tiled=True)
    d_probs = d_probs.reshape(experts, own_tokens)
    gate_sent, up_sent, down_got = tie(gate_sent, up_sent, swap(down_sent, 1))
    gate_got, up_got = swap(gate_sent, 1), swap(up_sent, 1)

    def onward(got, kept):
        return (kept[1] + got[1].astype(single)).astype(bfloat)

    down_sent = onward(down_got, down_kept)
    gate_sent = onward(gate_got, gate_kept)
    summed = lax.dynamic_update_slice(
        jnp.zeros((blk_size, weight_rows + own_tokens, width), bfloat), mixed_part, (0, weight_rows, 0)
    )
    d_ffn_in, summed, up_got, gate_sent, second_down = tie(
        d_ffn_in, summed, up_got, gate_sent, swap(down_sent[1], 2)
    )

    router_probs = lax.dynamic_index_in_dim(probs_all, blk, 0, keepdims=False)
    d_logits = (
        router_probs * (d_probs - jnp.sum(router_probs * d_probs, axis=0, keepdims=True))
    ).astype(bfloat)
    grad_router_part = jnp.dot(d_logits, ffn_in, preferred_element_type=single)
    d_ffn_in = d_ffn_in + dot_tn(d_logits, router_t)
    grad_ffn_part = jnp.sum(d_ffn_in * hat_two, axis=0)
    d_mid = cotangent.astype(single) + norm_back(d_ffn_in * ffn_g, hat_two, recip_two)

    d_attn_out = gather_ulysses(d_mid.astype(bfloat)).reshape(blk_tokens, width)
    narrow = scatter_sum_ulysses(
        lambda bits: lax.dynamic_slice_in_dim(
            jnp.concatenate([grad_ffn_part[None], grad_router_part]),
            (uly ^ bits) * local_width, local_width, 1,
        ),
        single,
    )
    d_attn_out, gate_sent, narrow = tie(d_attn_out, gate_sent, narrow)
    gate_across = swap(gate_sent, 2)
    d_attended = dot_nt(d_attn_out, w_o).astype(bfloat)
    grad_out_part = jnp.einsum("ti,to->io", attended, d_attn_out, preferred_element_type=single)
    grad_out_part = grad_out_part.astype(bfloat).reshape(blk_size, weight_rows, width)
    d_halves, up_got = tie(blk_halves(d_attended, blk_size), up_got)
    up_sent = onward(up_got, up_kept)
    d_out = lax.all_to_all(d_halves, BLK, split_axis=0, concat_axis=0, tiled=True)
    d_out = d_out.reshape(head_out.shape)
    d_out, grad_out_part, up_sent = tie(d_out, grad_out_part, up_sent)
    up_across = swap(up_sent, 2)
    summed = lax.dynamic_update_slice(summed, grad_out_part, (0, 0, 0))
    summed = lax.psum_scatter(summed, BLK, scatter_dimension=0)
    dq_head, keep, send = attention_backward(
        scalars, query_at, query_begin, lse, head_out, query, d_out, mine, other
    )
    d_keys = (keep + swap(send, 1).astype(single)).astype(bfloat)
    if groups > 1:
        moved = jnp.moveaxis(d_keys.reshape(blk_size, 2, groups, part_rows, HEAD_DIM), 2, 0)
        moved = lax.psum_scatter(
            moved, "far", scatter_dimension=0, axis_index_groups=head_groups(far_size, groups)
        )
        d_keys = moved
    d_keys, gate_across = tie(d_keys, gate_across)
    d_stack = jnp.concatenate(
        [dq_head.reshape(blk_size, 1, part_rows, HEAD_DIM), d_keys], axis=1
    )
    d_split = line_from_heads(d_stack, far_size)
    d_split, up_across = tie(d_split, up_across)
    gain_parts, means = rotated_sums(d_split, lin, recips, plane_gains, cosine, sine)
    means, first_down = tie(sum_plane(means), down_sent[0])
    first_down = swap(first_down, 2)
    means = columns(means / width)
    d_lin = rotated_back(d_split, lin, recips, means, plane_gains, cosine, sine)
    grads = jnp.einsum("td,to->do", normed, d_lin, preferred_element_type=single)
    grads = grads.astype(bfloat).reshape(ulysses_size, far_size, 2 * weight_rows, 3 * plane_width)
    grads = jnp.transpose(grads, (1, 0, 2, 3)).reshape(-1, 3 * plane_width)
    grads, d_lin, summed = tie(grads, d_lin, summed)
    grads = lax.psum_scatter(grads, "far", scatter_dimension=0, tiled=True)
    d_normed_part = dot_nt(d_lin, w_qkv)
    grad_attn_part = jnp.sum(d_normed_part * norm_parts(plane_input.astype(single))[0], axis=0)
    d_normed_part = d_normed_part.reshape(2, blk_tokens, width)
    side = blk % 2

    def near_rows(bits):
        mine, other = (
            lax.dynamic_slice(
                d_normed_part, (place, (uly ^ bits) * own_tokens, 0), (1, own_tokens, width)
            )[0]
            for place in (side, 1 - side)
        )
        return mine, other


    def whole_sum(kept, got, across):
        return kept[0] + got[0].astype(single) + across.astype(single)

    grad_w_gate = whole_sum(gate_kept, gate_got, gate_across)
    grad_w_up = whole_sum(up_kept, up_got, up_across)
    d_normed, beside = scatter_sum_plane(
        near_rows,
        (grad_w_gate, grad_w_up, grad_attn_part, summed, first_down),
    )
    grad_w_gate, grad_w_up, grad_attn_part, summed, first_down = beside
    down_across = jnp.stack([first_down, second_down])
    grad_w_out = summed[:weight_rows].astype(single)
    mixed = (residual_mid + summed[weight_rows:].astype(single)).astype(bfloat)
    grad_w_down = whole_sum(down_kept, down_got, down_across)
    input_grad = d_mid + norm_back(d_normed * attn_g, hat_one, recip_one)

    def own_columns(values):
        return scatter_sum_ulysses(
            lambda bits: lax.dynamic_slice_in_dim(values, (uly ^ bits) * local_width, local_width, 1),
            single,
        )

    gain_parts = lax.dynamic_update_slice_in_dim(
        jnp.zeros((2, local_width), single), gain_parts, side * plane_width, 1
    )
    last = own_columns(grad_attn_part[None])
    grads, gains = tie(grads, jnp.concatenate([last, narrow, gain_parts]))
    gains = scatter_sum_blk_small(gains)
    grads = grads.reshape(plane_size, weight_rows, 3 * plane_width)
    grads = lax.all_to_all(grads, PLANE, split_axis=0, concat_axis=0, tiled=True)
    grads = unpacked(grads)
    return (
        mixed,
        input_grad.astype(bfloat),
        grads[0],
        grads[1],
        grads[2],
        grad_w_out,
        gains[0],
        gains[1],
        gains[-2],
        gains[-1],
        gains[2:-2].T,
        grad_w_gate,
        grad_w_up,
        grad_w_down,
    )


def solution(mesh):
    in_specs = (
        P(("far", "near", "ulysses"), None),
        P(("ulysses", "far", "near"), None),
        P(("ulysses", "far", "near"), None),
        P(("ulysses", "far", "near"), None),
        P(("ulysses", "far", "near"), None),
        P(("ulysses", "far", "near")),
        P(("ulysses", "far", "near")),
        P(("ulysses", "far", "near")),
        P(("ulysses", "far", "near")),
        P(("ulysses", "far", "near"), None),
        P(BLK, None, "ulysses"),
        P(BLK, None, "ulysses"),
        P(BLK, "ulysses", None),
        P(("far", "near", "ulysses"), None),
        P(("far", "near", "ulysses"), None),
        P(),
        P(("far", "near", "ulysses"), None),
    )
    out_specs = (
        P(("far", "near", "ulysses"), None),
        P(("far", "near", "ulysses"), None),
        P(("ulysses", "far", "near"), None),
        P(("ulysses", "far", "near"), None),
        P(("ulysses", "far", "near"), None),
        P(("ulysses", "far", "near"), None),
        P(("ulysses", "far", "near")),
        P(("ulysses", "far", "near")),
        P(("ulysses", "far", "near")),
        P(("ulysses", "far", "near")),
        P(("ulysses", "far", "near"), None),
        P(BLK, None, "ulysses"),
        P(BLK, None, "ulysses"),
        P(BLK, "ulysses", None),
    )
    ulysses_size, blk_size = mesh.devices.shape
    shape = (ulysses_size, blk_size // 2, 2)
    split_mesh = jax.sharding.Mesh(mesh.devices.reshape(shape), ("ulysses", "far", "near"))
    return jax.shard_map(
        per_device, mesh=split_mesh, in_specs=in_specs, out_specs=out_specs, check_vma=False
    )
```
